32 devices in a mesh: section: 2 (over core), row: 8 (over z, y), col: 2 (over x).
Axes of the slice: x: 2, y: 2, z: 4, core: 2. Of those that a mesh axis runs over, the one named last changes fastest.
Arguments:
- hidden_in: bfloat16 [8, 256, 3072], P('row', None, 'col')
- patch_ends: int32 [8, 4], P('row'), may hold values from 1 to 256, as said below
- timestep: int32 [8], P('row'), may hold values from 0 to 999
- mod_weight: bfloat16 [2, 256, 3, 3072], P('section'), may hold values from -0.75 to 0.75
- qkv_weight: bfloat16 [2, 3072, 3, 3072], P('section', 'row', None, 'col'), may hold values from -0.109375 to 0.109375
- out_weight: bfloat16 [2, 3072, 3072], P('section', 'col', 'row'), may hold values from -0.109375 to 0.109375
- stale_keys: bfloat16 [2, 8, 256, 3072], P('section', 'row', None, 'col'), may hold values from -1.5 to 1.5
- stale_values: bfloat16 [2, 8, 256, 3072], P('section', 'row', None, 'col'), may hold values from -6 to 6
Outputs:
- layer_out: bfloat16 [2, 8, 256, 3072], P('section', 'row', None, 'col')
The draws below stay inside these ranges and needn't reach their ends.
Inputs may be any that keep to these rules, and one draw needn't show every extreme that they name: patch_ends rises along each request's 4 patches; each patch holds at least one and at most 64 positions, and in every draw some request has all 4 patches of exactly 64 positions.
All inputs are finite; a program needn't handle non-finite values.
Results may differ from the reference program's by a relative error of at most 0.018.
Values may be sent and summed in bfloat16 or wider, within the bound.
No kernel may reach another device: no remote copies, remote signals or barrier semaphores. Data moves between devices by JAX's collectives and lax.ppermute only.
A program may use at most 128 MiB of HBM per device.

```python
import math
import jax
import jax.numpy as jnp
from jax import lax

D = 3072
HD = 128
FREQ = 256
NP = 4
PATCH = 64
REQ = 8
SLOT = 256
LAYERS = 2


def draw_hidden_in(key, part):
    key_base = jax.random.fold_in(key, 11)
    key_cols = jax.random.fold_in(key, 12)
    key_rows = jax.random.fold_in(key, 13)
    feat_pos = jnp.arange(D, dtype=jnp.float32)[None, None, :] / D - 0.5
    rough = jnp.exp(jax.random.uniform(key_cols, (1, 1, D), jnp.float32, jnp.log(0.7), jnp.log(1.4)))
    row_scale = jnp.exp(jax.random.uniform(key_rows, (REQ, SLOT, 1), jnp.float32, jnp.log(0.5), jnp.log(2.0)))
    col_scale = jnp.exp(jnp.log(6.0) * feat_pos) * rough
    base_vals = jax.random.truncated_normal(key_base, -4.0, 4.0, (REQ, SLOT, D), jnp.float32)
    return (0.5 * base_vals * col_scale * row_scale).astype(jnp.bfloat16)


def draw_patch_ends(key, part):
    key_sizes = jax.random.fold_in(key, 21)
    key_pick = jax.random.fold_in(key, 22)
    sizes = jax.random.randint(key_sizes, (REQ, NP), PATCH // 4, PATCH + 1)
    chosen = jax.random.randint(key_pick, (), 0, REQ)
    full_row = (jnp.arange(REQ)[:, None] == chosen) & (jnp.arange(NP)[None, :] >= 0)
    sizes = jnp.where(full_row, PATCH, sizes)
    return jnp.cumsum(sizes, axis=1).astype(jnp.int32)


def touch_ends(entries, rng, low, top_value):
    spot = [jax.random.randint(jax.random.fold_in(rng, axis), (), 0, length) for axis, length in enumerate(entries.shape)]
    widest = entries.shape.index(max(entries.shape))
    beside = spot[:widest] + [(spot[widest] + 1) % entries.shape[widest]] + spot[widest + 1:]
    return entries.at[tuple(spot)].set(low).at[tuple(beside)].set(top_value)


def block_levels(rng, dims, shards, low, high):
    level, own = 1.0, jax.random.fold_in(rng, 6)
    for position, shards_of in shards:
        steps = jnp.exp(jax.random.uniform(jax.random.fold_in(own, position), (shards_of,), jnp.float32, low / len(shards), high / len(shards)))
        level = level * jnp.repeat(steps, dims[position] // shards_of).reshape([-1 if axis == position else 1 for axis in range(len(dims))])
    return level


def centred(stream_key, shape, width, reach, pieces=(), kind=jnp.bfloat16):
    gain = block_levels(stream_key, shape, pieces, -0.22, 0.18) if pieces else 1.0
    entries = jax.random.normal(stream_key, shape, jnp.float32) * width * gain
    return jnp.minimum(jnp.maximum(entries, -reach), reach).astype(kind)


def setup_inputs(seed: int = 0) -> dict:
    key_list = jax.random.split(jax.random.key(seed), 9)
    return {
        "hidden_in": draw_hidden_in(jax.random.fold_in(key_list[8], 71), 0),
        "patch_ends": draw_patch_ends(jax.random.fold_in(key_list[8], 71), 0),
        "timestep": touch_ends(jax.random.randint(key_list[2], (REQ,), 0, 1000), jax.random.fold_in(key_list[2], 1), 0, 999).astype(jnp.int32),
        "mod_weight": centred(key_list[3], (LAYERS, FREQ, 3, D), 0.125, 0.75, ((0, 2),)),
        "qkv_weight": centred(key_list[4], (LAYERS, D, 3, D), D ** -0.5, 0.109375, ((0, 2), (1, 8), (3, 2))),
        "out_weight": centred(key_list[5], (LAYERS, D, D), D ** -0.5, 0.109375, ((0, 2), (1, 2), (2, 8))),
        "stale_keys": jnp.clip(jax.random.uniform(key_list[6], (LAYERS, REQ, SLOT, D), jnp.float32, -1.5, 1.5) * block_levels(key_list[6], (LAYERS, REQ, SLOT, D), ((0, 2), (1, 8), (3, 2)), -0.4, 0.0), -1.5, 1.5).astype(jnp.bfloat16),
        "stale_values": centred(key_list[7], (LAYERS, REQ, SLOT, D), 1.0, 6.0, ((0, 2), (1, 8), (3, 2))),
    }


def embed_time(timestep, feat_width):
    half_width = feat_width // 2
    frequency = jnp.exp(jnp.arange(half_width, dtype=jnp.float32) * (-math.log(10000.0) / half_width))
    angles = timestep.astype(jnp.float32)[:, None] * frequency[None, :]
    return jnp.concatenate([jnp.cos(angles), jnp.sin(angles)], axis=1).astype(jnp.bfloat16)

def head_norm(raw_proj):
    shaped = raw_proj.reshape(raw_proj.shape[:-1] + (raw_proj.shape[-1] // HD, HD))
    scaled = shaped / jnp.sqrt(lax.optimization_barrier(jnp.mean(shaped * shaped, axis=-1, keepdims=True)) + 1e-06)
    return scaled.reshape(raw_proj.shape).astype(jnp.bfloat16)

def attend(queries, key_rows, value_rows, key_ok):
    query_heads = queries.astype(jnp.float32).reshape(queries.shape[0], -1, HD)
    key_heads = key_rows.astype(jnp.float32).reshape(key_rows.shape[0], -1, HD)
    value_heads = value_rows.astype(jnp.float32).reshape(value_rows.shape[0], -1, HD)
    scores = jnp.einsum('qhd,khd->hqk', query_heads, key_heads) / math.sqrt(HD)
    weights = jnp.exp(scores) * key_ok[None, None, :]
    weights = (weights / lax.optimization_barrier(jnp.sum(weights, axis=-1, keepdims=True))).astype(jnp.bfloat16)
    mixed = jnp.einsum('hqk,khd->qhd', weights.astype(jnp.float32), value_heads)
    return mixed.reshape(queries.shape).astype(jnp.bfloat16)

def reference(hidden_in, patch_ends, timestep, mod_weight, qkv_weight, out_weight, stale_keys, stale_values):
    time_feats = embed_time(timestep, FREQ)
    positions = jnp.arange(SLOT, dtype=jnp.int32)
    seq_len = patch_ends[:, NP - 1]
    valid = (positions[None, :] < seq_len[:, None])[:, :, None]
    key_ok = (positions[None, :] < seq_len[:, None]).astype(jnp.float32)
    patch_starts = jnp.concatenate([jnp.zeros((REQ, 1), jnp.int32), patch_ends[:, :NP - 1].astype(jnp.int32)], axis=1)
    layer_input = hidden_in
    results = []
    for layer_index in range(LAYERS):
        modulation = jnp.dot(time_feats, mod_weight[layer_index].reshape(FREQ, 3 * D), preferred_element_type=jnp.float32).reshape(REQ, 3, D)
        shift_vec = modulation[:, 0]
        scale_vec = modulation[:, 1]
        gate_vec = modulation[:, 2]
        as_float = layer_input.astype(jnp.float32)
        row_mean = lax.optimization_barrier(jnp.mean(as_float, axis=-1, keepdims=True))
        row_var = lax.optimization_barrier(jnp.mean(as_float * as_float, axis=-1, keepdims=True)) - row_mean * row_mean
        normed = (as_float - row_mean) / jnp.sqrt(row_var + 1e-06)
        modulated = (normed * (1.0 + scale_vec[:, None, :]) + shift_vec[:, None, :]).astype(jnp.bfloat16)
        projected = jnp.dot(modulated.reshape(REQ * SLOT, D), qkv_weight[layer_index].reshape(D, 3 * D), preferred_element_type=jnp.float32).reshape(REQ, SLOT, 3, D)
        queries = head_norm(projected[:, :, 0])
        fresh_keys = head_norm(projected[:, :, 1])
        fresh_values = projected[:, :, 2].astype(jnp.bfloat16)

        def one_request(items):
            query_rows, keys_new, values_new, keys_old, values_old, ends_row, starts_row, ok_row = items
            totals = jnp.zeros(query_rows.shape, jnp.bfloat16)
            for patch_index in range(NP):
                is_fresh = (positions < ends_row[patch_index])[:, None]
                mixed = attend(query_rows, jnp.where(is_fresh, keys_new, keys_old), jnp.where(is_fresh, values_new, values_old), ok_row)
                row_mask = ((positions >= starts_row[patch_index]) & (positions < ends_row[patch_index]))[:, None]
                totals = jnp.where(row_mask, mixed, totals)
            return totals
        attended = lax.map(one_request, (queries, fresh_keys, fresh_values, stale_keys[layer_index], stale_values[layer_index], patch_ends, patch_starts, key_ok))
        branch = jnp.dot(attended.reshape(REQ * SLOT, D), out_weight[layer_index], preferred_element_type=jnp.float32).reshape(REQ, SLOT, D)
        updated = as_float + gate_vec[:, None, :] * branch
        layer_result = jnp.where(valid, updated, 0.0).astype(jnp.bfloat16)
        results.append(layer_result)
        layer_input = layer_result
    return jnp.stack(results)
```

```python
import functools
import math

import jax
import jax.numpy as jnp
from jax import lax
from jax.experimental import pallas as pl
from jax.experimental.pallas import tpu as pltpu
from jax.sharding import PartitionSpec as P

HD = 128
FREQ = 256
NP = 4
AXES = ("section", "row", "col")
VMEM_LIMIT = 56 * 1024 * 1024


def send_to(array, where):
    ns, nr, nc = (lax.axis_size(axis) for axis in AXES)
    pairs = []
    for s in range(ns):
        for i in range(nr):
            for c in range(nc):
                ts, ti, tc = where(s, i, c)
                pairs.append(((s * nr + i) * nc + c, (ts * nr + ti) * nc + tc))
    return lax.ppermute(array, AXES, pairs)


def to_core(array):
    return send_to(array, lambda s, i, c: (1 - s, i, c))


def to_row(array, bit):
    return send_to(array, lambda s, i, c: (s, i ^ bit, c))


def after(array, *others):
    return lax.optimization_barrier((array,) + others)[0]


def pick(array, index):
    return lax.dynamic_index_in_dim(array, index, 0, keepdims=False)


def embed_time(timestep):
    half_width = FREQ // 2
    frequency = jnp.exp(
        jnp.arange(half_width, dtype=jnp.float32) * (-math.log(10000.0) / half_width)
    )
    angles = timestep.astype(jnp.float32)[:, None] * frequency[None, :]
    return jnp.concatenate([jnp.cos(angles), jnp.sin(angles)], axis=1).astype(jnp.bfloat16)


def any_spec():
    return pl.BlockSpec(memory_space=pl.ANY)


def vmem_spec():
    return pl.BlockSpec(memory_space=pltpu.VMEM)


def attend_kernel(plan, ends_ref, mod_ref, *refs):
    slots, slot_len, cols, n_x, n_w, kr, bw, wc = plan
    x_refs, refs = refs[:n_x], refs[n_x:]
    w_refs, refs = refs[:n_w], refs[n_w:]
    kv_refs, refs = refs[:slots], refs[slots:]
    out_ref, xv, xm, wv, kvv, x_sem, w_sem, kv_sem = refs
    s, i, c = (lax.axis_index(axis) for axis in AXES)
    half = slot_len // 2
    x_copies, w_copies, kv_copies = [], [], []
    place = 0
    for slot in range(slots):
        for dc in range(cols):
            for h in range(2):
                col = lax.rem(c + cols - dc, cols)
                row = slot * slot_len + jnp.where(s == h, 0, half)
                row = pl.multiple_of(row, half)
                x_copies.append(
                    pltpu.make_async_copy(
                        x_refs[place], xv.at[col, pl.ds(row, half), :], x_sem.at[place]
                    )
                )
                place += 1
    for d in range(n_w):
        rows = pl.ds(pl.multiple_of((i ^ d) * kr, 32), kr)
        w_copies.append(pltpu.make_async_copy(w_refs[d], wv.at[:, rows, :], w_sem.at[d]))
    for slot in range(slots):
        kv_copies.append(pltpu.make_async_copy(kv_refs[slot], kvv.at[slot], kv_sem.at[slot]))
    for copy in x_copies + w_copies + kv_copies:
        copy.start()
    for copy in x_copies:
        copy.wait()
    feat = cols * wc
    for slot in range(slots):
        rows = pl.ds(slot * slot_len, slot_len)
        total = jnp.zeros((slot_len, 1), jnp.float32)
        squares = jnp.zeros((slot_len, 1), jnp.float32)
        for col in range(cols):
            part = xv[col, rows, :].astype(jnp.float32)
            total += jnp.sum(part, axis=-1, keepdims=True)
            squares += jnp.sum(part * part, axis=-1, keepdims=True)
        mean = total / feat
        var = squares / feat - mean * mean
        inverse = 1.0 / jnp.sqrt(var + 1e-06)
        for col in range(cols):
            span = pl.ds(col * wc, wc)
            part = xv[col, rows, :].astype(jnp.float32)
            shift = mod_ref[slot, 0:1, span]
            scale = mod_ref[slot, 1:2, span]
            xm[rows, span] = ((part - mean) * inverse * (1.0 + scale) + shift).astype(jnp.bfloat16)
    for copy in w_copies + kv_copies:
        copy.wait()
    key_at = lax.broadcasted_iota(jnp.int32, (slot_len, slot_len), 1)
    query_at = lax.broadcasted_iota(jnp.int32, (slot_len, slot_len), 0)
    contract = (((1,), (1,)), ((), ()))
    for slot in range(slots):
        rows = pl.ds(slot * slot_len, slot_len)
        raw = [
            jnp.dot(xm[rows, :], wv[t], preferred_element_type=jnp.float32) for t in range(3)
        ]
        limit = jnp.full((slot_len, slot_len), ends_ref[slot, NP - 1], jnp.int32)
        for m in range(NP - 2, -1, -1):
            limit = jnp.where(query_at < ends_ref[slot, m], ends_ref[slot, m], limit)
        fresh = key_at < limit
        valid = key_at < ends_ref[slot, NP - 1]
        for head in range(bw // HD):
            lanes = slice(head * HD, (head + 1) * HD)

            def normed(block):
                return (
                    block / jnp.sqrt(jnp.mean(block * block, axis=-1, keepdims=True) + 1e-06)
                ).astype(jnp.bfloat16)

            query = normed(raw[0][:, lanes])
            key = normed(raw[1][:, lanes])
            value = raw[2][:, lanes].astype(jnp.bfloat16)
            old_key = kvv[slot, 0, :, lanes]
            old_value = kvv[slot, 1, :, lanes]
            new_scores = lax.dot_general(query, key, contract, preferred_element_type=jnp.float32)
            old_scores = lax.dot_general(
                query, old_key, contract, preferred_element_type=jnp.float32
            )
            scores = jnp.where(fresh, new_scores, old_scores) * (1.0 / math.sqrt(HD))
            weights = jnp.where(valid, jnp.exp(scores), 0.0)
            weights = weights / jnp.sum(weights, axis=-1, keepdims=True)
            mixed = jnp.dot(
                jnp.where(fresh, weights, 0.0).astype(jnp.bfloat16),
                value,
                preferred_element_type=jnp.float32,
            ) + jnp.dot(
                jnp.where(fresh, 0.0, weights).astype(jnp.bfloat16),
                old_value,
                preferred_element_type=jnp.float32,
            )
            out_ref[rows, lanes] = mixed.astype(jnp.bfloat16)


def out_kernel(plan, attended_ref, *refs):
    slots, slot_len, cols, n_w, nr, bw, wc = plan
    o_refs, refs = refs[:n_w], refs[n_w:]
    keep_ref, pass_ref, ov, o_sem = refs
    s, i, c = (lax.axis_index(axis) for axis in AXES)
    feat = cols * wc
    half = slot_len // 2
    copies = []
    for d in range(n_w):
        start = lax.rem((i ^ d) * nr + feat - c * wc, feat)
        rows = pl.ds(pl.multiple_of(start, 32), nr)
        copies.append(pltpu.make_async_copy(o_refs[d], ov.at[rows, :], o_sem.at[d]))
    for copy in copies:
        copy.start()
    for copy in copies:
        copy.wait()
    contract = (((1,), (1,)), ((), ()))
    blocks = []
    for side in (s, 1 - s):
        for slot in range(slots):
            row = pl.multiple_of(slot * slot_len + side * half, half)
            blocks.append(attended_ref[pl.ds(row, half), :])
    lhs = jnp.concatenate(blocks, axis=0)
    tile = wc // 3
    for first in range(0, feat, tile):
        part = lax.dot_general(
            lhs, ov[first : first + tile, :], contract, preferred_element_type=jnp.float32
        ).astype(jnp.bfloat16)
        part = part.reshape(2, slots, half, tile)
        keep_ref[:, :, first : first + tile] = part[0]
        pass_ref[:, :, first : first + tile] = part[1]


def shards(
    hidden_in, patch_ends, timestep, mod_weight, qkv_weight, out_weight, stale_keys, stale_values
):
    s, i, c = (lax.axis_index(axis) for axis in AXES)
    sections, rows, cols = (lax.axis_size(axis) for axis in AXES)
    _, slot_len, wc = hidden_in.shape
    feat = mod_weight.shape[-1]
    kr = qkv_weight.shape[1]
    nr = out_weight.shape[2]
    half = slot_len // 2
    slots = 2 if (wc // HD) % (2 * sections) == 0 else 1
    bw = wc // (sections * slots)
    row_bits = [1 << b for b in range(rows.bit_length() - 1)]
    split_bit = 2 if slots == 2 else 0
    group_bits = [b for b in reversed(row_bits) if b != split_bit]
    mine_at = (i // 2) % 2 if slots == 2 else 0
    offsets = [0, split_bit] if slots == 2 else [0]

    qkv_blocks = jnp.transpose(
        qkv_weight[0].transpose(1, 0, 2).reshape(3, kr, sections, slots, bw), (2, 3, 0, 1, 4)
    )
    out_blocks = out_weight[0].reshape(sections, slots, bw, nr).transpose(0, 1, 3, 2)
    stale = jnp.stack([stale_keys[0, 0], stale_values[0, 0]])
    stale_blocks = stale.reshape(2, slot_len, sections, slots, bw).transpose(2, 3, 0, 1, 4)

    def both_layers(blocks):
        own, other = pick(blocks, s), to_core(pick(blocks, 1 - s))
        return jnp.where(s == 0, own, other), jnp.where(s == 0, other, own)

    qkv_layers = both_layers(qkv_blocks)
    out_layers = both_layers(out_blocks)
    stale_layers = both_layers(stale_blocks)

    modulation = jnp.einsum(
        "f,kfd->kd",
        embed_time(timestep)[0],
        mod_weight[0].transpose(1, 0, 2),
        preferred_element_type=jnp.float32,
    )
    other_modulation = to_core(modulation)
    mod_layers = (
        jnp.where(s == 0, modulation, other_modulation),
        jnp.where(s == 0, other_modulation, modulation),
    )
    ends = patch_ends[0]
    if slots == 2:
        ends_all = jnp.stack([ends, to_row(ends, split_bit)])
        mod_both = jnp.stack([mod_layers[0][:2], mod_layers[1][:2]])
        mod_other = to_row(mod_both, split_bit)
        mod_slots = [jnp.stack([mod_both[l], mod_other[l]]) for l in range(2)]
    else:
        ends_all = ends[None]
        mod_slots = [mod_layers[l][:2][None] for l in range(2)]

    def spread(own, gate):
        pieces = {0: pick(own, mine_at)}
        if slots == 2:
            sent = pick(own, 1 - mine_at)
            pieces[split_bit] = to_row(after(sent, *gate) if gate else sent, split_bit)
        crossed = []
        for bit in group_bits:
            new = {}
            for d, piece in pieces.items():
                if bit == group_bits[0] and gate:
                    piece = after(piece, *gate)
                new[d ^ bit] = to_row(piece, bit)
            if bit == group_bits[0]:
                crossed = list(new.values())
            pieces.update(new)
        return [pieces[d] for d in range(rows)], crossed

    qkv0, gate_q = spread(qkv_layers[0], ())
    out0, gate_o = spread(out_layers[0], ())
    gate = gate_q + gate_o
    qkv1, gate_q = spread(qkv_layers[1], gate)
    out1, _ = spread(out_layers[1], gate)
    weights = ((qkv0, out0), (qkv1, out1))

    stale_slots = []
    for layer in range(2):
        own = stale_layers[layer]
        block = [pick(own, mine_at)]
        if slots == 2:
            block.append(to_row(pick(own, 1 - mine_at), split_bit))
        stale_slots.append(block)

    places = [(di, dc) for di in offsets for dc in range(cols)]

    def send_place(array, di, dc):
        return send_to(array, lambda si, ii, ci: (si, ii ^ di, (ci + dc) % cols))

    def gather(own_half):
        pieces = []
        for di, dc in places:
            got = own_half if (di, dc) == (0, 0) else send_place(own_half, di, dc)
            pieces.extend([got, to_core(got)])
        return pieces

    def layer_step(layer, x_pieces, x_half):
        qkv_pieces, out_pieces = weights[layer]
        n_w = rows
        plan = (slots, slot_len, cols, len(x_pieces), n_w, kr, bw, wc)
        attended = pl.pallas_call(
            functools.partial(attend_kernel, plan),
            out_shape=jax.ShapeDtypeStruct((slots * slot_len, bw), jnp.bfloat16),
            in_specs=[pl.BlockSpec(memory_space=pltpu.SMEM), vmem_spec()]
            + [any_spec()] * (len(x_pieces) + n_w + slots),
            out_specs=vmem_spec(),
            scratch_shapes=[
                pltpu.VMEM((cols, slots * slot_len, wc), jnp.bfloat16),
                pltpu.VMEM((slots * slot_len, feat), jnp.bfloat16),
                pltpu.VMEM((3, feat, bw), jnp.bfloat16),
                pltpu.VMEM((slots, 2, slot_len, bw), jnp.bfloat16),
                pltpu.SemaphoreType.DMA((len(x_pieces),)),
                pltpu.SemaphoreType.DMA((n_w,)),
                pltpu.SemaphoreType.DMA((slots,)),
            ],
            compiler_params=pltpu.CompilerParams(vmem_limit_bytes=VMEM_LIMIT),
            cost_estimate=pl.CostEstimate(
                flops=2 * slots * slot_len * feat * 3 * bw,
                bytes_accessed=2 * feat * (3 * bw + slots * slot_len),
                transcendentals=0,
            ),
            name="attend_layer",
        )(ends_all, mod_slots[layer], *x_pieces, *qkv_pieces, *stale_slots[layer])
        plan = (slots, slot_len, cols, n_w, nr, bw, wc)
        shape = jax.ShapeDtypeStruct((slots, half, feat), jnp.bfloat16)
        keep, passed = pl.pallas_call(
            functools.partial(out_kernel, plan),
            out_shape=(shape, shape),
            in_specs=[vmem_spec()] + [any_spec()] * n_w,
            out_specs=(vmem_spec(), vmem_spec()),
            scratch_shapes=[
                pltpu.VMEM((feat, bw), jnp.bfloat16),
                pltpu.SemaphoreType.DMA((n_w,)),
            ],
            compiler_params=pltpu.CompilerParams(vmem_limit_bytes=VMEM_LIMIT),
            cost_estimate=pl.CostEstimate(
                flops=2 * slots * slot_len * feat * bw,
                bytes_accessed=2 * feat * (bw + slots * slot_len),
                transcendentals=0,
            ),
            name="project_out",
        )(attended, *out_pieces)
        chip_sum = keep.astype(jnp.float32) + to_core(passed).astype(jnp.float32)
        branch = jnp.zeros((half, wc), jnp.float32)
        for slot, di in enumerate(offsets):
            for dc in range(cols):
                part = chip_sum[slot, :, dc * wc : (dc + 1) * wc]
                if (di, dc) != (0, 0):
                    part = send_place(part.astype(jnp.bfloat16), di, dc).astype(jnp.float32)
                branch = branch + part
        gate_own = lax.dynamic_slice_in_dim(mod_layers[layer][2], c * wc, wc, 0)
        updated = x_half.astype(jnp.float32) + gate_own[None, :] * branch
        positions = jnp.arange(half)[:, None] + s * half
        return jnp.where(positions < ends[NP - 1], updated, 0.0).astype(jnp.bfloat16)

    x_half = lax.dynamic_slice_in_dim(hidden_in[0], s * half, half, 0)
    first = layer_step(0, gather(x_half), x_half)
    x_pieces = gather(first)
    second = layer_step(1, x_pieces, first)
    second_other = to_core(second)
    low = jnp.where(s == 0, first, second_other)
    high = jnp.where(s == 0, x_pieces[1], second)
    return jnp.concatenate([low, high], axis=0)[None, None]


def solution(mesh):
    return jax.shard_map(
        shards,
        mesh=mesh,
        in_specs=(
            P("row", None, "col"),
            P("row", None),
            P("row"),
            P("section", None, None, None),
            P("section", "row", None, "col"),
            P("section", "col", "row"),
            P("section", "row", None, "col"),
            P("section", "row", None, "col"),
        ),
        out_specs=P("section", "row", None, "col"),
        check_vma=False,
    )
```

```python
import functools
import math

import jax
import jax.numpy as jnp
from jax import lax
from jax.experimental import pallas as pl
from jax.experimental.pallas import tpu as pltpu
from jax.sharding import PartitionSpec as P

HD = 128
FREQ = 256
NP = 4
AXES = ("section", "row", "col")
VMEM_LIMIT = 56 * 1024 * 1024


def send_to(array, where):
    ns, nr, nc = (lax.axis_size(axis) for axis in AXES)
    pairs = []
    for s in range(ns):
        for i in range(nr):
            for c in range(nc):
                ts, ti, tc = where(s, i, c)
                pairs.append(((s * nr + i) * nc + c, (ts * nr + ti) * nc + tc))
    return lax.ppermute(array, AXES, pairs)


def to_core(array):
    return send_to(array, lambda s, i, c: (1 - s, i, c))


def to_row(array, bit):
    return send_to(array, lambda s, i, c: (s, i ^ bit, c))


def after(array, *others):
    return lax.optimization_barrier((array,) + others)[0]


def pick(array, index):
    return lax.dynamic_index_in_dim(array, index, 0, keepdims=False)


def embed_time(timestep):
    half_width = FREQ // 2
    frequency = jnp.exp(
        jnp.arange(half_width, dtype=jnp.float32) * (-math.log(10000.0) / half_width)
    )
    angles = timestep.astype(jnp.float32)[:, None] * frequency[None, :]
    return jnp.concatenate([jnp.cos(angles), jnp.sin(angles)], axis=1).astype(jnp.bfloat16)


def any_spec():
    return pl.BlockSpec(memory_space=pl.ANY)


def vmem_spec():
    return pl.BlockSpec(memory_space=pltpu.VMEM)


def attend_kernel(plan, ends_ref, mod_ref, *refs):
    slots, slot_len, cols, n_x, n_w, kr, bw, wc = plan
    x_refs, refs = refs[:n_x], refs[n_x:]
    w_refs, refs = refs[: 3 * n_w], refs[3 * n_w :]
    kv_refs, refs = refs[:slots], refs[slots:]
    out_ref, xv, xm, wv, kvv, x_sem, w_sem, kv_sem = refs
    s, i, c = (lax.axis_index(axis) for axis in AXES)
    half = slot_len // 2
    x_copies, w_copies, kv_copies = [], [], []
    place = 0
    for slot in range(slots):
        for dc in range(cols):
            for h in range(2):
                col = lax.rem(c + cols - dc, cols)
                row = slot * slot_len + jnp.where(s == h, 0, half)
                row = pl.multiple_of(row, half)
                x_copies.append(
                    pltpu.make_async_copy(
                        x_refs[place], xv.at[col, pl.ds(row, half), :], x_sem.at[place]
                    )
                )
                place += 1
    for d in range(n_w):
        rows = pl.ds(pl.multiple_of((i ^ d) * kr, 32), kr)
        for t in range(3):
            w_copies.append(
                pltpu.make_async_copy(w_refs[3 * d + t], wv.at[t, rows, :], w_sem.at[3 * d + t])
            )
    for slot in range(slots):
        kv_copies.append(pltpu.make_async_copy(kv_refs[slot], kvv.at[slot], kv_sem.at[slot]))
    for copy in x_copies + w_copies + kv_copies:
        copy.start()
    for copy in x_copies:
        copy.wait()
    feat = cols * wc
    for slot in range(slots):
        rows = pl.ds(slot * slot_len, slot_len)
        total = jnp.zeros((slot_len, 1), jnp.float32)
        squares = jnp.zeros((slot_len, 1), jnp.float32)
        for col in range(cols):
            part = xv[col, rows, :].astype(jnp.float32)
            total += jnp.sum(part, axis=-1, keepdims=True)
            squares += jnp.sum(part * part, axis=-1, keepdims=True)
        mean = total / feat
        var = squares / feat - mean * mean
        inverse = 1.0 / jnp.sqrt(var + 1e-06)
        for col in range(cols):
            span = pl.ds(col * wc, wc)
            part = xv[col, rows, :].astype(jnp.float32)
            shift = mod_ref[slot, 0:1, span]
            scale = mod_ref[slot, 1:2, span]
            xm[rows, span] = ((part - mean) * inverse * (1.0 + scale) + shift).astype(jnp.bfloat16)
    for copy in w_copies + kv_copies:
        copy.wait()
    key_at = lax.broadcasted_iota(jnp.int32, (slot_len, slot_len), 1)
    query_at = lax.broadcasted_iota(jnp.int32, (slot_len, slot_len), 0)
    contract = (((1,), (1,)), ((), ()))
    for slot in range(slots):
        rows = pl.ds(slot * slot_len, slot_len)
        raw = [
            jnp.dot(xm[rows, :], wv[t], preferred_element_type=jnp.float32) for t in range(3)
        ]
        limit = jnp.full((slot_len, slot_len), ends_ref[slot, NP - 1], jnp.int32)
        for m in range(NP - 2, -1, -1):
            limit = jnp.where(query_at < ends_ref[slot, m], ends_ref[slot, m], limit)
        fresh = key_at < limit
        valid = key_at < ends_ref[slot, NP - 1]
        for head in range(bw // HD):
            lanes = slice(head * HD, (head + 1) * HD)

            def normed(block):
                return (
                    block / jnp.sqrt(jnp.mean(block * block, axis=-1, keepdims=True) + 1e-06)
                ).astype(jnp.bfloat16)

            query = normed(raw[0][:, lanes])
            key = normed(raw[1][:, lanes])
            value = raw[2][:, lanes].astype(jnp.bfloat16)
            old_key = kvv[slot, 0, :, lanes]
            old_value = kvv[slot, 1, :, lanes]
            new_scores = lax.dot_general(query, key, contract, preferred_element_type=jnp.float32)
            old_scores = lax.dot_general(
                query, old_key, contract, preferred_element_type=jnp.float32
            )
            scores = jnp.where(fresh, new_scores, old_scores) * (1.0 / math.sqrt(HD))
            weights = jnp.where(valid, jnp.exp(scores), 0.0)
            weights = weights / jnp.sum(weights, axis=-1, keepdims=True)
            mixed = jnp.dot(
                jnp.where(fresh, weights, 0.0).astype(jnp.bfloat16),
                value,
                preferred_element_type=jnp.float32,
            ) + jnp.dot(
                jnp.where(fresh, 0.0, weights).astype(jnp.bfloat16),
                old_value,
                preferred_element_type=jnp.float32,
            )
            out_ref[rows, lanes] = mixed.astype(jnp.bfloat16)


def out_kernel(plan, attended_ref, *refs):
    slots, slot_len, cols, n_w, nr, bw, wc = plan
    o_refs, refs = refs[:n_w], refs[n_w:]
    keep_ref, pass_ref, ov, o_sem = refs
    s, i, c = (lax.axis_index(axis) for axis in AXES)
    half = slot_len // 2
    copies = []
    for d in range(n_w):
        place = lax.rem((i ^ d) + n_w - c * (n_w // cols), n_w)
        copies.append(pltpu.make_async_copy(o_refs[d], ov.at[place], o_sem.at[d]))
    for copy in copies:
        copy.start()
    for copy in copies:
        copy.wait()
    blocks = []
    for side in (s, 1 - s):
        for slot in range(slots):
            row = pl.multiple_of(slot * slot_len + side * half, half)
            blocks.append(attended_ref[pl.ds(row, half), :])
    lhs = jnp.concatenate(blocks, axis=0)
    for place in range(n_w):
        part = jnp.dot(lhs, ov[place], preferred_element_type=jnp.float32).astype(jnp.bfloat16)
        part = part.reshape(2, slots, half, nr)
        lanes = slice(place * nr, (place + 1) * nr)
        keep_ref[:, :, lanes] = part[0]
        pass_ref[:, :, lanes] = part[1]


def split_kernel(plan, *refs):
    slots, bw = plan
    qkv_ref, o_ref, key_ref, value_ref = refs[:4]
    outs, sem = refs[4:-1], refs[-1]
    s, i = lax.axis_index("section"), lax.axis_index("row")
    mine_at = lax.rem(i // 2, 2) if slots == 2 else 0
    copies = []
    for kind in range(5):
        for side, core in enumerate((1 - s, s)):
            for slot in range(slots):
                block = core * slots + (mine_at if slot == 0 else 1 - mine_at)
                span = pl.ds(pl.multiple_of(block * bw, 128), bw)
                out = outs[2 * kind + side]
                if kind < 3:
                    pairs = [(qkv_ref.at[kind, :, span], out.at[slot])]
                elif kind == 3:
                    pairs = [(o_ref.at[span, :], out.at[slot])]
                else:
                    pairs = [
                        (ref.at[:, span], out.at[slot, t])
                        for t, ref in enumerate((key_ref, value_ref))
                    ]
                for source, target in pairs:
                    one = pltpu.make_async_copy(source, target, sem.at[len(copies)])
                    one.start()
                    copies.append(one)
    for one in copies:
        one.wait()


def choose_kernel(plan, *refs):
    slots, layer, kinds = plan
    pairs, outs, sem = refs[: 2 * kinds], refs[2 * kinds : -1], refs[-1]
    s = lax.axis_index("section")
    for side, mine in enumerate((s == layer, s != layer)):

        @pl.when(mine)
        def _(side=side):
            copies = []
            for kind in range(kinds):
                for slot in range(slots):
                    place = kind * slots + slot
                    one = pltpu.make_async_copy(
                        pairs[2 * kind + side].at[slot], outs[place], sem.at[place]
                    )
                    one.start()
                    copies.append(one)
            for one in copies:
                one.wait()


def mod_kernel(slots, feats_ref, weight_ref, out_ref):
    for k in range(3):
        part = jnp.dot(feats_ref[...], weight_ref[k], preferred_element_type=jnp.float32)
        for slot in range(slots):
            out_ref[slot, k : k + 1, :] = part[slot : slot + 1, :]


def shards(
    hidden_in, patch_ends, timestep, mod_weight, qkv_weight, out_weight, stale_keys, stale_values
):
    s, i, c = (lax.axis_index(axis) for axis in AXES)
    sections, rows, cols = (lax.axis_size(axis) for axis in AXES)
    _, slot_len, wc = hidden_in.shape
    feat = mod_weight.shape[-1]
    kr = qkv_weight.shape[1]
    nr = out_weight.shape[2]
    half = slot_len // 2
    slots = 2 if (wc // HD) % (2 * sections) == 0 else 1
    bw = wc // (sections * slots)
    row_bits = [1 << b for b in range(rows.bit_length() - 1)]
    split_bit = 2 if slots == 2 else 0
    group_bits = [b for b in reversed(row_bits) if b != split_bit]
    offsets = [0, split_bit] if slots == 2 else [0]

    places = [(di, dc) for di in offsets for dc in range(cols)]

    def send_place(array, di, dc):
        return send_to(array, lambda si, ii, ci: (si, ii ^ di, (ci + dc) % cols))

    def gather_chips(own_half):
        return [own_half if p == (0, 0) else send_place(own_half, *p) for p in places]

    def gather(pieces):
        return [one for piece in pieces for one in (piece, to_core(piece))]

    numbers = jnp.concatenate([patch_ends[0], timestep])
    numbers = jnp.stack([numbers] + [to_row(numbers, bit) for bit in offsets[1:]])
    ends_all, steps = numbers[:, :NP], numbers[:, NP]
    x_half = lax.dynamic_slice_in_dim(hidden_in[0], s * half, half, 0)
    x_chips = gather_chips(x_half)

    shapes = [(kr, bw)] * 3 + [(bw, nr), (2, slot_len, bw)]
    shapes = [jax.ShapeDtypeStruct(shape, jnp.bfloat16) for shape in shapes]
    stacked = [jax.ShapeDtypeStruct((slots,) + b.shape, b.dtype) for b in shapes]
    cut = pl.pallas_call(
        functools.partial(split_kernel, (slots, bw)),
        out_shape=[b for b in stacked for _ in range(2)],
        in_specs=[any_spec()] * 4,
        out_specs=[any_spec()] * 10,
        scratch_shapes=[pltpu.SemaphoreType.DMA((12 * slots,))],
        compiler_params=pltpu.CompilerParams(vmem_limit_bytes=VMEM_LIMIT),
        name="split_blocks",
    )(qkv_weight[0].transpose(1, 0, 2), out_weight[0], stale_keys[0, 0], stale_values[0, 0])
    got = [to_core(cut[2 * kind]) for kind in range(5)]

    def blocks_of(layer):
        pairs = [one for kind in range(5) for one in (cut[2 * kind + 1], got[kind])]
        flat = pl.pallas_call(
            functools.partial(choose_kernel, (slots, layer, 5)),
            out_shape=[b for b in shapes for _ in range(slots)],
            in_specs=[any_spec()] * 10,
            out_specs=[any_spec()] * (5 * slots),
            scratch_shapes=[pltpu.SemaphoreType.DMA((5 * slots,))],
            compiler_params=pltpu.CompilerParams(vmem_limit_bytes=VMEM_LIMIT),
            name="choose_blocks",
        )(*pairs)
        return [flat[kind * slots : (kind + 1) * slots] for kind in range(5)]

    feats = jnp.pad(embed_time(steps), ((0, 8 - slots), (0, 0)))
    modulation = pl.pallas_call(
        functools.partial(mod_kernel, slots),
        out_shape=jax.ShapeDtypeStruct((slots, 3, feat), jnp.float32),
        in_specs=[vmem_spec(), vmem_spec()],
        out_specs=vmem_spec(),
        compiler_params=pltpu.CompilerParams(vmem_limit_bytes=VMEM_LIMIT),
        name="modulation",
    )(feats, mod_weight[0].transpose(1, 0, 2))
    other_modulation = to_core(modulation)
    mod_layers = [
        jnp.where(s == layer, modulation, other_modulation) for layer in range(2)
    ]

    first_bit, last_bits = group_bits[0], group_bits[1:]
    lines = {}

    def move(array, bit, depth, *gates):
        line = lines.setdefault(bit, [])
        gates = gates + tuple(line[-depth : len(line) - depth + 1] if len(line) >= depth else ())
        out = to_row(after(array, *gates) if gates else array, bit)
        line.append(out)
        return out

    def leave(held, kind, *gates):
        for d in offsets:
            held[kind][d ^ first_bit] = move(held[kind][d], first_bit, 2, *gates)

    start = (ends_all,)
    layers = []
    for layer in range(2):
        blocks = blocks_of(layer)
        gate = start if layer == 0 else (layers[0][1][first_bit],)
        held = [{0: after(blocks[kind][0], *gate)} for kind in range(5)]
        for kind in (0, 1, 4, 2, 3):
            for bit in offsets[1:]:
                held[kind][bit] = move(blocks[kind][1], bit, 2, *gate)
        if layer == 0:
            for kind in range(4):
                gates = {2: (held[4][offsets[-1]],), 3: tuple(x_chips[1:])}.get(kind, ())
                leave(held, kind, *gates)
        layers.append(held)
    def spread(held, kinds):
        for kind in kinds:
            for bit in last_bits:
                for d in list(held[kind]):
                    held[kind][d ^ bit] = move(held[kind][d], bit, 4)

    def by_row(held, kinds):
        return [held[kind][d] for d in range(rows) for kind in kinds]

    def attend(layer, x_pieces, gates):
        held = layers[layer]
        plan = (slots, slot_len, cols, len(x_pieces), rows, kr, bw, wc)
        return pl.pallas_call(
            functools.partial(attend_kernel, plan),
            out_shape=jax.ShapeDtypeStruct((slots * slot_len, bw), jnp.bfloat16),
            in_specs=[pl.BlockSpec(memory_space=pltpu.SMEM), vmem_spec()]
            + [any_spec()] * (len(x_pieces) + 3 * rows + slots),
            out_specs=vmem_spec(),
            scratch_shapes=[
                pltpu.VMEM((cols, slots * slot_len, wc), jnp.bfloat16),
                pltpu.VMEM((slots * slot_len, feat), jnp.bfloat16),
                pltpu.VMEM((3, feat, bw), jnp.bfloat16),
                pltpu.VMEM((slots, 2, slot_len, bw), jnp.bfloat16),
                pltpu.SemaphoreType.DMA((len(x_pieces),)),
                pltpu.SemaphoreType.DMA((3 * rows,)),
                pltpu.SemaphoreType.DMA((slots,)),
            ],
            compiler_params=pltpu.CompilerParams(vmem_limit_bytes=VMEM_LIMIT),
            name="attend_layer",
        )(
            after(ends_all, *gates) if gates else ends_all,
            mod_layers[layer],
            *x_pieces,
            *by_row(held, range(3)),
            *[held[4][d] for d in offsets],
        )

    def project(layer, attended):
        plan = (slots, slot_len, cols, rows, nr, bw, wc)
        shape = jax.ShapeDtypeStruct((slots, half, feat), jnp.bfloat16)
        return pl.pallas_call(
            functools.partial(out_kernel, plan),
            out_shape=(shape, shape),
            in_specs=[vmem_spec()] + [any_spec()] * rows,
            out_specs=(vmem_spec(), vmem_spec()),
            scratch_shapes=[
                pltpu.VMEM((rows, bw, nr), jnp.bfloat16),
                pltpu.SemaphoreType.DMA((rows,)),
            ],
            compiler_params=pltpu.CompilerParams(vmem_limit_bytes=VMEM_LIMIT),
            name="project_out",
        )(attended, *by_row(layers[layer], (3,)))

    def chip_parts(keep, passed):
        chip_sum = keep.astype(jnp.float32) + passed.astype(jnp.float32)
        return [
            chip_sum[offsets.index(di), :, dc * wc : (dc + 1) * wc] for di, dc in places
        ]

    def send_parts(parts):
        return [send_place(part.astype(jnp.bfloat16), *p) for part, p in zip(parts[1:], places[1:])]

    def finish(layer, x_own, part, arrived):
        branch = part + sum(one.astype(jnp.float32) for one in arrived)
        gate_own = lax.dynamic_slice_in_dim(mod_layers[layer][0, 2], c * wc, wc, 0)
        updated = x_own.astype(jnp.float32) + gate_own[None, :] * branch
        positions = jnp.arange(half)[:, None] + s * half
        return jnp.where(positions < patch_ends[0, NP - 1], updated, 0.0).astype(jnp.bfloat16)

    ahead = layers[1]
    spread(layers[0], range(4))
    leave(ahead, 0)
    attended = attend(0, gather(x_chips), (ahead[0][first_bit], ahead[0][offsets[-1]]))
    leave(ahead, 1)
    keep, passed = project(0, attended)
    passed = to_core(after(passed, ahead[1][first_bit], ahead[0][first_bit ^ offsets[-1]]))
    spread(ahead, (0,))
    leave(ahead, 2, passed, ahead[4][offsets[-1]])
    spread(ahead, (1,))
    parts = chip_parts(keep, passed)
    arrived = send_parts(parts)
    leave(ahead, 3, *arrived)
    spread(ahead, (2, 3))
    first = finish(0, x_half, parts[0], arrived)
    x_pieces = gather(gather_chips(first))

    keep, passed = project(1, attend(1, x_pieces, ()))
    parts = chip_parts(keep, to_core(passed))
    second = finish(1, first, parts[0], send_parts(parts))
    second_other = to_core(second)
    low = jnp.where(s == 0, first, second_other)
    high = jnp.where(s == 0, x_pieces[1], second)
    return jnp.concatenate([low, high], axis=0)[None, None]


def solution(mesh):
    return jax.shard_map(
        shards,
        mesh=mesh,
        in_specs=(
            P("row", None, "col"),
            P("row", None),
            P("row"),
            P("section", None, None, None),
            P("section", "row", None, "col"),
            P("section", "col", "row"),
            P("section", "row", None, "col"),
            P("section", "row", None, "col"),
        ),
        out_specs=P("section", "row", None, "col"),
        check_vma=False,
    )
```

```python
import functools
import math

import jax
import jax.numpy as jnp
from jax import lax
from jax.experimental import pallas as pl
from jax.experimental.pallas import tpu as pltpu
from jax.sharding import PartitionSpec as P

HD = 128
FREQ = 256
NP = 4
AXES = ("section", "row", "col")
VMEM_LIMIT = 56 * 1024 * 1024


def send_to(array, where):
    ns, nr, nc = (lax.axis_size(axis) for axis in AXES)
    pairs = []
    for s in range(ns):
        for i in range(nr):
            for c in range(nc):
                ts, ti, tc = where(s, i, c)
                pairs.append(((s * nr + i) * nc + c, (ts * nr + ti) * nc + tc))
    return lax.ppermute(array, AXES, pairs)


def to_core(array):
    return send_to(array, lambda s, i, c: (1 - s, i, c))


def to_row(array, bit):
    return send_to(array, lambda s, i, c: (s, i ^ bit, c))


def after(array, *others):
    return lax.optimization_barrier((array,) + others)[0]


def pick(array, index):
    return lax.dynamic_index_in_dim(array, index, 0, keepdims=False)


def embed_time(timestep):
    half_width = FREQ // 2
    frequency = jnp.exp(
        jnp.arange(half_width, dtype=jnp.float32) * (-math.log(10000.0) / half_width)
    )
    angles = timestep.astype(jnp.float32)[:, None] * frequency[None, :]
    return jnp.concatenate([jnp.cos(angles), jnp.sin(angles)], axis=1).astype(jnp.bfloat16)


def any_spec():
    return pl.BlockSpec(memory_space=pl.ANY)


def vmem_spec():
    return pl.BlockSpec(memory_space=pltpu.VMEM)


def attend_kernel(plan, ends_ref, mod_ref, *refs):
    slots, slot_len, cols, n_x, n_w, kr, bw, wc = plan
    x_refs, refs = refs[:n_x], refs[n_x:]
    w_refs, refs = refs[: 3 * n_w], refs[3 * n_w :]
    kv_refs, refs = refs[:slots], refs[slots:]
    out_ref, xv, xm, wv, kvv, x_sem, w_sem, kv_sem = refs
    s, i, c = (lax.axis_index(axis) for axis in AXES)
    half = slot_len // 2
    x_copies, w_copies, kv_copies = [], [], []
    place = 0
    for slot in range(slots):
        for dc in range(cols):
            for h in range(2):
                col = lax.rem(c + cols - dc, cols)
                row = slot * slot_len + jnp.where(s == h, 0, half)
                row = pl.multiple_of(row, half)
                x_copies.append(
                    pltpu.make_async_copy(
                        x_refs[place], xv.at[col, pl.ds(row, half), :], x_sem.at[place]
                    )
                )
                place += 1
    for d in range(n_w):
        rows = pl.ds(pl.multiple_of((i ^ d) * kr, 32), kr)
        for t in range(3):
            w_copies.append(
                pltpu.make_async_copy(w_refs[3 * d + t], wv.at[t, rows, :], w_sem.at[3 * d + t])
            )
    for slot in range(slots):
        kv_copies.append(pltpu.make_async_copy(kv_refs[slot], kvv.at[slot], kv_sem.at[slot]))
    for copy in x_copies + w_copies + kv_copies:
        copy.start()
    for copy in x_copies:
        copy.wait()
    feat = cols * wc
    for slot in range(slots):
        rows = pl.ds(slot * slot_len, slot_len)
        total = jnp.zeros((slot_len, 1), jnp.float32)
        squares = jnp.zeros((slot_len, 1), jnp.float32)
        for col in range(cols):
            part = xv[col, rows, :].astype(jnp.float32)
            total += jnp.sum(part, axis=-1, keepdims=True)
            squares += jnp.sum(part * part, axis=-1, keepdims=True)
        mean = total / feat
        var = squares / feat - mean * mean
        inverse = 1.0 / jnp.sqrt(var + 1e-06)
        for col in range(cols):
            span = pl.ds(col * wc, wc)
            part = xv[col, rows, :].astype(jnp.float32)
            shift = mod_ref[slot, 0:1, span]
            scale = mod_ref[slot, 1:2, span]
            xm[rows, span] = ((part - mean) * inverse * (1.0 + scale) + shift).astype(jnp.bfloat16)
    for copy in w_copies + kv_copies:
        copy.wait()
    key_at = lax.broadcasted_iota(jnp.int32, (slot_len, slot_len), 1)
    query_at = lax.broadcasted_iota(jnp.int32, (slot_len, slot_len), 0)
    contract = (((1,), (1,)), ((), ()))
    for slot in range(slots):
        rows = pl.ds(slot * slot_len, slot_len)
        raw = [
            jnp.dot(xm[rows, :], wv[t], preferred_element_type=jnp.float32) for t in range(3)
        ]
        limit = jnp.full((slot_len, slot_len), ends_ref[slot, NP - 1], jnp.int32)
        for m in range(NP - 2, -1, -1):
            limit = jnp.where(query_at < ends_ref[slot, m], ends_ref[slot, m], limit)
        fresh = key_at < limit
        valid = key_at < ends_ref[slot, NP - 1]
        for head in range(bw // HD):
            lanes = slice(head * HD, (head + 1) * HD)

            def normed(block):
                return (
                    block / jnp.sqrt(jnp.mean(block * block, axis=-1, keepdims=True) + 1e-06)
                ).astype(jnp.bfloat16)

            query = normed(raw[0][:, lanes])
            key = normed(raw[1][:, lanes])
            value = raw[2][:, lanes].astype(jnp.bfloat16)
            old_key = kvv[slot, 0, :, lanes]
            old_value = kvv[slot, 1, :, lanes]
            new_scores = lax.dot_general(query, key, contract, preferred_element_type=jnp.float32)
            old_scores = lax.dot_general(
                query, old_key, contract, preferred_element_type=jnp.float32
            )
            scores = jnp.where(fresh, new_scores, old_scores) * (1.0 / math.sqrt(HD))
            weights = jnp.where(valid, jnp.exp(scores), 0.0)
            weights = weights / jnp.sum(weights, axis=-1, keepdims=True)
            mixed = jnp.dot(
                jnp.where(fresh, weights, 0.0).astype(jnp.bfloat16),
                value,
                preferred_element_type=jnp.float32,
            ) + jnp.dot(
                jnp.where(fresh, 0.0, weights).astype(jnp.bfloat16),
                old_value,
                preferred_element_type=jnp.float32,
            )
            out_ref[rows, lanes] = mixed.astype(jnp.bfloat16)


def out_kernel(plan, attended_ref, *refs):
    slots, slot_len, cols, n_w, nr, bw, wc = plan
    o_refs, refs = refs[:n_w], refs[n_w:]
    keep_ref, pass_ref, ov, o_sem = refs
    s, i, c = (lax.axis_index(axis) for axis in AXES)
    half = slot_len // 2
    copies = []
    for d in range(n_w):
        place = lax.rem((i ^ d) + n_w - c * (n_w // cols), n_w)
        copies.append(pltpu.make_async_copy(o_refs[d], ov.at[place], o_sem.at[d]))
    for copy in copies:
        copy.start()
    for copy in copies:
        copy.wait()
    blocks = []
    for side in (s, 1 - s):
        for slot in range(slots):
            row = pl.multiple_of(slot * slot_len + side * half, half)
            blocks.append(attended_ref[pl.ds(row, half), :])
    lhs = jnp.concatenate(blocks, axis=0)
    for place in range(n_w):
        part = jnp.dot(lhs, ov[place], preferred_element_type=jnp.float32).astype(jnp.bfloat16)
        part = part.reshape(2, slots, half, nr)
        lanes = slice(place * nr, (place + 1) * nr)
        keep_ref[:, :, lanes] = part[0]
        pass_ref[:, :, lanes] = part[1]


def mod_kernel(slots, feats_ref, weight_ref, out_ref):
    for k in range(3):
        part = jnp.dot(feats_ref[...], weight_ref[k], preferred_element_type=jnp.float32)
        for slot in range(slots):
            out_ref[slot, k : k + 1, :] = part[slot : slot + 1, :]


def shards(
    hidden_in, patch_ends, timestep, mod_weight, qkv_weight, out_weight, stale_keys, stale_values
):
    s, i, c = (lax.axis_index(axis) for axis in AXES)
    sections, rows, cols = (lax.axis_size(axis) for axis in AXES)
    _, slot_len, wc = hidden_in.shape
    feat = mod_weight.shape[-1]
    kr = qkv_weight.shape[1]
    nr = out_weight.shape[2]
    half = slot_len // 2
    slots = 2 if (wc // HD) % (2 * sections) == 0 else 1
    bw = wc // (sections * slots)
    row_bits = [1 << b for b in range(rows.bit_length() - 1)]
    split_bit = 2 if slots == 2 else 0
    group_bits = [b for b in reversed(row_bits) if b != split_bit]
    offsets = [0, split_bit] if slots == 2 else [0]

    places = [(di, dc) for di in offsets for dc in range(cols)]

    def send_place(array, di, dc):
        return send_to(array, lambda si, ii, ci: (si, ii ^ di, (ci + dc) % cols))

    def gather_chips(own_half):
        return [own_half if p == (0, 0) else send_place(own_half, *p) for p in places]

    def gather(pieces):
        return [one for piece in pieces for one in (piece, to_core(piece))]

    numbers = jnp.concatenate([patch_ends[0], timestep])
    numbers = jnp.stack([numbers] + [to_row(numbers, bit) for bit in offsets[1:]])
    ends_all, steps = numbers[:, :NP], numbers[:, NP]
    x_half = lax.dynamic_slice_in_dim(hidden_in[0], s * half, half, 0)

    def columns(array, start, width):
        return lax.dynamic_slice_in_dim(array, start, width, array.ndim - 1)

    wide = slots * bw
    qkv = qkv_weight[0].transpose(1, 0, 2)
    stale = (stale_keys[0, 0], stale_values[0, 0])
    cores_kv = jnp.concatenate([columns(one, (1 - s) * wide, wide) for one in stale])
    got = [to_core(columns(qkv[t], (1 - s) * wide, wide)) for t in range(3)]
    got.append(to_core(lax.dynamic_slice_in_dim(out_weight[0], (1 - s) * wide, wide, 0)))
    got.append(to_core(cores_kv))
    mine_at = (i // 2) % 2 if slots == 2 else 0

    def block_of(layer, kind, slot):
        at = (mine_at if slot == 0 else 1 - mine_at) * bw
        if kind == 3:
            own = lax.dynamic_slice_in_dim(out_weight[0], s * wide + at, bw, 0)
            other = lax.dynamic_slice_in_dim(got[3], at, bw, 0)
        elif kind == 4:
            own = jnp.concatenate([columns(one, s * wide + at, bw) for one in stale])
            other = columns(got[4], at, bw)
        else:
            own, other = columns(qkv[kind], s * wide + at, bw), columns(got[kind], at, bw)
        block = jnp.where(s == layer, own, other)
        return block.reshape(2, slot_len, bw) if kind == 4 else block

    first_bit, last_bits = group_bits[0], group_bits[1:]
    lines = {}

    def move(array, bit, line, depth, *gates):
        line = lines.setdefault(line, [])
        gates = gates + tuple(line[-depth : len(line) - depth + 1] if len(line) >= depth else ())
        out = to_row(after(array, *gates) if gates else array, bit)
        line.append(out)
        return out

    def leave(layer, kind, *gates):
        own = [block_of(layer, kind, slot) for slot in range(slots)]
        held = {0: after(own[0], *gates) if gates else own[0]}
        for bit in offsets[1:]:
            held[bit] = move(own[1], bit, "pair", 3, *gates)
        if kind < 4:
            for d in offsets:
                held[d ^ first_bit] = move(own[1 if d else 0], d ^ first_bit, "cut", 4, *gates)
        return held

    def spread(held):
        for bit in last_bits:
            for d in list(held):
                held[d ^ bit] = move(held[d], bit, bit, 6)
        return held

    start = (ends_all,)
    layers = [{}, {}]
    for kind in (0, 1, 4, 2):
        layers[0][kind] = leave(0, kind, *start)
    early = layers[0][0][first_bit]
    x_chips = gather_chips(after(x_half, early))
    layers[0][3] = leave(0, 3, *x_chips[1:], layers[0][4][offsets[-1]])

    feats = jnp.pad(embed_time(steps), ((0, 8 - slots), (0, 0)))
    modulation = pl.pallas_call(
        functools.partial(mod_kernel, slots),
        out_shape=jax.ShapeDtypeStruct((slots, 3, feat), jnp.float32),
        in_specs=[vmem_spec(), vmem_spec()],
        out_specs=vmem_spec(),
        compiler_params=pltpu.CompilerParams(vmem_limit_bytes=VMEM_LIMIT),
        name="modulation",
    )(after(feats, early), mod_weight[0].transpose(1, 0, 2))
    other_modulation = to_core(modulation)
    mod_layers = [
        jnp.where(s == layer, modulation, other_modulation) for layer in range(2)
    ]

    def by_row(held, kinds):
        return [held[kind][d] for d in range(rows) for kind in kinds]

    def attend(layer, x_pieces, gates):
        held = layers[layer]
        plan = (slots, slot_len, cols, len(x_pieces), rows, kr, bw, wc)
        return pl.pallas_call(
            functools.partial(attend_kernel, plan),
            out_shape=jax.ShapeDtypeStruct((slots * slot_len, bw), jnp.bfloat16),
            in_specs=[pl.BlockSpec(memory_space=pltpu.SMEM), vmem_spec()]
            + [any_spec()] * (len(x_pieces) + 3 * rows + slots),
            out_specs=vmem_spec(),
            scratch_shapes=[
                pltpu.VMEM((cols, slots * slot_len, wc), jnp.bfloat16),
                pltpu.VMEM((slots * slot_len, feat), jnp.bfloat16),
                pltpu.VMEM((3, feat, bw), jnp.bfloat16),
                pltpu.VMEM((slots, 2, slot_len, bw), jnp.bfloat16),
                pltpu.SemaphoreType.DMA((len(x_pieces),)),
                pltpu.SemaphoreType.DMA((3 * rows,)),
                pltpu.SemaphoreType.DMA((slots,)),
            ],
            compiler_params=pltpu.CompilerParams(vmem_limit_bytes=VMEM_LIMIT),
            name="attend_layer",
        )(
            after(ends_all, *gates) if gates else ends_all,
            mod_layers[layer],
            *x_pieces,
            *by_row(held, range(3)),
            *[held[4][d] for d in offsets],
        )

    def project(layer, attended):
        plan = (slots, slot_len, cols, rows, nr, bw, wc)
        shape = jax.ShapeDtypeStruct((slots, half, feat), jnp.bfloat16)
        return pl.pallas_call(
            functools.partial(out_kernel, plan),
            out_shape=(shape, shape),
            in_specs=[vmem_spec()] + [any_spec()] * rows,
            out_specs=(vmem_spec(), vmem_spec()),
            scratch_shapes=[
                pltpu.VMEM((rows, bw, nr), jnp.bfloat16),
                pltpu.SemaphoreType.DMA((rows,)),
            ],
            compiler_params=pltpu.CompilerParams(vmem_limit_bytes=VMEM_LIMIT),
            name="project_out",
        )(attended, *by_row(layers[layer], (3,)))

    def chip_parts(keep, passed):
        chip_sum = keep.astype(jnp.float32) + passed.astype(jnp.float32)
        return [
            chip_sum[offsets.index(di), :, dc * wc : (dc + 1) * wc] for di, dc in places
        ]

    def send_parts(parts):
        return [send_place(part.astype(jnp.bfloat16), *p) for part, p in zip(parts[1:], places[1:])]

    def finish(layer, x_own, part, arrived):
        branch = part + sum(one.astype(jnp.float32) for one in arrived)
        gate_own = lax.dynamic_slice_in_dim(mod_layers[layer][0, 2], c * wc, wc, 0)
        updated = x_own.astype(jnp.float32) + gate_own[None, :] * branch
        positions = jnp.arange(half)[:, None] + s * half
        return jnp.where(positions < patch_ends[0, NP - 1], updated, 0.0).astype(jnp.bfloat16)

    ahead = layers[1]
    for kind in range(4):
        spread(layers[0][kind])
    across = first_bit ^ offsets[-1]
    ahead[0] = leave(1, 0)
    attended = attend(0, gather(x_chips), ())
    ahead[1] = leave(1, 1)
    spread(ahead[0])
    keep, passed = project(0, attended)
    passed = to_core(after(passed, *(ahead[0][d] for d in (offsets[-1], first_bit, across))))
    parts = chip_parts(keep, passed)
    arrived = send_parts(parts)
    ahead[4] = leave(1, 4)
    ahead[2] = leave(1, 2, passed)
    spread(ahead[1])
    first = finish(0, x_half, parts[0], arrived)
    ahead[3] = leave(1, 3, ahead[4][offsets[-1]], *arrived)
    spread(ahead[2])
    spread(ahead[3])
    x_pieces = gather(gather_chips(after(first, ahead[1][first_bit])))

    keep, passed = project(1, attend(1, x_pieces, ()))
    parts = chip_parts(keep, to_core(passed))
    second = finish(1, first, parts[0], send_parts(parts))
    second_other = to_core(second)
    low = jnp.where(s == 0, first, second_other)
    high = jnp.where(s == 0, x_pieces[1], second)
    return jnp.concatenate([low, high], axis=0)[None, None]


def solution(mesh):
    return jax.shard_map(
        shards,
        mesh=mesh,
        in_specs=(
            P("row", None, "col"),
            P("row", None),
            P("row"),
            P("section", None, None, None),
            P("section", "row", None, "col"),
            P("section", "col", "row"),
            P("section", "row", None, "col"),
            P("section", "row", None, "col"),
        ),
        out_specs=P("section", "row", None, "col"),
        check_vma=False,
    )
```

```python
import functools
import math

import jax
import jax.numpy as jnp
from jax import lax
from jax.experimental import pallas as pl
from jax.experimental.pallas import tpu as pltpu
from jax.sharding import PartitionSpec as P

HD = 128
FREQ = 256
NP = 4
AXES = ("section", "row", "col")
VMEM_LIMIT = 56 * 1024 * 1024


def send_to(array, where):
    ns, nr, nc = (lax.axis_size(axis) for axis in AXES)
    pairs = []
    for s in range(ns):
        for i in range(nr):
            for c in range(nc):
                ts, ti, tc = where(s, i, c)
                pairs.append(((s * nr + i) * nc + c, (ts * nr + ti) * nc + tc))
    return lax.ppermute(array, AXES, pairs)


def to_core(array):
    return send_to(array, lambda s, i, c: (1 - s, i, c))


def after(array, *others):
    return lax.optimization_barrier((array,) + others)[0]


def pick(array, index):
    return lax.dynamic_index_in_dim(array, index, 0, keepdims=False)


def embed_time(timestep):
    half_width = FREQ // 2
    frequency = jnp.exp(
        jnp.arange(half_width, dtype=jnp.float32) * (-math.log(10000.0) / half_width)
    )
    angles = timestep.astype(jnp.float32)[:, None] * frequency[None, :]
    return jnp.concatenate([jnp.cos(angles), jnp.sin(angles)], axis=1).astype(jnp.bfloat16)


def any_spec():
    return pl.BlockSpec(memory_space=pl.ANY)


def vmem_spec():
    return pl.BlockSpec(memory_space=pltpu.VMEM)


def load_rows(pieces, target, sem, first, rows_each):
    i = lax.axis_index("row")
    copies = []
    for d, piece in enumerate(pieces):
        if rows_each is None:
            place = target.at[i ^ d]
        else:
            place = target.at[pl.ds(pl.multiple_of((i ^ d) * rows_each, 32), rows_each), :]
        copies.append(pltpu.make_async_copy(piece, place, sem.at[first + d]))
        copies[-1].start()
    return copies


def fresh_and_valid(ends_ref, slot, slot_len):
    key_at = lax.broadcasted_iota(jnp.int32, (slot_len, slot_len), 1)
    query_at = lax.broadcasted_iota(jnp.int32, (slot_len, slot_len), 0)
    limit = jnp.full((slot_len, slot_len), ends_ref[slot, NP - 1], jnp.int32)
    for m in range(NP - 2, -1, -1):
        limit = jnp.where(query_at < ends_ref[slot, m], ends_ref[slot, m], limit)
    return key_at < limit, key_at < ends_ref[slot, NP - 1]


def scores_kernel(plan, ends_ref, mod_ref, *refs):
    slots, slot_len, cols, n_x, n_w, kr, bw, wc = plan
    x_refs, refs = refs[:n_x], refs[n_x:]
    w_refs, refs = (refs[:n_w], refs[n_w : 2 * n_w]), refs[2 * n_w :]
    kv_refs, refs = refs[:slots], refs[slots:]
    xm, weights_ref, xv, wv, kvv, x_sem, w_sem, kv_sem = refs
    s, c = lax.axis_index("section"), lax.axis_index("col")
    half = slot_len // 2
    x_copies, w_copies, kv_copies = [], [], []
    for slot in range(slots):
        for dc in range(cols):
            for h in range(2):
                place = len(x_copies)
                col = lax.rem(c + cols - dc, cols)
                row = slot * slot_len + jnp.where(s == h, 0, half)
                row = pl.multiple_of(row, half)
                x_copies.append(
                    pltpu.make_async_copy(
                        x_refs[place], xv.at[col, pl.ds(row, half), :], x_sem.at[place]
                    )
                )
                x_copies[-1].start()
    for t in range(2):
        w_copies.append(load_rows(w_refs[t], wv.at[t], w_sem, t * n_w, kr))
    for slot in range(slots):
        kv_copies.append(
            pltpu.make_async_copy(kv_refs[slot].at[0], kvv.at[slot], kv_sem.at[slot])
        )
        kv_copies[-1].start()
    for copy in x_copies:
        copy.wait()
    feat = cols * wc
    for slot in range(slots):
        rows = pl.ds(slot * slot_len, slot_len)
        total = jnp.zeros((slot_len, 1), jnp.float32)
        squares = jnp.zeros((slot_len, 1), jnp.float32)
        for col in range(cols):
            part = xv[col, rows, :].astype(jnp.float32)
            total += jnp.sum(part, axis=-1, keepdims=True)
            squares += jnp.sum(part * part, axis=-1, keepdims=True)
        mean = total / feat
        var = squares / feat - mean * mean
        inverse = 1.0 / jnp.sqrt(var + 1e-06)
        for col in range(cols):
            span = pl.ds(col * wc, wc)
            part = xv[col, rows, :].astype(jnp.float32)
            shift = mod_ref[slot, 0:1, span]
            scale = mod_ref[slot, 1:2, span]
            xm[rows, span] = ((part - mean) * inverse * (1.0 + scale) + shift).astype(jnp.bfloat16)
    for copy in w_copies[0] + w_copies[1] + kv_copies:
        copy.wait()
    contract = (((1,), (1,)), ((), ()))

    def normed(block):
        return (
            block / jnp.sqrt(jnp.mean(block * block, axis=-1, keepdims=True) + 1e-06)
        ).astype(jnp.bfloat16)

    for slot in range(slots):
        rows = pl.ds(slot * slot_len, slot_len)
        raw = [jnp.dot(xm[rows, :], wv[t], preferred_element_type=jnp.float32) for t in range(2)]
        fresh, valid = fresh_and_valid(ends_ref, slot, slot_len)
        for head in range(bw // HD):
            lanes = slice(head * HD, (head + 1) * HD)
            query, key = normed(raw[0][:, lanes]), normed(raw[1][:, lanes])
            new_scores = lax.dot_general(query, key, contract, preferred_element_type=jnp.float32)
            old_scores = lax.dot_general(
                query, kvv[slot, :, lanes], contract, preferred_element_type=jnp.float32
            )
            scores = jnp.where(fresh, new_scores, old_scores) * (1.0 / math.sqrt(HD))
            weights = jnp.where(valid, jnp.exp(scores), 0.0)
            weights = weights / jnp.sum(weights, axis=-1, keepdims=True)
            weights_ref[slot, head] = weights.astype(jnp.bfloat16)


def mix_kernel(plan, ends_ref, xm_ref, weights_ref, *refs):
    slots, slot_len, cols, n_w, kr, nr, bw, wc = plan
    v_refs, o_refs, refs = refs[:n_w], refs[n_w : 2 * n_w], refs[2 * n_w :]
    kv_refs, refs = refs[:slots], refs[slots:]
    keep_ref, pass_ref, wv, ov, kvv, att, w_sem, kv_sem = refs
    s, i, c = (lax.axis_index(axis) for axis in AXES)
    half = slot_len // 2
    copies = load_rows(v_refs, wv, w_sem, 0, kr)
    for slot in range(slots):
        copies.append(
            pltpu.make_async_copy(kv_refs[slot].at[1], kvv.at[slot], kv_sem.at[slot])
        )
        copies[-1].start()
    o_copies = load_rows(o_refs, ov, w_sem, n_w, None)
    for copy in copies:
        copy.wait()
    for slot in range(slots):
        rows = pl.ds(slot * slot_len, slot_len)
        raw = jnp.dot(xm_ref[rows, :], wv[...], preferred_element_type=jnp.float32)
        value = raw.astype(jnp.bfloat16)
        fresh, _ = fresh_and_valid(ends_ref, slot, slot_len)
        for head in range(bw // HD):
            lanes = slice(head * HD, (head + 1) * HD)
            weights = weights_ref[slot, head]
            none = jnp.zeros_like(weights)
            mixed = jnp.dot(
                jnp.where(fresh, weights, none),
                value[:, lanes],
                preferred_element_type=jnp.float32,
            ) + jnp.dot(
                jnp.where(fresh, none, weights),
                kvv[slot, :, lanes],
                preferred_element_type=jnp.float32,
            )
            att[rows, lanes] = mixed.astype(jnp.bfloat16)
    for copy in o_copies:
        copy.wait()
    blocks = []
    for side in (s, 1 - s):
        for slot in range(slots):
            row = pl.multiple_of(slot * slot_len + side * half, half)
            blocks.append(att[pl.ds(row, half), :])
    lhs = jnp.concatenate(blocks, axis=0)
    for place in range(n_w):
        row = lax.rem(c * (n_w // cols) + place, n_w)
        part = jnp.dot(lhs, ov[row], preferred_element_type=jnp.float32).astype(jnp.bfloat16)
        part = part.reshape(2, slots, half, nr)
        lanes = slice(place * nr, (place + 1) * nr)
        keep_ref[:, :, lanes] = part[0]
        pass_ref[:, :, lanes] = part[1]


def mod_kernel(slots, feats_ref, weight_ref, out_ref):
    for k in range(3):
        part = jnp.dot(feats_ref[...], weight_ref[k], preferred_element_type=jnp.float32)
        for slot in range(slots):
            out_ref[slot, k : k + 1, :] = part[slot : slot + 1, :]


GATES = {
    "V0.4": ("Q0.4",),
    "V0.6": ("Q0.6",),
    "O0.4": ("K0.4",),
    "O0.6": ("K0.6",),
    "Q1.4": ("V0.4",),
    "Q1.6": ("V0.6",),
    "K1.4": ("O0.4",),
    "K1.6": ("O0.6",),
    "V1.4": ("Q1.4",),
    "V1.6": ("Q1.6",),
    "O1.4": ("K1.4",),
    "O1.6": ("K1.6",),
    "O0.2": ("Q0.2",),
    "Q1.2": ("K0.2",),
    "K1.2": ("S0.2",),
    "V1.2": ("V0.2",),
    "O1.2": ("O0.2",),
    "S1.2": ("Q1.2",),
    "K0.1": ("Q0.1",),
    "K0.3": ("Q0.3",),
    "Q0.5": ("K0.1",),
    "Q0.7": ("K0.3",),
    "V0.1": ("Q0.5",),
    "V0.3": ("Q0.7",),
    "K0.5": ("V0.1",),
    "K0.7": ("V0.3",),
    "O0.1": ("K0.5",),
    "O0.3": ("K0.7",),
    "V0.5": ("O0.1",),
    "V0.7": ("O0.3",),
    "Q1.1": ("V0.5",),
    "Q1.3": ("V0.7",),
    "O0.5": ("Q1.1",),
    "O0.7": ("Q1.3",),
    "K1.1": ("O0.5",),
    "K1.3": ("O0.7",),
    "Q1.5": ("K1.1",),
    "Q1.7": ("K1.3",),
    "V1.1": ("Q1.5",),
    "V1.3": ("Q1.7",),
    "K1.5": ("V1.1",),
    "K1.7": ("V1.3",),
    "O1.1": ("K1.5",),
    "O1.3": ("K1.7",),
    "V1.5": ("O1.1",),
    "V1.7": ("O1.3",),
    "O1.5": ("V1.5",),
    "O1.7": ("V1.7",),
    "n": ("aQ",),
    "x.0.0": ("Q0.4",),
    "m": ("Q0.6",),
    "p0": ("Q1.4", "Q1.6",),
    "r0.0.1": ("K1.4",),
    "g.2.0": ("K1.6",),
    "k0": ("Q1.2",),
}
TREE = ("x", "r0", "g", )


def shards(
    hidden_in, patch_ends, timestep, mod_weight, qkv_weight, out_weight, stale_keys, stale_values
):
    s, i, c = (lax.axis_index(axis) for axis in AXES)
    sections, rows, cols = (lax.axis_size(axis) for axis in AXES)
    _, slot_len, wc = hidden_in.shape
    feat = mod_weight.shape[-1]
    kr, nr = qkv_weight.shape[1], out_weight.shape[2]
    half = slot_len // 2
    slots = 2 if (wc // HD) % (2 * sections) == 0 else 1
    bw = wc // (sections * slots)
    pair_bit = 2 if slots == 2 else 0
    group_bits = [1 << b for b in reversed(range(rows.bit_length() - 1)) if 1 << b != pair_bit]
    first_bit, last_bits = group_bits[0], group_bits[1:]
    offsets = [0, pair_bit] if slots == 2 else [0]
    places = [(di, dc) for di in offsets for dc in range(cols)]
    mine_at = (i // 2) % 2 if slots == 2 else 0
    gates = GATES if rows == 8 and slots == 2 else {}
    made, steps = {}, {}

    def get(name):
        if name not in made:
            made[name] = None
            made[name] = steps[name]()
        return made[name]

    def gated(array, name):
        waits = [get(other) for other in gates.get(name, ())]
        return after(array, *waits) if waits else array

    def send(name, array, di=0, dc=0):
        def where(si, ii, ci):
            return si, ii ^ di, (ci + dc) % cols

        return send_to(gated(array, name), where)

    def swap(name, array):
        return send_to(gated(array, name), lambda si, ii, ci: (1 - si, ii, ci))

    def step(name):
        def note(make):
            steps[name] = make
            return make

        return note

    wide = slots * bw
    qkv = qkv_weight[0].transpose(1, 0, 2)
    stale = (stale_keys[0, 0], stale_values[0, 0])

    def columns(array, start, width):
        return lax.dynamic_slice_in_dim(array, start, width, array.ndim - 1)

    def cut(kind, start, width):
        if kind == "O":
            return lax.dynamic_slice_in_dim(out_weight[0], start, width, 0)
        if kind == "S":
            return jnp.concatenate([columns(one, start, width) for one in stale])
        return columns(qkv["QKV".index(kind)], start, width)

    def block_of(kind, layer, slot):
        at = (mine_at if slot == 0 else 1 - mine_at) * bw
        got = get("a" + kind)
        other = lax.dynamic_slice_in_dim(got, at, bw, 0) if kind == "O" else columns(got, at, bw)
        block = jnp.where(s == layer, cut(kind, s * wide + at, bw), other)
        return block.reshape(2, slot_len, bw) if kind == "S" else block

    for kind in "QKVOS":
        step("a" + kind)(
            lambda kind=kind: swap("a" + kind, cut(kind, (1 - s) * wide, wide))
        )

    def move(kind, layer, d):
        name = f"{kind}{layer}.{d}"
        for bit in reversed(last_bits):
            if d & bit:
                return send(name, get(f"{kind}{layer}.{d ^ bit}"), bit)
        block = block_of(kind, layer, 1 if d & pair_bit else 0)
        return send(name, block, d) if d else gated(block, name)

    for layer in range(2):
        for kind in "QKVO":
            for d in range(rows):
                step(f"{kind}{layer}.{d}")(functools.partial(move, kind, layer, d))
        for d in offsets:
            step(f"S{layer}.{d}")(functools.partial(move, "S", layer, d))

    def of_rows(kind, layer):
        return [get(f"{kind}{layer}.{d}") for d in range(rows)]

    def stale_of(layer):
        return [get(f"S{layer}.{d}") for d in offsets]

    @step("n")
    def _():
        numbers = jnp.concatenate([patch_ends[0], timestep])
        return jnp.stack([numbers] + [send("n", numbers, di) for di in offsets[1:]])

    @step("m")
    def _():
        feats = jnp.pad(embed_time(get("n")[:, NP]), ((0, 8 - slots), (0, 0)))
        own = pl.pallas_call(
            functools.partial(mod_kernel, slots),
            out_shape=jax.ShapeDtypeStruct((slots, 3, feat), jnp.float32),
            in_specs=[vmem_spec(), vmem_spec()],
            out_specs=vmem_spec(),
            compiler_params=pltpu.CompilerParams(vmem_limit_bytes=VMEM_LIMIT),
            name="modulation",
        )(gated(feats, "m"), mod_weight[0].transpose(1, 0, 2))
        other = swap("mc", own)
        return [jnp.where(s == layer, own, other) for layer in range(2)]

    x_half = lax.dynamic_slice_in_dim(hidden_in[0], s * half, half, 0)
    step("x.0.0")(lambda: gated(x_half, "x.0.0"))
    step("g.0.0")(lambda: finish(0, x_half))
    for kind in "xg":
        for di, dc in places:
            name = f"{kind}.{di}.{dc}"

            def bring(kind=kind, name=name, di=di, dc=dc):
                if dc and kind in TREE:
                    return send(name, get(f"{kind}.{di}.0"), 0, dc)
                return send(name, get(f"{kind}.0.0"), di, dc)

            if (di, dc) != (0, 0):
                step(name)(bring)
            step(name + "c")(lambda name=name: swap(name + "c", get(name)))

    def x_pieces(kind):
        return [get(f"{kind}.{di}.{dc}" + end) for di, dc in places for end in ("", "c")]

    def scores(layer):
        pieces = x_pieces("xg"[layer])
        plan = (slots, slot_len, cols, len(pieces), rows, kr, bw, wc)
        return pl.pallas_call(
            functools.partial(scores_kernel, plan),
            out_shape=(
                jax.ShapeDtypeStruct((slots * slot_len, feat), jnp.bfloat16),
                jax.ShapeDtypeStruct((slots, bw // HD, slot_len, slot_len), jnp.bfloat16),
            ),
            in_specs=[pl.BlockSpec(memory_space=pltpu.SMEM), vmem_spec()]
            + [any_spec()] * (len(pieces) + 2 * rows + slots),
            out_specs=(vmem_spec(), vmem_spec()),
            scratch_shapes=[
                pltpu.VMEM((cols, slots * slot_len, wc), jnp.bfloat16),
                pltpu.VMEM((2, feat, bw), jnp.bfloat16),
                pltpu.VMEM((slots, slot_len, bw), jnp.bfloat16),
                pltpu.SemaphoreType.DMA((len(pieces),)),
                pltpu.SemaphoreType.DMA((2 * rows,)),
                pltpu.SemaphoreType.DMA((slots,)),
            ],
            compiler_params=pltpu.CompilerParams(vmem_limit_bytes=VMEM_LIMIT),
            name="scores",
        )(
            gated(get("n")[:, :NP], f"k{layer}"),
            get("m")[layer],
            *pieces,
            *of_rows("Q", layer),
            *of_rows("K", layer),
            *stale_of(layer),
        )

    def mix(layer):
        plan = (slots, slot_len, cols, rows, kr, nr, bw, wc)
        shape = jax.ShapeDtypeStruct((slots, half, feat), jnp.bfloat16)
        return pl.pallas_call(
            functools.partial(mix_kernel, plan),
            out_shape=(shape, shape),
            in_specs=[pl.BlockSpec(memory_space=pltpu.SMEM), vmem_spec(), vmem_spec()]
            + [any_spec()] * (2 * rows + slots),
            out_specs=(vmem_spec(), vmem_spec()),
            scratch_shapes=[
                pltpu.VMEM((feat, bw), jnp.bfloat16),
                pltpu.VMEM((rows, bw, nr), jnp.bfloat16),
                pltpu.VMEM((slots, slot_len, bw), jnp.bfloat16),
                pltpu.VMEM((slots * slot_len, bw), jnp.bfloat16),
                pltpu.SemaphoreType.DMA((2 * rows,)),
                pltpu.SemaphoreType.DMA((slots,)),
            ],
            compiler_params=pltpu.CompilerParams(vmem_limit_bytes=VMEM_LIMIT),
            name="mix",
        )(
            gated(get("n")[:, :NP], f"v{layer}"),
            *get(f"k{layer}"),
            *of_rows("V", layer),
            *of_rows("O", layer),
            *stale_of(layer),
        )

    def parts(layer):
        keep, passed = get(f"v{layer}")
        total = keep.astype(jnp.float32) + get(f"p{layer}").astype(jnp.float32)
        return {
            (di, dc): total[offsets.index(di), :, dc * wc : (dc + 1) * wc] for di, dc in places
        }

    def summed(layer, di):
        part = get(f"t{layer}")[di, 0]
        for dc in range(1, cols):
            part = part + get(f"r{layer}.{di}.{dc}").astype(jnp.float32)
        return part

    def give(layer, di, dc):
        name = f"r{layer}.{di}.{dc}"
        if f"r{layer}" not in TREE:
            return send(name, get(f"t{layer}")[di, dc].astype(jnp.bfloat16), di, dc)
        if dc:
            return send(name, get(f"t{layer}")[di, dc].astype(jnp.bfloat16), 0, dc)
        return send(name, get(f"u{layer}.{di}").astype(jnp.bfloat16), di, 0)

    for layer in range(2):
        step(f"k{layer}")(functools.partial(scores, layer))
        step(f"v{layer}")(functools.partial(mix, layer))
        step(f"p{layer}")(lambda layer=layer: swap(f"p{layer}", get(f"v{layer}")[1]))
        step(f"t{layer}")(functools.partial(parts, layer))
        for di, dc in places:
            if (di, dc) != (0, 0):
                step(f"r{layer}.{di}.{dc}")(functools.partial(give, layer, di, dc))
        for di in offsets:
            step(f"u{layer}.{di}")(functools.partial(summed, layer, di))

    def finish(layer, x_own):
        if f"r{layer}" in TREE:
            branch = get(f"u{layer}.0")
            for di in offsets[1:]:
                branch = branch + get(f"r{layer}.{di}.0").astype(jnp.float32)
        else:
            branch = get(f"t{layer}")[0, 0]
            for di, dc in places[1:]:
                branch = branch + get(f"r{layer}.{di}.{dc}").astype(jnp.float32)
        gate_own = columns(get("m")[layer][0, 2], c * wc, wc)
        updated = x_own.astype(jnp.float32) + gate_own[None, :] * branch
        positions = jnp.arange(half)[:, None] + s * half
        return jnp.where(positions < patch_ends[0, NP - 1], updated, 0.0).astype(jnp.bfloat16)

    first = get("g.0.0")
    second = finish(1, first)
    low = jnp.where(s == 0, first, swap("e", second))
    high = jnp.where(s == 0, get("g.0.0c"), second)
    return jnp.concatenate([low, high], axis=0)[None, None]


def solution(mesh):
    return jax.shard_map(
        shards,
        mesh=mesh,
        in_specs=(
            P("row", None, "col"),
            P("row", None),
            P("row"),
            P("section", None, None, None),
            P("section", "row", None, "col"),
            P("section", "col", "row"),
            P("section", "row", None, "col"),
            P("section", "row", None, "col"),
        ),
        out_specs=P("section", "row", None, "col"),
        check_vma=False,
    )
```

```python
import functools
import math

import jax
import jax.numpy as jnp
from jax import lax
from jax.experimental import pallas as pl
from jax.experimental.pallas import tpu as pltpu
from jax.sharding import PartitionSpec as P

HD = 128
FREQ = 256
NP = 4
AXES = ("section", "row", "col")
VMEM_LIMIT = 56 * 1024 * 1024


def send_to(array, where):
    ns, nr, nc = (lax.axis_size(axis) for axis in AXES)
    pairs = []
    for s in range(ns):
        for i in range(nr):
            for c in range(nc):
                ts, ti, tc = where(s, i, c)
                pairs.append(((s * nr + i) * nc + c, (ts * nr + ti) * nc + tc))
    return lax.ppermute(array, AXES, pairs)


def to_core(array):
    return send_to(array, lambda s, i, c: (1 - s, i, c))


def after(array, *others):
    return lax.optimization_barrier((array,) + others)[0]


def pick(array, index):
    return lax.dynamic_index_in_dim(array, index, 0, keepdims=False)


def embed_time(timestep):
    half_width = FREQ // 2
    frequency = jnp.exp(
        jnp.arange(half_width, dtype=jnp.float32) * (-math.log(10000.0) / half_width)
    )
    angles = timestep.astype(jnp.float32)[:, None] * frequency[None, :]
    return jnp.concatenate([jnp.cos(angles), jnp.sin(angles)], axis=1).astype(jnp.bfloat16)


def any_spec():
    return pl.BlockSpec(memory_space=pl.ANY)


def vmem_spec():
    return pl.BlockSpec(memory_space=pltpu.VMEM)


def load_rows(pieces, target, sem, first, rows_each):
    i = lax.axis_index("row")
    copies = []
    for d, piece in enumerate(pieces):
        if rows_each is None:
            place = target.at[i ^ d]
        else:
            place = target.at[pl.ds(pl.multiple_of((i ^ d) * rows_each, 32), rows_each), :]
        copies.append(pltpu.make_async_copy(piece, place, sem.at[first + d]))
        copies[-1].start()
    return copies


def fresh_and_valid(ends_ref, slot, slot_len):
    key_at = lax.broadcasted_iota(jnp.int32, (slot_len, slot_len), 1)
    query_at = lax.broadcasted_iota(jnp.int32, (slot_len, slot_len), 0)
    limit = jnp.full((slot_len, slot_len), ends_ref[slot, NP - 1], jnp.int32)
    for m in range(NP - 2, -1, -1):
        limit = jnp.where(query_at < ends_ref[slot, m], ends_ref[slot, m], limit)
    return key_at < limit, key_at < ends_ref[slot, NP - 1]


def load_x(plan, x_refs, xv, sem):
    slots, slot_len, cols = plan
    s, c = lax.axis_index("section"), lax.axis_index("col")
    half = slot_len // 2
    copies = []
    for slot in range(slots):
        for dc in range(cols):
            for h in range(2):
                place = len(copies)
                col = lax.rem(c + cols - dc, cols)
                row = pl.multiple_of(slot * slot_len + jnp.where(s == h, 0, half), half)
                copies.append(
                    pltpu.make_async_copy(
                        x_refs[place], xv.at[col, pl.ds(row, half), :], sem.at[place]
                    )
                )
                copies[-1].start()
    return copies


def modulate(plan, wc, mod_ref, xv, xm):
    slots, slot_len, cols = plan
    feat = cols * wc
    for slot in range(slots):
        rows = pl.ds(slot * slot_len, slot_len)
        total = jnp.zeros((slot_len, 1), jnp.float32)
        squares = jnp.zeros((slot_len, 1), jnp.float32)
        for col in range(cols):
            part = xv[col, rows, :].astype(jnp.float32)
            total += jnp.sum(part, axis=-1, keepdims=True)
            squares += jnp.sum(part * part, axis=-1, keepdims=True)
        mean = total / feat
        var = squares / feat - mean * mean
        inverse = lax.rsqrt(var + 1e-06)
        for col in range(cols):
            span = pl.ds(col * wc, wc)
            part = xv[col, rows, :].astype(jnp.float32)
            shift = mod_ref[slot, 0:1, span]
            scale = mod_ref[slot, 1:2, span]
            xm[rows, span] = ((part - mean) * inverse * (1.0 + scale) + shift).astype(jnp.bfloat16)


def modulate_kernel(plan, wc, mod_ref, *refs):
    n_x = len(refs) - 3
    x_refs, (xm, xv, sem) = refs[:n_x], refs[n_x:]
    for copy in load_x(plan, x_refs, xv, sem):
        copy.wait()
    modulate(plan, wc, mod_ref, xv, xm)


def scores_kernel(plan, ends_ref, *refs):
    slots, slot_len, n_w, kr, bw = plan
    x_ref, refs = refs[0], refs[1:]
    w_refs, refs = (refs[:n_w], refs[n_w : 2 * n_w]), refs[2 * n_w :]
    kv_refs, refs = refs[:slots], refs[slots:]
    weights_ref, xm, wv, kvv, x_sem, w_sem, kv_sem = refs
    x_copies = [pltpu.make_async_copy(x_ref, xm, x_sem.at[0])]
    x_copies[0].start()
    copies = load_rows(w_refs[0], wv.at[0], w_sem, 0, kr)
    copies += load_rows(w_refs[1], wv.at[1], w_sem, n_w, kr)
    for slot in range(slots):
        one = kv_refs[slot].at[0]
        target = kvv.at[slot, pl.ds(slot_len, slot_len), :]
        copies.append(pltpu.make_async_copy(one, target, kv_sem.at[slot]))
        copies[-1].start()
    for copy in x_copies + copies:
        copy.wait()
    contract = (((1,), (1,)), ((), ()))

    def normed(block):
        mean = jnp.mean(block * block, axis=-1, keepdims=True)
        return (block * lax.rsqrt(mean + 1e-06)).astype(jnp.bfloat16)

    for slot in range(slots):
        rows = pl.ds(slot * slot_len, slot_len)
        raw = [jnp.dot(xm[rows, :], wv[t], preferred_element_type=jnp.float32) for t in range(2)]
        fresh, valid = fresh_and_valid(ends_ref, slot, slot_len)
        for head in range(bw // HD):
            lanes = slice(head * HD, (head + 1) * HD)
            query = normed(raw[0][:, lanes])
            kvv[slot, 0:slot_len, lanes] = normed(raw[1][:, lanes])
            both = lax.dot_general(
                query, kvv[slot, :, lanes], contract, preferred_element_type=jnp.float32
            )
            scores = jnp.where(fresh, both[:, :slot_len], both[:, slot_len:])
            weights = jnp.where(valid, jnp.exp(scores * (1.0 / math.sqrt(HD))), 0.0)
            weights = weights * (1.0 / jnp.sum(weights, axis=-1, keepdims=True))
            weights_ref[slot, head, :, 0:slot_len] = jnp.where(fresh, weights, 0.0).astype(
                jnp.bfloat16
            )
            weights_ref[slot, head, :, slot_len:] = jnp.where(fresh, 0.0, weights).astype(
                jnp.bfloat16
            )


def mix_kernel(plan, x_ref, weights_ref, *refs):
    slots, slot_len, cols, n_w, kr, nr, bw, wc = plan
    v_refs, o_refs, refs = refs[:n_w], refs[n_w : 2 * n_w], refs[2 * n_w :]
    kv_refs, refs = refs[:slots], refs[slots:]
    keep_ref, pass_ref, xm, pv, wv, ov, kvv, att, x_sem, w_sem, kv_sem = refs
    s, c = lax.axis_index("section"), lax.axis_index("col")
    half = slot_len // 2
    x_copy = pltpu.make_async_copy(x_ref, xm, x_sem.at[0])
    x_copy.start()
    copies = load_rows(v_refs, wv, w_sem, 0, kr)
    p_copy = pltpu.make_async_copy(weights_ref, pv, x_sem.at[1])
    p_copy.start()
    late = [p_copy]
    for slot in range(slots):
        one = kv_refs[slot].at[1]
        target = kvv.at[slot, pl.ds(slot_len, slot_len), :]
        late.append(pltpu.make_async_copy(one, target, kv_sem.at[slot]))
        late[-1].start()
    o_copies = load_rows(o_refs, ov, w_sem, n_w, None)
    for copy in [x_copy] + copies:
        copy.wait()
    for slot in range(slots):
        rows = pl.ds(slot * slot_len, slot_len)
        raw = jnp.dot(xm[rows, :], wv[...], preferred_element_type=jnp.float32)
        kvv[slot, 0:slot_len, :] = raw.astype(jnp.bfloat16)
    for copy in late:
        copy.wait()
    for slot in range(slots):
        rows = pl.ds(slot * slot_len, slot_len)
        for head in range(bw // HD):
            lanes = slice(head * HD, (head + 1) * HD)
            mixed = jnp.dot(pv[slot, head], kvv[slot, :, lanes], preferred_element_type=jnp.float32)
            att[rows, lanes] = mixed.astype(jnp.bfloat16)
    for copy in o_copies:
        copy.wait()
    for side, out_ref in ((1 - s, pass_ref), (s, keep_ref)):
        blocks = []
        for slot in range(slots):
            row = pl.multiple_of(slot * slot_len + side * half, half)
            blocks.append(att[pl.ds(row, half), :])
        lhs = jnp.concatenate(blocks, axis=0)
        for place in range(n_w):
            row = lax.rem(c * (n_w // cols) + place, n_w)
            part = jnp.dot(lhs, ov[row], preferred_element_type=jnp.float32).astype(jnp.bfloat16)
            for slot in range(slots):
                out_ref[slot, :, place * nr : (place + 1) * nr] = part[
                    slot * half : (slot + 1) * half
                ]


def mod_kernel(slots, feats_ref, weight_ref, out_ref):
    for k in range(3):
        part = jnp.dot(feats_ref[...], weight_ref[k], preferred_element_type=jnp.float32)
        for slot in range(slots):
            out_ref[slot, k : k + 1, :] = part[slot : slot + 1, :]


GATES = {
    "V0.4": ("Q0.4",),
    "V0.6": ("Q0.6",),
    "O0.4": ("K0.4",),
    "O0.6": ("K0.6",),
    "Q1.4": ("V0.4",),
    "Q1.6": ("V0.6",),
    "K1.4": ("O0.4",),
    "K1.6": ("O0.6",),
    "V1.4": ("Q1.4",),
    "V1.6": ("Q1.6",),
    "O1.4": ("K1.4",),
    "O1.6": ("K1.6",),
    "O0.2": ("Q0.2",),
    "Q1.2": ("K0.2",),
    "K1.2": ("S0.2",),
    "V1.2": ("V0.2",),
    "O1.2": ("O0.2",),
    "S1.2": ("Q1.2",),
    "K0.1": ("Q0.1",),
    "K0.3": ("Q0.3",),
    "Q0.5": ("K0.1",),
    "Q0.7": ("K0.3",),
    "V0.1": ("Q0.5",),
    "V0.3": ("Q0.7",),
    "K0.5": ("V0.1",),
    "K0.7": ("V0.3",),
    "O0.1": ("K0.5",),
    "O0.3": ("K0.7",),
    "V0.5": ("O0.1",),
    "V0.7": ("O0.3",),
    "Q1.1": ("V0.5",),
    "Q1.3": ("V0.7",),
    "O0.5": ("Q1.1",),
    "O0.7": ("Q1.3",),
    "K1.1": ("O0.5",),
    "K1.3": ("O0.7",),
    "Q1.5": ("K1.1",),
    "Q1.7": ("K1.3",),
    "V1.1": ("Q1.5",),
    "V1.3": ("Q1.7",),
    "K1.5": ("V1.1",),
    "K1.7": ("V1.3",),
    "O1.1": ("K1.5",),
    "O1.3": ("K1.7",),
    "V1.5": ("O1.1",),
    "V1.7": ("O1.3",),
    "O1.5": ("V1.5",),
    "O1.7": ("V1.7",),
    "n": ("aQ",),
    "x.0.0": ("Q0.4",),
    "m": ("Q0.6",),
    "p0": ("Q1.4", "Q1.6",),
    "r0.0.1": ("K1.4",),
    "g.2.0": ("K1.6",),
    "k0": ("Q1.2",),
}
TREE = ("x", "r0", "g", )


def shards(
    hidden_in, patch_ends, timestep, mod_weight, qkv_weight, out_weight, stale_keys, stale_values
):
    s, i, c = (lax.axis_index(axis) for axis in AXES)
    sections, rows, cols = (lax.axis_size(axis) for axis in AXES)
    _, slot_len, wc = hidden_in.shape
    feat = mod_weight.shape[-1]
    kr, nr = qkv_weight.shape[1], out_weight.shape[2]
    half = slot_len // 2
    slots = 2 if (wc // HD) % (2 * sections) == 0 else 1
    bw = wc // (sections * slots)
    pair_bit = 2 if slots == 2 else 0
    group_bits = [1 << b for b in reversed(range(rows.bit_length() - 1)) if 1 << b != pair_bit]
    first_bit, last_bits = group_bits[0], group_bits[1:]
    offsets = [0, pair_bit] if slots == 2 else [0]
    places = [(di, dc) for di in offsets for dc in range(cols)]
    mine_at = (i // 2) % 2 if slots == 2 else 0
    gates = GATES if rows == 8 and slots == 2 else {}
    made, steps = {}, {}

    def get(name):
        if name not in made:
            made[name] = None
            made[name] = steps[name]()
        return made[name]

    def gated(array, name):
        waits = [get(other) for other in gates.get(name, ())]
        return after(array, *waits) if waits else array

    def send(name, array, di=0, dc=0):
        def where(si, ii, ci):
            return si, ii ^ di, (ci + dc) % cols

        return send_to(gated(array, name), where)

    def swap(name, array):
        return send_to(gated(array, name), lambda si, ii, ci: (1 - si, ii, ci))

    def step(name):
        def note(make):
            steps[name] = make
            return make

        return note

    wide = slots * bw
    qkv = qkv_weight[0].transpose(1, 0, 2)
    stale = (stale_keys[0, 0], stale_values[0, 0])

    def columns(array, start, width):
        return lax.dynamic_slice_in_dim(array, start, width, array.ndim - 1)

    def cut(kind, start, width):
        if kind == "O":
            return lax.dynamic_slice_in_dim(out_weight[0], start, width, 0)
        if kind == "S":
            return jnp.concatenate([columns(one, start, width) for one in stale])
        return columns(qkv["QKV".index(kind)], start, width)

    def block_of(kind, layer, slot):
        at = (mine_at if slot == 0 else 1 - mine_at) * bw
        got = get("a" + kind)
        other = lax.dynamic_slice_in_dim(got, at, bw, 0) if kind == "O" else columns(got, at, bw)
        block = jnp.where(s == layer, cut(kind, s * wide + at, bw), other)
        return block.reshape(2, slot_len, bw) if kind == "S" else block

    for kind in "QKVOS":
        step("a" + kind)(
            lambda kind=kind: swap("a" + kind, cut(kind, (1 - s) * wide, wide))
        )

    def move(kind, layer, d):
        name = f"{kind}{layer}.{d}"
        for bit in reversed(last_bits):
            if d & bit:
                return send(name, get(f"{kind}{layer}.{d ^ bit}"), bit)
        block = block_of(kind, layer, 1 if d & pair_bit else 0)
        return send(name, block, d) if d else gated(block, name)

    for layer in range(2):
        for kind in "QKVO":
            for d in range(rows):
                step(f"{kind}{layer}.{d}")(functools.partial(move, kind, layer, d))
        for d in offsets:
            step(f"S{layer}.{d}")(functools.partial(move, "S", layer, d))

    def of_rows(kind, layer):
        return [get(f"{kind}{layer}.{d}") for d in range(rows)]

    def stale_of(layer):
        return [get(f"S{layer}.{d}") for d in offsets]

    @step("n")
    def _():
        numbers = jnp.concatenate([patch_ends[0], timestep])
        return jnp.stack([numbers] + [send("n", numbers, di) for di in offsets[1:]])

    @step("m")
    def _():
        feats = jnp.pad(embed_time(get("n")[:, NP]), ((0, 8 - slots), (0, 0)))
        own = pl.pallas_call(
            functools.partial(mod_kernel, slots),
            out_shape=jax.ShapeDtypeStruct((slots, 3, feat), jnp.float32),
            in_specs=[vmem_spec(), vmem_spec()],
            out_specs=vmem_spec(),
            compiler_params=pltpu.CompilerParams(vmem_limit_bytes=VMEM_LIMIT),
            name="modulation",
        )(gated(feats, "m"), mod_weight[0].transpose(1, 0, 2))
        other = swap("mc", own)
        return [jnp.where(s == layer, own, other) for layer in range(2)]

    x_half = lax.dynamic_slice_in_dim(hidden_in[0], s * half, half, 0)
    step("x.0.0")(lambda: gated(x_half, "x.0.0"))
    step("g.0.0")(lambda: finish(0, x_half))
    for kind in "xg":
        for di, dc in places:
            name = f"{kind}.{di}.{dc}"

            def bring(kind=kind, name=name, di=di, dc=dc):
                if dc and kind in TREE:
                    return send(name, get(f"{kind}.{di}.0"), 0, dc)
                return send(name, get(f"{kind}.0.0"), di, dc)

            if (di, dc) != (0, 0):
                step(name)(bring)
            step(name + "c")(lambda name=name: swap(name + "c", get(name)))
    x_rest = lax.dynamic_slice_in_dim(hidden_in[0], (1 - s) * half, half, 0)
    step("x.0.0c")(lambda: x_rest)

    def x_pieces(kind):
        return [get(f"{kind}.{di}.{dc}" + end) for di, dc in places for end in ("", "c")]

    def modulated(layer):
        pieces = x_pieces("xg"[layer])
        shape = (slots * slot_len, feat)
        return pl.pallas_call(
            functools.partial(modulate_kernel, (slots, slot_len, cols), wc),
            out_shape=jax.ShapeDtypeStruct(shape, jnp.bfloat16),
            in_specs=[vmem_spec()] + [any_spec()] * len(pieces),
            out_specs=vmem_spec(),
            scratch_shapes=[
                pltpu.VMEM((cols, slots * slot_len, wc), jnp.bfloat16),
                pltpu.SemaphoreType.DMA((len(pieces),)),
            ],
            compiler_params=pltpu.CompilerParams(vmem_limit_bytes=VMEM_LIMIT),
            name="modulate",
        )(gated(get("m")[layer], f"l{layer}"), *pieces)

    def scores(layer):
        return pl.pallas_call(
            functools.partial(scores_kernel, (slots, slot_len, rows, kr, bw)),
            out_shape=jax.ShapeDtypeStruct(
                (slots, bw // HD, slot_len, 2 * slot_len), jnp.bfloat16
            ),
            in_specs=[pl.BlockSpec(memory_space=pltpu.SMEM)]
            + [any_spec()] * (1 + 2 * rows + slots),
            out_specs=vmem_spec(),
            scratch_shapes=[
                pltpu.VMEM((slots * slot_len, feat), jnp.bfloat16),
                pltpu.VMEM((2, feat, bw), jnp.bfloat16),
                pltpu.VMEM((slots, 2 * slot_len, bw), jnp.bfloat16),
                pltpu.SemaphoreType.DMA((1,)),
                pltpu.SemaphoreType.DMA((2 * rows,)),
                pltpu.SemaphoreType.DMA((slots,)),
            ],
            compiler_params=pltpu.CompilerParams(vmem_limit_bytes=VMEM_LIMIT),
            name="scores",
        )(
            gated(get("n")[:, :NP], f"k{layer}"),
            get(f"l{layer}"),
            *of_rows("Q", layer),
            *of_rows("K", layer),
            *stale_of(layer),
        )

    def mix(layer):
        plan = (slots, slot_len, cols, rows, kr, nr, bw, wc)
        shape = jax.ShapeDtypeStruct((slots, half, feat), jnp.bfloat16)
        return pl.pallas_call(
            functools.partial(mix_kernel, plan),
            out_shape=(shape, shape),
            in_specs=[any_spec()] * (2 + 2 * rows + slots),
            out_specs=(vmem_spec(), vmem_spec()),
            scratch_shapes=[
                pltpu.VMEM((slots * slot_len, feat), jnp.bfloat16),
                pltpu.VMEM((slots, bw // HD, slot_len, 2 * slot_len), jnp.bfloat16),
                pltpu.VMEM((feat, bw), jnp.bfloat16),
                pltpu.VMEM((rows, bw, nr), jnp.bfloat16),
                pltpu.VMEM((slots, 2 * slot_len, bw), jnp.bfloat16),
                pltpu.VMEM((slots * slot_len, bw), jnp.bfloat16),
                pltpu.SemaphoreType.DMA((2,)),
                pltpu.SemaphoreType.DMA((2 * rows,)),
                pltpu.SemaphoreType.DMA((slots,)),
            ],
            compiler_params=pltpu.CompilerParams(vmem_limit_bytes=VMEM_LIMIT),
            name="mix",
        )(
            get(f"l{layer}"),
            gated(get(f"k{layer}"), f"v{layer}"),
            *of_rows("V", layer),
            *of_rows("O", layer),
            *stale_of(layer),
        )

    def parts(layer):
        keep, other = get(f"v{layer}")[0], get(f"p{layer}")

        def part(array, di, dc):
            return array[offsets.index(di), :, dc * wc : (dc + 1) * wc].astype(jnp.float32)

        return {place: part(keep, *place) + part(other, *place) for place in places}

    def summed(layer, di):
        part = get(f"t{layer}")[di, 0]
        for dc in range(1, cols):
            part = part + get(f"r{layer}.{di}.{dc}").astype(jnp.float32)
        return part

    def give(layer, di, dc):
        name = f"r{layer}.{di}.{dc}"
        if f"r{layer}" not in TREE:
            return send(name, get(f"t{layer}")[di, dc].astype(jnp.bfloat16), di, dc)
        if dc:
            return send(name, get(f"t{layer}")[di, dc].astype(jnp.bfloat16), 0, dc)
        return send(name, get(f"u{layer}.{di}").astype(jnp.bfloat16), di, 0)

    for layer in range(2):
        step(f"l{layer}")(functools.partial(modulated, layer))
        step(f"k{layer}")(functools.partial(scores, layer))
        step(f"v{layer}")(functools.partial(mix, layer))
        step(f"p{layer}")(lambda layer=layer: swap(f"p{layer}", get(f"v{layer}")[1]))
        step(f"t{layer}")(functools.partial(parts, layer))
        for di, dc in places:
            if (di, dc) != (0, 0):
                step(f"r{layer}.{di}.{dc}")(functools.partial(give, layer, di, dc))
        for di in offsets:
            step(f"u{layer}.{di}")(functools.partial(summed, layer, di))

    def finish(layer, x_own):
        if f"r{layer}" in TREE:
            branch = get(f"u{layer}.0")
            for di in offsets[1:]:
                branch = branch + get(f"r{layer}.{di}.0").astype(jnp.float32)
        else:
            branch = get(f"t{layer}")[0, 0]
            for di, dc in places[1:]:
                branch = branch + get(f"r{layer}.{di}.{dc}").astype(jnp.float32)
        gate_own = columns(get("m")[layer][0, 2], c * wc, wc)
        updated = x_own.astype(jnp.float32) + gate_own[None, :] * branch
        positions = jnp.arange(half)[:, None] + s * half
        return jnp.where(positions < patch_ends[0, NP - 1], updated, 0.0).astype(jnp.bfloat16)

    first = get("g.0.0")
    second = finish(1, first)
    low = jnp.where(s == 0, first, swap("e", second))
    high = jnp.where(s == 0, get("g.0.0c"), second)
    return jnp.concatenate([low, high], axis=0)[None, None]


def solution(mesh):
    return jax.shard_map(
        shards,
        mesh=mesh,
        in_specs=(
            P("row", None, "col"),
            P("row", None),
            P("row"),
            P("section", None, None, None),
            P("section", "row", None, "col"),
            P("section", "col", "row"),
            P("section", "row", None, "col"),
            P("section", "row", None, "col"),
        ),
        out_specs=P("section", "row", None, "col"),
        check_vma=False,
    )
```

```python
import functools
import math

import jax
import jax.numpy as jnp
from jax import lax
from jax.experimental import pallas as pl
from jax.experimental.pallas import tpu as pltpu
from jax.sharding import PartitionSpec as P

HD = 128
FREQ = 256
NP = 4
AXES = ("section", "row", "col")
VMEM_LIMIT = 56 * 1024 * 1024


def send_to(array, where):
    ns, nr, nc = (lax.axis_size(axis) for axis in AXES)
    pairs = []
    for s in range(ns):
        for i in range(nr):
            for c in range(nc):
                ts, ti, tc = where(s, i, c)
                pairs.append(((s * nr + i) * nc + c, (ts * nr + ti) * nc + tc))
    return lax.ppermute(array, AXES, pairs)


def to_core(array):
    return send_to(array, lambda s, i, c: (1 - s, i, c))


def after(array, *others):
    return lax.optimization_barrier((array,) + others)[0]


def pick(array, index):
    return lax.dynamic_index_in_dim(array, index, 0, keepdims=False)


def embed_time(timestep):
    half_width = FREQ // 2
    frequency = jnp.exp(
        jnp.arange(half_width, dtype=jnp.float32) * (-math.log(10000.0) / half_width)
    )
    angles = timestep.astype(jnp.float32)[:, None] * frequency[None, :]
    return jnp.concatenate([jnp.cos(angles), jnp.sin(angles)], axis=1).astype(jnp.bfloat16)


def any_spec():
    return pl.BlockSpec(memory_space=pl.ANY)


def vmem_spec():
    return pl.BlockSpec(memory_space=pltpu.VMEM)


def load_rows(pieces, target, sem, first, rows_each):
    i = lax.axis_index("row")
    copies = []
    for d, piece in enumerate(pieces):
        if rows_each is None:
            place = target.at[i ^ d]
        else:
            place = target.at[pl.ds(pl.multiple_of((i ^ d) * rows_each, 32), rows_each), :]
        copies.append(pltpu.make_async_copy(piece, place, sem.at[first + d]))
        copies[-1].start()
    return copies


def fresh_and_valid(ends_ref, slot, slot_len):
    key_at = lax.broadcasted_iota(jnp.int32, (slot_len, slot_len), 1)
    query_at = lax.broadcasted_iota(jnp.int32, (slot_len, slot_len), 0)
    limit = jnp.full((slot_len, slot_len), ends_ref[slot, NP - 1], jnp.int32)
    for m in range(NP - 2, -1, -1):
        limit = jnp.where(query_at < ends_ref[slot, m], ends_ref[slot, m], limit)
    return key_at < limit, key_at < ends_ref[slot, NP - 1]


def load_x(plan, x_refs, xv, sem):
    slots, slot_len, cols = plan
    s, c = lax.axis_index("section"), lax.axis_index("col")
    half = slot_len // 2
    copies = []
    for slot in range(slots):
        for dc in range(cols):
            for h in range(2):
                place = len(copies)
                col = lax.rem(c + cols - dc, cols)
                row = pl.multiple_of(slot * slot_len + jnp.where(s == h, 0, half), half)
                copies.append(
                    pltpu.make_async_copy(
                        x_refs[place], xv.at[col, pl.ds(row, half), :], sem.at[place]
                    )
                )
                copies[-1].start()
    return copies


def modulate(plan, wc, mod_ref, xv, xm):
    slots, slot_len, cols = plan
    feat, tile = cols * wc, 16
    for slot in range(slots):

        def some_rows(step, carry, slot=slot):
            rows = pl.ds(pl.multiple_of(slot * slot_len + step * tile, tile), tile)
            parts = [xv[col, rows, :].astype(jnp.float32) for col in range(cols)]
            total = sum(jnp.sum(part, axis=-1, keepdims=True) for part in parts)
            squares = sum(jnp.sum(part * part, axis=-1, keepdims=True) for part in parts)
            mean = total / feat
            var = squares / feat - mean * mean
            inverse = lax.rsqrt(var + 1e-06)
            for col in range(cols):
                span = pl.ds(col * wc, wc)
                part = xv[col, rows, :].astype(jnp.float32)
                shift = mod_ref[slot, 0:1, span]
                scale = mod_ref[slot, 1:2, span]
                part = (part - mean) * inverse * (1.0 + scale) + shift
                xm[rows, span] = part.astype(jnp.bfloat16)
            return carry

        lax.fori_loop(0, slot_len // tile, some_rows, 0, unroll=2)


def modulate_kernel(plan, wc, mod_ref, *refs):
    n_x = len(refs) - 3
    x_refs, (xm, xv, sem) = refs[:n_x], refs[n_x:]
    for copy in load_x(plan, x_refs, xv, sem):
        copy.wait()
    modulate(plan, wc, mod_ref, xv, xm)


def scores_kernel(plan, ends_ref, *refs):
    slots, slot_len, n_w, kr, bw = plan
    x_ref, refs = refs[0], refs[1:]
    w_refs, refs = (refs[:n_w], refs[n_w : 2 * n_w]), refs[2 * n_w :]
    kv_refs, refs = refs[:slots], refs[slots:]
    weights_ref, xm, wv, raw_ref, kvv, x_sem, w_sem, kv_sem = refs
    x_copies = [pltpu.make_async_copy(x_ref, xm, x_sem.at[0])]
    x_copies[0].start()
    copies = load_rows(w_refs[0], wv.at[0], w_sem, 0, kr)
    copies += load_rows(w_refs[1], wv.at[1], w_sem, n_w, kr)
    for slot in range(slots):
        one = kv_refs[slot].at[0]
        target = kvv.at[slot, pl.ds(slot_len, slot_len), :]
        copies.append(pltpu.make_async_copy(one, target, kv_sem.at[slot]))
        copies[-1].start()
    for copy in x_copies + copies:
        copy.wait()
    contract = (((1,), (1,)), ((), ()))

    def normed(block):
        mean = jnp.mean(block * block, axis=-1, keepdims=True)
        return (block * lax.rsqrt(mean + 1e-06)).astype(jnp.bfloat16)

    for t in range(2):
        raw_ref[t] = jnp.dot(xm[...], wv[t], preferred_element_type=jnp.float32)
    for slot in range(slots):
        rows = pl.ds(slot * slot_len, slot_len)
        fresh, valid = fresh_and_valid(ends_ref, slot, slot_len)
        for head in range(bw // HD):
            lanes = slice(head * HD, (head + 1) * HD)
            query = normed(raw_ref[0, rows, lanes])
            kvv[slot, 0:slot_len, lanes] = normed(raw_ref[1, rows, lanes])
            both = lax.dot_general(
                query, kvv[slot, :, lanes], contract, preferred_element_type=jnp.float32
            )
            scores = jnp.where(fresh, both[:, :slot_len], both[:, slot_len:])
            weights = jnp.where(valid, jnp.exp(scores * (1.0 / math.sqrt(HD))), 0.0)
            weights = weights * (1.0 / jnp.sum(weights, axis=-1, keepdims=True))
            weights_ref[slot, head, :, 0:slot_len] = jnp.where(fresh, weights, 0.0).astype(
                jnp.bfloat16
            )
            weights_ref[slot, head, :, slot_len:] = jnp.where(fresh, 0.0, weights).astype(
                jnp.bfloat16
            )


def mix_kernel(plan, x_ref, weights_ref, *refs):
    slots, slot_len, cols, n_w, kr, nr, bw, wc = plan
    v_refs, o_refs, refs = refs[:n_w], refs[n_w : 2 * n_w], refs[2 * n_w :]
    kv_refs, refs = refs[:slots], refs[slots:]
    keep_ref, pass_ref, xm, pv, wv, ov, kvv, att, x_sem, w_sem, kv_sem = refs
    s, c = lax.axis_index("section"), lax.axis_index("col")
    half = slot_len // 2
    x_copy = pltpu.make_async_copy(x_ref, xm, x_sem.at[0])
    x_copy.start()
    copies = load_rows(v_refs, wv, w_sem, 0, kr)
    p_copy = pltpu.make_async_copy(weights_ref, pv, x_sem.at[1])
    p_copy.start()
    late = [p_copy]
    for slot in range(slots):
        one = kv_refs[slot].at[1]
        target = kvv.at[slot, pl.ds(slot_len, slot_len), :]
        late.append(pltpu.make_async_copy(one, target, kv_sem.at[slot]))
        late[-1].start()
    o_copies = load_rows(o_refs, ov, w_sem, n_w, None)
    for copy in [x_copy] + copies:
        copy.wait()
    raw = jnp.dot(xm[...], wv[...], preferred_element_type=jnp.float32).astype(jnp.bfloat16)
    for slot in range(slots):
        kvv[slot, 0:slot_len, :] = raw[slot * slot_len : (slot + 1) * slot_len]
    for copy in late:
        copy.wait()
    for slot in range(slots):
        rows = pl.ds(slot * slot_len, slot_len)
        for head in range(bw // HD):
            lanes = slice(head * HD, (head + 1) * HD)
            mixed = jnp.dot(pv[slot, head], kvv[slot, :, lanes], preferred_element_type=jnp.float32)
            att[rows, lanes] = mixed.astype(jnp.bfloat16)
    for copy in o_copies:
        copy.wait()
    blocks = []
    for side in (1 - s, s):
        for slot in range(slots):
            row = pl.multiple_of(slot * slot_len + side * half, half)
            blocks.append(att[pl.ds(row, half), :])
    lhs = jnp.concatenate(blocks, axis=0)
    for place in range(n_w):
        row = lax.rem(c * (n_w // cols) + place, n_w)
        part = jnp.dot(lhs, ov[row], preferred_element_type=jnp.float32).astype(jnp.bfloat16)
        lanes = slice(place * nr, (place + 1) * nr)
        for k, out_ref in enumerate((pass_ref, keep_ref)):
            for slot in range(slots):
                first = (k * slots + slot) * half
                out_ref[slot, :, lanes] = part[first : first + half]


def mod_kernel(slots, feats_ref, weight_ref, out_ref):
    for k in range(3):
        part = jnp.dot(feats_ref[...], weight_ref[k], preferred_element_type=jnp.float32)
        for slot in range(slots):
            out_ref[slot, k : k + 1, :] = part[slot : slot + 1, :]


GATES = {
    "K0.4": ("Q0.4",),
    "K0.6": ("Q0.6",),
    "V0.4": ("K0.4",),
    "V0.6": ("K0.6",),
    "O0.4": ("V0.4",),
    "O0.6": ("V0.6",),
    "Q1.4": ("O0.4", "Q0.3",),
    "Q1.6": ("O0.6",),
    "K1.4": ("Q1.4",),
    "K1.6": ("Q1.6",),
    "V1.4": ("K1.4",),
    "V1.6": ("K1.6",),
    "O1.4": ("V1.4",),
    "O1.6": ("V1.6",),
    "O0.2": ("Q0.2",),
    "Q1.2": ("S0.2",),
    "K1.2": ("K0.2",),
    "V1.2": ("V0.2",),
    "O1.2": ("O0.2", "O0.5",),
    "S1.2": ("Q1.2",),
    "K0.1": ("Q0.1",),
    "K0.3": ("Q0.3",),
    "Q0.5": ("K0.1",),
    "Q0.7": ("K0.3",),
    "V0.1": ("Q0.5",),
    "V0.3": ("Q0.7",),
    "K0.5": ("V0.1",),
    "K0.7": ("V0.3",),
    "O0.1": ("K0.5",),
    "O0.3": ("K0.7",),
    "V0.5": ("O0.1",),
    "V0.7": ("O0.3",),
    "Q1.1": ("V0.5",),
    "Q1.3": ("V0.7",),
    "O0.5": ("Q1.1",),
    "O0.7": ("Q1.3",),
    "K1.1": ("O0.5",),
    "K1.3": ("O0.7",),
    "Q1.5": ("K1.1",),
    "Q1.7": ("K1.3",),
    "V1.1": ("Q1.5",),
    "V1.3": ("Q1.7",),
    "K1.5": ("V1.1",),
    "K1.7": ("V1.3",),
    "O1.1": ("K1.5",),
    "O1.3": ("K1.7",),
    "V1.5": ("O1.1",),
    "V1.7": ("O1.3",),
    "O1.5": ("V1.5",),
    "O1.7": ("V1.7",),
    "n": ("aQ",),
    "x.0.0": ("Q0.4",),
    "m": ("Q0.6",),
    "p0": ("Q1.4", "Q1.6",),
    "r0.0.1": ("K1.4",),
    "g.2.0": ("K1.6",),
    "O1.0": ("V1.3",),
    "x.0.0c": ("aV",),
}
TREE = ("x", "r0", "g", )


def shards(
    hidden_in, patch_ends, timestep, mod_weight, qkv_weight, out_weight, stale_keys, stale_values
):
    s, i, c = (lax.axis_index(axis) for axis in AXES)
    sections, rows, cols = (lax.axis_size(axis) for axis in AXES)
    _, slot_len, wc = hidden_in.shape
    feat = mod_weight.shape[-1]
    kr, nr = qkv_weight.shape[1], out_weight.shape[2]
    half = slot_len // 2
    slots = 2 if (wc // HD) % (2 * sections) == 0 else 1
    bw = wc // (sections * slots)
    pair_bit = 2 if slots == 2 else 0
    group_bits = [1 << b for b in reversed(range(rows.bit_length() - 1)) if 1 << b != pair_bit]
    first_bit, last_bits = group_bits[0], group_bits[1:]
    offsets = [0, pair_bit] if slots == 2 else [0]
    places = [(di, dc) for di in offsets for dc in range(cols)]
    mine_at = (i // 2) % 2 if slots == 2 else 0
    gates = GATES if rows == 8 and slots == 2 else {}
    made, steps = {}, {}

    def get(name):
        if name not in made:
            made[name] = None
            made[name] = steps[name]()
        return made[name]

    def gated(array, name):
        waits = [get(other) for other in gates.get(name, ())]
        return after(array, *waits) if waits else array

    def send(name, array, di=0, dc=0):
        def where(si, ii, ci):
            return si, ii ^ di, (ci + dc) % cols

        return send_to(gated(array, name), where)

    def swap(name, array):
        return send_to(gated(array, name), lambda si, ii, ci: (1 - si, ii, ci))

    def step(name):
        def note(make):
            steps[name] = make
            return make

        return note

    wide = slots * bw
    qkv = qkv_weight[0].transpose(1, 0, 2)
    stale = (stale_keys[0, 0], stale_values[0, 0])

    def columns(array, start, width):
        return lax.dynamic_slice_in_dim(array, start, width, array.ndim - 1)

    def cut(kind, start, width):
        if kind == "O":
            return lax.dynamic_slice_in_dim(out_weight[0], start, width, 0)
        if kind == "S":
            return jnp.concatenate([columns(one, start, width) for one in stale])
        return columns(qkv["QKV".index(kind)], start, width)

    def block_of(kind, layer, slot):
        at = (mine_at if slot == 0 else 1 - mine_at) * bw
        got = get("a" + kind)
        other = lax.dynamic_slice_in_dim(got, at, bw, 0) if kind == "O" else columns(got, at, bw)
        block = jnp.where(s == layer, cut(kind, s * wide + at, bw), other)
        return block.reshape(2, slot_len, bw) if kind == "S" else block

    for kind in "QKVOS":
        step("a" + kind)(
            lambda kind=kind: swap("a" + kind, cut(kind, (1 - s) * wide, wide))
        )

    def move(kind, layer, d):
        name = f"{kind}{layer}.{d}"
        for bit in reversed(last_bits):
            if d & bit:
                return send(name, get(f"{kind}{layer}.{d ^ bit}"), bit)
        block = block_of(kind, layer, 1 if d & pair_bit else 0)
        return send(name, block, d) if d else gated(block, name)

    for layer in range(2):
        for kind in "QKVO":
            for d in range(rows):
                step(f"{kind}{layer}.{d}")(functools.partial(move, kind, layer, d))
        for d in offsets:
            step(f"S{layer}.{d}")(functools.partial(move, "S", layer, d))

    def of_rows(kind, layer):
        return [get(f"{kind}{layer}.{d}") for d in range(rows)]

    def stale_of(layer):
        return [get(f"S{layer}.{d}") for d in offsets]

    @step("n")
    def _():
        numbers = jnp.concatenate([patch_ends[0], timestep])
        return jnp.stack([numbers] + [send("n", numbers, di) for di in offsets[1:]])

    @step("m")
    def _():
        feats = jnp.pad(embed_time(get("n")[:, NP]), ((0, 8 - slots), (0, 0)))
        own = pl.pallas_call(
            functools.partial(mod_kernel, slots),
            out_shape=jax.ShapeDtypeStruct((slots, 3, feat), jnp.float32),
            in_specs=[vmem_spec(), vmem_spec()],
            out_specs=vmem_spec(),
            compiler_params=pltpu.CompilerParams(vmem_limit_bytes=VMEM_LIMIT),
            name="modulation",
        )(gated(feats, "m"), mod_weight[0].transpose(1, 0, 2))
        other = swap("mc", own)
        return [jnp.where(s == layer, own, other) for layer in range(2)]

    x_half = lax.dynamic_slice_in_dim(hidden_in[0], s * half, half, 0)
    step("x.0.0")(lambda: gated(x_half, "x.0.0"))
    step("g.0.0")(lambda: finish(0, x_half))
    for kind in "xg":
        for di, dc in places:
            name = f"{kind}.{di}.{dc}"

            def bring(kind=kind, name=name, di=di, dc=dc):
                if dc and kind in TREE:
                    return send(name, get(f"{kind}.{di}.0"), 0, dc)
                return send(name, get(f"{kind}.0.0"), di, dc)

            if (di, dc) != (0, 0):
                step(name)(bring)
            step(name + "c")(lambda name=name: swap(name + "c", get(name)))
    x_rest = lax.dynamic_slice_in_dim(hidden_in[0], (1 - s) * half, half, 0)
    step("x.0.0c")(lambda: x_rest)

    def x_pieces(kind):
        return [get(f"{kind}.{di}.{dc}" + end) for di, dc in places for end in ("", "c")]

    def modulated(layer):
        pieces = x_pieces("xg"[layer])
        shape = (slots * slot_len, feat)
        return pl.pallas_call(
            functools.partial(modulate_kernel, (slots, slot_len, cols), wc),
            out_shape=jax.ShapeDtypeStruct(shape, jnp.bfloat16),
            in_specs=[vmem_spec()] + [any_spec()] * len(pieces),
            out_specs=vmem_spec(),
            scratch_shapes=[
                pltpu.VMEM((cols, slots * slot_len, wc), jnp.bfloat16),
                pltpu.SemaphoreType.DMA((len(pieces),)),
            ],
            compiler_params=pltpu.CompilerParams(vmem_limit_bytes=VMEM_LIMIT),
            name="modulate",
        )(gated(get("m")[layer], f"l{layer}"), *pieces)

    def scores(layer):
        return pl.pallas_call(
            functools.partial(scores_kernel, (slots, slot_len, rows, kr, bw)),
            out_shape=jax.ShapeDtypeStruct(
                (slots, bw // HD, slot_len, 2 * slot_len), jnp.bfloat16
            ),
            in_specs=[pl.BlockSpec(memory_space=pltpu.SMEM)]
            + [any_spec()] * (1 + 2 * rows + slots),
            out_specs=vmem_spec(),
            scratch_shapes=[
                pltpu.VMEM((slots * slot_len, feat), jnp.bfloat16),
                pltpu.VMEM((2, feat, bw), jnp.bfloat16),
                pltpu.VMEM((2, slots * slot_len, bw), jnp.float32),
                pltpu.VMEM((slots, 2 * slot_len, bw), jnp.bfloat16),
                pltpu.SemaphoreType.DMA((1,)),
                pltpu.SemaphoreType.DMA((2 * rows,)),
                pltpu.SemaphoreType.DMA((slots,)),
            ],
            compiler_params=pltpu.CompilerParams(vmem_limit_bytes=VMEM_LIMIT),
            name="scores",
        )(
            gated(get("n")[:, :NP], f"k{layer}"),
            get(f"l{layer}"),
            *of_rows("Q", layer),
            *of_rows("K", layer),
            *stale_of(layer),
        )

    def mix(layer):
        plan = (slots, slot_len, cols, rows, kr, nr, bw, wc)
        shape = jax.ShapeDtypeStruct((slots, half, feat), jnp.bfloat16)
        return pl.pallas_call(
            functools.partial(mix_kernel, plan),
            out_shape=(shape, shape),
            in_specs=[any_spec()] * (2 + 2 * rows + slots),
            out_specs=(vmem_spec(), vmem_spec()),
            scratch_shapes=[
                pltpu.VMEM((slots * slot_len, feat), jnp.bfloat16),
                pltpu.VMEM((slots, bw // HD, slot_len, 2 * slot_len), jnp.bfloat16),
                pltpu.VMEM((feat, bw), jnp.bfloat16),
                pltpu.VMEM((rows, bw, nr), jnp.bfloat16),
                pltpu.VMEM((slots, 2 * slot_len, bw), jnp.bfloat16),
                pltpu.VMEM((slots * slot_len, bw), jnp.bfloat16),
                pltpu.SemaphoreType.DMA((2,)),
                pltpu.SemaphoreType.DMA((2 * rows,)),
                pltpu.SemaphoreType.DMA((slots,)),
            ],
            compiler_params=pltpu.CompilerParams(vmem_limit_bytes=VMEM_LIMIT),
            name="mix",
        )(
            get(f"l{layer}"),
            gated(get(f"k{layer}"), f"v{layer}"),
            *of_rows("V", layer),
            *of_rows("O", layer),
            *stale_of(layer),
        )

    def parts(layer):
        keep, other = get(f"v{layer}")[0], get(f"p{layer}")

        def part(array, di, dc):
            return array[offsets.index(di), :, dc * wc : (dc + 1) * wc].astype(jnp.float32)

        return {place: part(keep, *place) + part(other, *place) for place in places}

    def summed(layer, di):
        part = get(f"t{layer}")[di, 0]
        for dc in range(1, cols):
            part = part + get(f"r{layer}.{di}.{dc}").astype(jnp.float32)
        return part

    def give(layer, di, dc):
        name = f"r{layer}.{di}.{dc}"
        if f"r{layer}" not in TREE:
            return send(name, get(f"t{layer}")[di, dc].astype(jnp.bfloat16), di, dc)
        if dc:
            return send(name, get(f"t{layer}")[di, dc].astype(jnp.bfloat16), 0, dc)
        return send(name, get(f"u{layer}.{di}").astype(jnp.bfloat16), di, 0)

    for layer in range(2):
        step(f"l{layer}")(functools.partial(modulated, layer))
        step(f"k{layer}")(functools.partial(scores, layer))
        step(f"v{layer}")(functools.partial(mix, layer))
        step(f"p{layer}")(lambda layer=layer: swap(f"p{layer}", get(f"v{layer}")[1]))
        step(f"t{layer}")(functools.partial(parts, layer))
        for di, dc in places:
            if (di, dc) != (0, 0):
                step(f"r{layer}.{di}.{dc}")(functools.partial(give, layer, di, dc))
        for di in offsets:
            step(f"u{layer}.{di}")(functools.partial(summed, layer, di))

    def finish(layer, x_own):
        if f"r{layer}" in TREE:
            branch = get(f"u{layer}.0")
            for di in offsets[1:]:
                branch = branch + get(f"r{layer}.{di}.0").astype(jnp.float32)
        else:
            branch = get(f"t{layer}")[0, 0]
            for di, dc in places[1:]:
                branch = branch + get(f"r{layer}.{di}.{dc}").astype(jnp.float32)
        gate_own = columns(get("m")[layer][0, 2], c * wc, wc)
        updated = x_own.astype(jnp.float32) + gate_own[None, :] * branch
        positions = jnp.arange(half)[:, None] + s * half
        return jnp.where(positions < patch_ends[0, NP - 1], updated, 0.0).astype(jnp.bfloat16)

    first = get("g.0.0")
    second = finish(1, first)
    low = jnp.where(s == 0, first, swap("e", second))
    high = jnp.where(s == 0, get("g.0.0c"), second)
    return jnp.concatenate([low, high], axis=0)[None, None]


def solution(mesh):
    return jax.shard_map(
        shards,
        mesh=mesh,
        in_specs=(
            P("row", None, "col"),
            P("row", None),
            P("row"),
            P("section", None, None, None),
            P("section", "row", None, "col"),
            P("section", "col", "row"),
            P("section", "row", None, "col"),
            P("section", "row", None, "col"),
        ),
        out_specs=P("section", "row", None, "col"),
        check_vma=False,
    )
```

```python
import functools
import math

import jax
import jax.numpy as jnp
from jax import lax
from jax.experimental import pallas as pl
from jax.experimental.pallas import tpu as pltpu
from jax.sharding import PartitionSpec as P

HD = 128
FREQ = 256
NP = 4
AXES = ("section", "row", "col")
VMEM_LIMIT = 56 * 1024 * 1024


def send_to(array, where):
    ns, nr, nc = (lax.axis_size(axis) for axis in AXES)
    pairs = []
    for s in range(ns):
        for i in range(nr):
            for c in range(nc):
                ts, ti, tc = where(s, i, c)
                pairs.append(((s * nr + i) * nc + c, (ts * nr + ti) * nc + tc))
    return lax.ppermute(array, AXES, pairs)


def to_core(array):
    return send_to(array, lambda s, i, c: (1 - s, i, c))


def after(array, *others):
    return lax.optimization_barrier((array,) + others)[0]


def pick(array, index):
    return lax.dynamic_index_in_dim(array, index, 0, keepdims=False)


def embed_time(timestep):
    half_width = FREQ // 2
    frequency = jnp.exp(
        jnp.arange(half_width, dtype=jnp.float32) * (-math.log(10000.0) / half_width)
    )
    angles = timestep.astype(jnp.float32)[:, None] * frequency[None, :]
    return jnp.concatenate([jnp.cos(angles), jnp.sin(angles)], axis=1).astype(jnp.bfloat16)


def any_spec():
    return pl.BlockSpec(memory_space=pl.ANY)


def vmem_spec():
    return pl.BlockSpec(memory_space=pltpu.VMEM)


def load_rows(pieces, target, sem, first, rows_each):
    i = lax.axis_index("row")
    copies = []
    for d, piece in enumerate(pieces):
        if rows_each is None:
            place = target.at[i ^ d]
        else:
            place = target.at[pl.ds(pl.multiple_of((i ^ d) * rows_each, 32), rows_each), :]
        copies.append(pltpu.make_async_copy(piece, place, sem.at[first + d]))
        copies[-1].start()
    return copies


def fresh_and_valid(ends_ref, slot, slot_len):
    key_at = lax.broadcasted_iota(jnp.int32, (slot_len, slot_len), 1)
    query_at = lax.broadcasted_iota(jnp.int32, (slot_len, slot_len), 0)
    limit = jnp.full((slot_len, slot_len), ends_ref[slot, NP - 1], jnp.int32)
    for m in range(NP - 2, -1, -1):
        limit = jnp.where(query_at < ends_ref[slot, m], ends_ref[slot, m], limit)
    return key_at < limit, key_at < ends_ref[slot, NP - 1]


def load_x(plan, x_refs, xv, sem):
    slots, slot_len, cols = plan
    s, c = lax.axis_index("section"), lax.axis_index("col")
    half = slot_len // 2
    copies = []
    for slot in range(slots):
        for dc in range(cols):
            for h in range(2):
                place = len(copies)
                col = lax.rem(c + cols - dc, cols)
                row = pl.multiple_of(slot * slot_len + jnp.where(s == h, 0, half), half)
                copies.append(
                    pltpu.make_async_copy(
                        x_refs[place], xv.at[col, pl.ds(row, half), :], sem.at[place]
                    )
                )
                copies[-1].start()
    return copies


def modulate_kernel(plan, wc, mod_ref, *refs):
    n_x = len(refs) - 5
    x_refs, (xm, xv, stats, one_plus, sem) = refs[:n_x], refs[n_x:]
    slots, slot_len, cols = plan
    feat, tile, lane = cols * wc, 16, 128
    copies = load_x(plan, x_refs, xv, sem)
    one_plus[...] = 1.0 + mod_ref[:, 1:2, :]
    for copy in copies:
        copy.wait()

    def add_up(step, carry):
        rows = pl.ds(pl.multiple_of(step * tile, tile), tile)
        total = jnp.zeros((tile, lane), jnp.float32)
        squares = jnp.zeros((tile, lane), jnp.float32)
        for col in range(cols):
            for first in range(0, wc, lane):
                part = xv[col, rows, first : first + lane].astype(jnp.float32)
                total += part
                squares += part * part
        stats[0, rows, :] = total
        stats[1, rows, :] = squares
        return carry

    steps = slots * slot_len // tile
    lax.fori_loop(0, steps, add_up, 0, unroll=4)
    mean = jnp.sum(stats[0], axis=-1, keepdims=True) / feat
    var = jnp.sum(stats[1], axis=-1, keepdims=True) / feat - mean * mean
    shape = (slots * slot_len, lane)
    stats[0] = jnp.broadcast_to(mean, shape)
    stats[1] = jnp.broadcast_to(lax.rsqrt(var + 1e-06), shape)
    for slot in range(slots):

        def write(step, carry, slot=slot):
            rows = pl.ds(pl.multiple_of(slot * slot_len + step * tile, tile), tile)
            mean, inverse = stats[0, rows, :], stats[1, rows, :]
            for col in range(cols):
                for first in range(0, wc, lane):
                    span = slice(col * wc + first, col * wc + first + lane)
                    part = xv[col, rows, first : first + lane].astype(jnp.float32)
                    part = (part - mean) * inverse * one_plus[slot, :, span]
                    xm[rows, span] = (part + mod_ref[slot, 0:1, span]).astype(jnp.bfloat16)
            return carry

        lax.fori_loop(0, slot_len // tile, write, 0, unroll=2)


def scores_kernel(plan, ends_ref, *refs):
    slots, slot_len, n_w, kr, bw = plan
    x_ref, refs = refs[0], refs[1:]
    w_refs, refs = (refs[:n_w], refs[n_w : 2 * n_w]), refs[2 * n_w :]
    kv_refs, refs = refs[:slots], refs[slots:]
    weights_ref, xm, wv, raw_ref, queries, kvv, x_sem, w_sem, kv_sem = refs
    x_copies = [pltpu.make_async_copy(x_ref, xm, x_sem.at[0])]
    x_copies[0].start()
    copies = load_rows(w_refs[0], wv.at[0], w_sem, 0, kr)
    copies += load_rows(w_refs[1], wv.at[1], w_sem, n_w, kr)
    for slot in range(slots):
        one = kv_refs[slot].at[0]
        target = kvv.at[slot, pl.ds(slot_len, slot_len), :]
        copies.append(pltpu.make_async_copy(one, target, kv_sem.at[slot]))
        copies[-1].start()
    for copy in x_copies + copies:
        copy.wait()
    contract = (((1,), (1,)), ((), ()))

    def normed(block):
        mean = jnp.mean(block * block, axis=-1, keepdims=True)
        return (block * lax.rsqrt(mean + 1e-06)).astype(jnp.bfloat16)

    for t in range(2):
        raw_ref[t] = jnp.dot(xm[...], wv[t], preferred_element_type=jnp.float32)
    for head in range(bw // HD):
        lanes = slice(head * HD, (head + 1) * HD)
        queries[:, lanes] = normed(raw_ref[0, :, lanes])
        keys = normed(raw_ref[1, :, lanes])
        for slot in range(slots):
            kvv[slot, 0:slot_len, lanes] = keys[slot * slot_len : (slot + 1) * slot_len]
    for slot in range(slots):
        rows = pl.ds(slot * slot_len, slot_len)
        fresh, valid = fresh_and_valid(ends_ref, slot, slot_len)
        for head in range(bw // HD):
            lanes = slice(head * HD, (head + 1) * HD)
            both = lax.dot_general(
                queries[rows, lanes],
                kvv[slot, :, lanes],
                contract,
                preferred_element_type=jnp.float32,
            )
            scores = jnp.where(fresh, both[:, :slot_len], both[:, slot_len:])
            weights = jnp.where(valid, jnp.exp(scores * (1.0 / math.sqrt(HD))), 0.0)
            weights = weights * (1.0 / jnp.sum(weights, axis=-1, keepdims=True))
            weights_ref[slot, head, :, 0:slot_len] = jnp.where(fresh, weights, 0.0).astype(
                jnp.bfloat16
            )
            weights_ref[slot, head, :, slot_len:] = jnp.where(fresh, 0.0, weights).astype(
                jnp.bfloat16
            )


def mix_kernel(plan, x_ref, weights_ref, *refs):
    slots, slot_len, cols, n_w, kr, nr, bw, wc = plan
    v_refs, o_refs, refs = refs[:n_w], refs[n_w : 2 * n_w], refs[2 * n_w :]
    kv_refs, refs = refs[:slots], refs[slots:]
    keep_ref, pass_ref, xm, pv, wv, ov, kvv, att, x_sem, w_sem, kv_sem = refs
    s, c = lax.axis_index("section"), lax.axis_index("col")
    half = slot_len // 2
    x_copy = pltpu.make_async_copy(x_ref, xm, x_sem.at[0])
    x_copy.start()
    copies = load_rows(v_refs, wv, w_sem, 0, kr)
    p_copy = pltpu.make_async_copy(weights_ref, pv, x_sem.at[1])
    p_copy.start()
    late = [p_copy]
    for slot in range(slots):
        one = kv_refs[slot].at[1]
        target = kvv.at[slot, pl.ds(slot_len, slot_len), :]
        late.append(pltpu.make_async_copy(one, target, kv_sem.at[slot]))
        late[-1].start()
    o_copies = load_rows(o_refs, ov, w_sem, n_w, None)
    for copy in [x_copy] + copies:
        copy.wait()
    raw = jnp.dot(xm[...], wv[...], preferred_element_type=jnp.float32).astype(jnp.bfloat16)
    for slot in range(slots):
        kvv[slot, 0:slot_len, :] = raw[slot * slot_len : (slot + 1) * slot_len]
    for copy in late:
        copy.wait()
    for slot in range(slots):
        rows = pl.ds(slot * slot_len, slot_len)
        for head in range(bw // HD):
            lanes = slice(head * HD, (head + 1) * HD)
            mixed = jnp.dot(pv[slot, head], kvv[slot, :, lanes], preferred_element_type=jnp.float32)
            att[rows, lanes] = mixed.astype(jnp.bfloat16)
    for copy in o_copies:
        copy.wait()
    blocks = []
    for side in (1 - s, s):
        for slot in range(slots):
            row = pl.multiple_of(slot * slot_len + side * half, half)
            blocks.append(att[pl.ds(row, half), :])
    lhs = jnp.concatenate(blocks, axis=0)
    for place in range(n_w):
        row = lax.rem(c * (n_w // cols) + place, n_w)
        part = jnp.dot(lhs, ov[row], preferred_element_type=jnp.float32).astype(jnp.bfloat16)
        lanes = slice(place * nr, (place + 1) * nr)
        for k, out_ref in enumerate((pass_ref, keep_ref)):
            for slot in range(slots):
                first = (k * slots + slot) * half
                out_ref[slot, :, lanes] = part[first : first + half]


def mod_kernel(slots, feats_ref, weight_ref, out_ref):
    for k in range(3):
        part = jnp.dot(feats_ref[...], weight_ref[k], preferred_element_type=jnp.float32)
        for slot in range(slots):
            out_ref[slot, k : k + 1, :] = part[slot : slot + 1, :]


GATES = {
    "K0.4": ("Q0.4",),
    "K0.6": ("Q0.6",),
    "V0.4": ("K0.4",),
    "V0.6": ("K0.6",),
    "O0.4": ("V0.4",),
    "O0.6": ("V0.6",),
    "Q1.4": ("O0.4",),
    "Q1.6": ("O0.6",),
    "K1.4": ("Q1.4",),
    "K1.6": ("Q1.6",),
    "V1.4": ("K1.4",),
    "V1.6": ("K1.6",),
    "O1.4": ("V1.4",),
    "O1.6": ("V1.6",),
    "O0.2": ("Q0.2",),
    "Q1.2": ("S0.2",),
    "K1.2": ("K0.2",),
    "V1.2": ("V0.2",),
    "O1.2": ("O0.2", "O0.5",),
    "S1.2": ("Q1.2",),
    "K0.1": ("Q0.1",),
    "K0.3": ("Q0.3",),
    "Q0.5": ("K0.1",),
    "Q0.7": ("K0.3",),
    "V0.1": ("Q0.5",),
    "V0.3": ("Q0.7",),
    "K0.5": ("V0.1",),
    "K0.7": ("V0.3",),
    "O0.1": ("K0.5",),
    "O0.3": ("K0.7",),
    "V0.5": ("O0.1",),
    "V0.7": ("O0.3",),
    "Q1.1": ("V0.5",),
    "Q1.3": ("V0.7",),
    "O0.5": ("Q1.1",),
    "O0.7": ("Q1.3",),
    "K1.1": ("O0.5",),
    "K1.3": ("O0.7",),
    "Q1.5": ("K1.1",),
    "Q1.7": ("K1.3",),
    "V1.1": ("Q1.5",),
    "V1.3": ("Q1.7",),
    "K1.5": ("V1.1",),
    "K1.7": ("V1.3",),
    "O1.1": ("K1.5",),
    "O1.3": ("K1.7",),
    "V1.5": ("O1.1",),
    "V1.7": ("O1.3",),
    "O1.5": ("V1.5",),
    "O1.7": ("V1.7",),
    "n": ("aQ",),
    "m": ("Q0.6", "aV",),
    "p0": ("Q1.4", "Q1.6",),
    "r0.0.1": ("K1.4",),
    "g.2.0": ("K1.6",),
    "O1.0": ("V1.3",),
    "x.0.0c": ("aV",),
    "v0": ("n",),
    "V0.2": ("Q0.6",),
}
TREE = ("x", "r0", "g", )


def shards(
    hidden_in, patch_ends, timestep, mod_weight, qkv_weight, out_weight, stale_keys, stale_values
):
    s, i, c = (lax.axis_index(axis) for axis in AXES)
    sections, rows, cols = (lax.axis_size(axis) for axis in AXES)
    _, slot_len, wc = hidden_in.shape
    feat = mod_weight.shape[-1]
    kr, nr = qkv_weight.shape[1], out_weight.shape[2]
    half = slot_len // 2
    slots = 2 if (wc // HD) % (2 * sections) == 0 else 1
    bw = wc // (sections * slots)
    pair_bit = 2 if slots == 2 else 0
    group_bits = [1 << b for b in reversed(range(rows.bit_length() - 1)) if 1 << b != pair_bit]
    first_bit, last_bits = group_bits[0], group_bits[1:]
    offsets = [0, pair_bit] if slots == 2 else [0]
    places = [(di, dc) for di in offsets for dc in range(cols)]
    mine_at = (i // 2) % 2 if slots == 2 else 0
    gates = GATES if rows == 8 and slots == 2 else {}
    made, steps = {}, {}

    def get(name):
        if name not in made:
            made[name] = None
            made[name] = steps[name]()
        return made[name]

    def gated(array, name):
        waits = [get(other) for other in gates.get(name, ())]
        return after(array, *waits) if waits else array

    def send(name, array, di=0, dc=0):
        def where(si, ii, ci):
            return si, ii ^ di, (ci + dc) % cols

        return send_to(gated(array, name), where)

    def swap(name, array):
        return send_to(gated(array, name), lambda si, ii, ci: (1 - si, ii, ci))

    def step(name):
        def note(make):
            steps[name] = make
            return make

        return note

    wide = slots * bw
    qkv = qkv_weight[0].transpose(1, 0, 2)
    stale = (stale_keys[0, 0], stale_values[0, 0])

    def columns(array, start, width):
        return lax.dynamic_slice_in_dim(array, start, width, array.ndim - 1)

    def cut(kind, start, width):
        if kind == "O":
            return lax.dynamic_slice_in_dim(out_weight[0], start, width, 0)
        if kind == "S":
            return jnp.concatenate([columns(one, start, width) for one in stale])
        return columns(qkv["QKV".index(kind)], start, width)

    def block_of(kind, layer, slot):
        at = (mine_at if slot == 0 else 1 - mine_at) * bw
        got = get("a" + kind)
        other = lax.dynamic_slice_in_dim(got, at, bw, 0) if kind == "O" else columns(got, at, bw)
        block = jnp.where(s == layer, cut(kind, s * wide + at, bw), other)
        return block.reshape(2, slot_len, bw) if kind == "S" else block

    for kind in "QKVOS":
        step("a" + kind)(
            lambda kind=kind: swap("a" + kind, cut(kind, (1 - s) * wide, wide))
        )

    def move(kind, layer, d):
        name = f"{kind}{layer}.{d}"
        for bit in reversed(last_bits):
            if d & bit:
                return send(name, get(f"{kind}{layer}.{d ^ bit}"), bit)
        block = block_of(kind, layer, 1 if d & pair_bit else 0)
        return send(name, block, d) if d else gated(block, name)

    for layer in range(2):
        for kind in "QKVO":
            for d in range(rows):
                step(f"{kind}{layer}.{d}")(functools.partial(move, kind, layer, d))
        for d in offsets:
            step(f"S{layer}.{d}")(functools.partial(move, "S", layer, d))

    def of_rows(kind, layer):
        return [get(f"{kind}{layer}.{d}") for d in range(rows)]

    def stale_of(layer):
        return [get(f"S{layer}.{d}") for d in offsets]

    @step("n")
    def _():
        numbers = jnp.concatenate([patch_ends[0], timestep])
        return jnp.stack([numbers] + [send("n", numbers, di) for di in offsets[1:]])

    @step("m")
    def _():
        feats = jnp.pad(embed_time(get("n")[:, NP]), ((0, 8 - slots), (0, 0)))
        own = pl.pallas_call(
            functools.partial(mod_kernel, slots),
            out_shape=jax.ShapeDtypeStruct((slots, 3, feat), jnp.float32),
            in_specs=[vmem_spec(), vmem_spec()],
            out_specs=vmem_spec(),
            compiler_params=pltpu.CompilerParams(vmem_limit_bytes=VMEM_LIMIT),
            name="modulation",
        )(gated(feats, "m"), mod_weight[0].transpose(1, 0, 2))
        other = swap("mc", own)
        return [jnp.where(s == layer, own, other) for layer in range(2)]

    x_half = lax.dynamic_slice_in_dim(hidden_in[0], s * half, half, 0)
    step("x.0.0")(lambda: gated(x_half, "x.0.0"))
    step("g.0.0")(lambda: finish(0, x_half))
    for kind in "xg":
        for di, dc in places:
            name = f"{kind}.{di}.{dc}"

            def bring(kind=kind, name=name, di=di, dc=dc):
                if dc and kind in TREE:
                    return send(name, get(f"{kind}.{di}.0"), 0, dc)
                return send(name, get(f"{kind}.0.0"), di, dc)

            if (di, dc) != (0, 0):
                step(name)(bring)
            step(name + "c")(lambda name=name: swap(name + "c", get(name)))
    x_rest = lax.dynamic_slice_in_dim(hidden_in[0], (1 - s) * half, half, 0)
    step("x.0.0c")(lambda: x_rest)

    def x_pieces(kind):
        return [get(f"{kind}.{di}.{dc}" + end) for di, dc in places for end in ("", "c")]

    def modulated(layer):
        pieces = x_pieces("xg"[layer])
        shape = (slots * slot_len, feat)
        return pl.pallas_call(
            functools.partial(modulate_kernel, (slots, slot_len, cols), wc),
            out_shape=jax.ShapeDtypeStruct(shape, jnp.bfloat16),
            in_specs=[vmem_spec()] + [any_spec()] * len(pieces),
            out_specs=vmem_spec(),
            scratch_shapes=[
                pltpu.VMEM((cols, slots * slot_len, wc), jnp.bfloat16),
                pltpu.VMEM((2, slots * slot_len, 128), jnp.float32),
                pltpu.VMEM((slots, 1, feat), jnp.float32),
                pltpu.SemaphoreType.DMA((len(pieces),)),
            ],
            compiler_params=pltpu.CompilerParams(vmem_limit_bytes=VMEM_LIMIT),
            name="modulate",
        )(gated(get("m")[layer], f"l{layer}"), *pieces)

    def scores(layer):
        return pl.pallas_call(
            functools.partial(scores_kernel, (slots, slot_len, rows, kr, bw)),
            out_shape=jax.ShapeDtypeStruct(
                (slots, bw // HD, slot_len, 2 * slot_len), jnp.bfloat16
            ),
            in_specs=[pl.BlockSpec(memory_space=pltpu.SMEM)]
            + [any_spec()] * (1 + 2 * rows + slots),
            out_specs=vmem_spec(),
            scratch_shapes=[
                pltpu.VMEM((slots * slot_len, feat), jnp.bfloat16),
                pltpu.VMEM((2, feat, bw), jnp.bfloat16),
                pltpu.VMEM((2, slots * slot_len, bw), jnp.float32),
                pltpu.VMEM((slots * slot_len, bw), jnp.bfloat16),
                pltpu.VMEM((slots, 2 * slot_len, bw), jnp.bfloat16),
                pltpu.SemaphoreType.DMA((1,)),
                pltpu.SemaphoreType.DMA((2 * rows,)),
                pltpu.SemaphoreType.DMA((slots,)),
            ],
            compiler_params=pltpu.CompilerParams(vmem_limit_bytes=VMEM_LIMIT),
            name="scores",
        )(
            gated(get("n")[:, :NP], f"k{layer}"),
            get(f"l{layer}"),
            *of_rows("Q", layer),
            *of_rows("K", layer),
            *stale_of(layer),
        )

    def mix(layer):
        plan = (slots, slot_len, cols, rows, kr, nr, bw, wc)
        shape = jax.ShapeDtypeStruct((slots, half, feat), jnp.bfloat16)
        return pl.pallas_call(
            functools.partial(mix_kernel, plan),
            out_shape=(shape, shape),
            in_specs=[any_spec()] * (2 + 2 * rows + slots),
            out_specs=(vmem_spec(), vmem_spec()),
            scratch_shapes=[
                pltpu.VMEM((slots * slot_len, feat), jnp.bfloat16),
                pltpu.VMEM((slots, bw // HD, slot_len, 2 * slot_len), jnp.bfloat16),
                pltpu.VMEM((feat, bw), jnp.bfloat16),
                pltpu.VMEM((rows, bw, nr), jnp.bfloat16),
                pltpu.VMEM((slots, 2 * slot_len, bw), jnp.bfloat16),
                pltpu.VMEM((slots * slot_len, bw), jnp.bfloat16),
                pltpu.SemaphoreType.DMA((2,)),
                pltpu.SemaphoreType.DMA((2 * rows,)),
                pltpu.SemaphoreType.DMA((slots,)),
            ],
            compiler_params=pltpu.CompilerParams(vmem_limit_bytes=VMEM_LIMIT),
            name="mix",
        )(
            get(f"l{layer}"),
            gated(get(f"k{layer}"), f"v{layer}"),
            *of_rows("V", layer),
            *of_rows("O", layer),
            *stale_of(layer),
        )

    def parts(layer):
        keep, other = get(f"v{layer}")[0], get(f"p{layer}")

        def part(array, di, dc):
            return array[offsets.index(di), :, dc * wc : (dc + 1) * wc].astype(jnp.float32)

        return {place: part(keep, *place) + part(other, *place) for place in places}

    def summed(layer, di):
        part = get(f"t{layer}")[di, 0]
        for dc in range(1, cols):
            part = part + get(f"r{layer}.{di}.{dc}").astype(jnp.float32)
        return part

    def give(layer, di, dc):
        name = f"r{layer}.{di}.{dc}"
        if f"r{layer}" not in TREE:
            return send(name, get(f"t{layer}")[di, dc].astype(jnp.bfloat16), di, dc)
        if dc:
            return send(name, get(f"t{layer}")[di, dc].astype(jnp.bfloat16), 0, dc)
        return send(name, get(f"u{layer}.{di}").astype(jnp.bfloat16), di, 0)

    for layer in range(2):
        step(f"l{layer}")(functools.partial(modulated, layer))
        step(f"k{layer}")(functools.partial(scores, layer))
        step(f"v{layer}")(functools.partial(mix, layer))
        step(f"p{layer}")(lambda layer=layer: swap(f"p{layer}", get(f"v{layer}")[1]))
        step(f"t{layer}")(functools.partial(parts, layer))
        for di, dc in places:
            if (di, dc) != (0, 0):
                step(f"r{layer}.{di}.{dc}")(functools.partial(give, layer, di, dc))
        for di in offsets:
            step(f"u{layer}.{di}")(functools.partial(summed, layer, di))

    def finish(layer, x_own):
        if f"r{layer}" in TREE:
            branch = get(f"u{layer}.0")
            for di in offsets[1:]:
                branch = branch + get(f"r{layer}.{di}.0").astype(jnp.float32)
        else:
            branch = get(f"t{layer}")[0, 0]
            for di, dc in places[1:]:
                branch = branch + get(f"r{layer}.{di}.{dc}").astype(jnp.float32)
        gate_own = columns(get("m")[layer][0, 2], c * wc, wc)
        updated = x_own.astype(jnp.float32) + gate_own[None, :] * branch
        positions = jnp.arange(half)[:, None] + s * half
        return jnp.where(positions < patch_ends[0, NP - 1], updated, 0.0).astype(jnp.bfloat16)

    first = get("g.0.0")
    second = finish(1, first)
    low = jnp.where(s == 0, first, swap("e", second))
    high = jnp.where(s == 0, get("g.0.0c"), second)
    return jnp.concatenate([low, high], axis=0)[None, None]


def solution(mesh):
    return jax.shard_map(
        shards,
        mesh=mesh,
        in_specs=(
            P("row", None, "col"),
            P("row", None),
            P("row"),
            P("section", None, None, None),
            P("section", "row", None, "col"),
            P("section", "col", "row"),
            P("section", "row", None, "col"),
            P("section", "row", None, "col"),
        ),
        out_specs=P("section", "row", None, "col"),
        check_vma=False,
    )
```

```python
import functools
import math

import jax
import jax.numpy as jnp
from jax import lax
from jax.experimental import pallas as pl
from jax.experimental.pallas import tpu as pltpu
from jax.sharding import PartitionSpec as P

HD = 128
FREQ = 256
NP = 4
AXES = ("section", "row", "col")
VMEM_LIMIT = 56 * 1024 * 1024


def send_to(array, where):
    ns, nr, nc = (lax.axis_size(axis) for axis in AXES)
    pairs = []
    for s in range(ns):
        for i in range(nr):
            for c in range(nc):
                ts, ti, tc = where(s, i, c)
                pairs.append(((s * nr + i) * nc + c, (ts * nr + ti) * nc + tc))
    return lax.ppermute(array, AXES, pairs)


def to_core(array):
    return send_to(array, lambda s, i, c: (1 - s, i, c))


def after(array, *others):
    return lax.optimization_barrier((array,) + others)[0]


def pick(array, index):
    return lax.dynamic_index_in_dim(array, index, 0, keepdims=False)


def embed_time(timestep):
    half_width = FREQ // 2
    frequency = jnp.exp(
        jnp.arange(half_width, dtype=jnp.float32) * (-math.log(10000.0) / half_width)
    )
    angles = timestep.astype(jnp.float32)[:, None] * frequency[None, :]
    return jnp.concatenate([jnp.cos(angles), jnp.sin(angles)], axis=1).astype(jnp.bfloat16)


def any_spec():
    return pl.BlockSpec(memory_space=pl.ANY)


def vmem_spec():
    return pl.BlockSpec(memory_space=pltpu.VMEM)


def load_rows(pieces, target, sem, first, rows_each):
    i = lax.axis_index("row")
    copies = []
    for d, piece in enumerate(pieces):
        if rows_each is None:
            place = target.at[i ^ d]
        else:
            place = target.at[pl.ds(pl.multiple_of((i ^ d) * rows_each, 32), rows_each), :]
        copies.append(pltpu.make_async_copy(piece, place, sem.at[first + d]))
        copies[-1].start()
    return copies


def fresh_and_valid(ends_ref, slot, slot_len):
    key_at = lax.broadcasted_iota(jnp.int32, (slot_len, slot_len), 1)
    query_at = lax.broadcasted_iota(jnp.int32, (slot_len, slot_len), 0)
    limit = jnp.full((slot_len, slot_len), ends_ref[slot, NP - 1], jnp.int32)
    for m in range(NP - 2, -1, -1):
        limit = jnp.where(query_at < ends_ref[slot, m], ends_ref[slot, m], limit)
    return key_at < limit, key_at < ends_ref[slot, NP - 1]


def load_x(plan, x_refs, xv, sem):
    slots, slot_len, cols = plan
    s, c = lax.axis_index("section"), lax.axis_index("col")
    half = slot_len // 2
    copies = []
    for slot in range(slots):
        for dc in range(cols):
            for h in range(2):
                place = len(copies)
                col = lax.rem(c + cols - dc, cols)
                row = pl.multiple_of(slot * slot_len + jnp.where(s == h, 0, half), half)
                copies.append(
                    pltpu.make_async_copy(
                        x_refs[place], xv.at[col, pl.ds(row, half), :], sem.at[place]
                    )
                )
                copies[-1].start()
    return copies


def modulate(plan, wc, mod_ref, xv, stats, one_plus, xm):
    slots, slot_len, cols = plan
    feat, tile, lane = cols * wc, 16, 128

    def add_up(step, carry):
        rows = pl.ds(pl.multiple_of(step * tile, tile), tile)
        total = jnp.zeros((tile, lane), jnp.float32)
        squares = jnp.zeros((tile, lane), jnp.float32)
        for col in range(cols):
            for first in range(0, wc, lane):
                part = xv[col, rows, first : first + lane].astype(jnp.float32)
                total += part
                squares += part * part
        stats[0, rows, :] = total
        stats[1, rows, :] = squares
        return carry

    steps = slots * slot_len // tile
    lax.fori_loop(0, steps, add_up, 0, unroll=4)
    mean = jnp.sum(stats[0], axis=-1, keepdims=True) / feat
    var = jnp.sum(stats[1], axis=-1, keepdims=True) / feat - mean * mean
    shape = (slots * slot_len, lane)
    stats[0] = jnp.broadcast_to(mean, shape)
    stats[1] = jnp.broadcast_to(lax.rsqrt(var + 1e-06), shape)
    for slot in range(slots):

        def write(step, carry, slot=slot):
            rows = pl.ds(pl.multiple_of(slot * slot_len + step * tile, tile), tile)
            mean, inverse = stats[0, rows, :], stats[1, rows, :]
            for col in range(cols):
                for first in range(0, wc, lane):
                    span = slice(col * wc + first, col * wc + first + lane)
                    part = xv[col, rows, first : first + lane].astype(jnp.float32)
                    part = (part - mean) * inverse * one_plus[slot, :, span]
                    xm[rows, span] = (part + mod_ref[slot, 0:1, span]).astype(jnp.bfloat16)
            return carry

        lax.fori_loop(0, slot_len // tile, write, 0, unroll=2)


def layer_kernel(plan, ends_ref, mod_ref, *refs):
    slots, slot_len, cols, n_x, n_w, kr, nr, bw, wc = plan
    x_refs, refs = refs[:n_x], refs[n_x:]
    w_refs, refs = [refs[t * n_w : (t + 1) * n_w] for t in range(4)], refs[4 * n_w :]
    kv_refs, refs = refs[:slots], refs[slots:]
    keep_ref, pass_ref, xv, stats, one_plus, xm, wv, ov, raw, queries, keys, values, att, out = refs[:14]
    x_sem, w_sem, kv_sem, out_sem = refs[14:]
    s, c = lax.axis_index("section"), lax.axis_index("col")
    half, lanes_of = slot_len // 2, [slice(h * HD, (h + 1) * HD) for h in range(bw // HD)]
    x_copies = load_x((slots, slot_len, cols), x_refs, xv, x_sem)
    copies = [load_rows(w_refs[t], wv.at[t], w_sem, t * n_w, kr) for t in range(2)]
    kv_copies = []
    for slot in range(slots):
        for t, target in enumerate((keys, values)):
            place = target.at[slot, pl.ds(slot_len, slot_len), :]
            kv_copies.append(
                pltpu.make_async_copy(kv_refs[slot].at[t], place, kv_sem.at[2 * slot + t])
            )
            kv_copies[-1].start()
    copies.append(load_rows(w_refs[2], wv.at[2], w_sem, 2 * n_w, kr))
    copies.append(load_rows(w_refs[3], ov, w_sem, 3 * n_w, None))
    one_plus[...] = 1.0 + mod_ref[:, 1:2, :]
    for copy in x_copies:
        copy.wait()
    modulate((slots, slot_len, cols), wc, mod_ref, xv, stats, one_plus, xm)
    for t in range(2):
        for copy in copies[t]:
            copy.wait()
        raw[t] = jnp.dot(xm[...], wv[t], preferred_element_type=jnp.float32)
    for copy in kv_copies + copies[2]:
        copy.wait()

    def normed(block):
        mean = jnp.mean(block * block, axis=-1, keepdims=True)
        return (block * lax.rsqrt(mean + 1e-06)).astype(jnp.bfloat16)

    for lanes in lanes_of:
        queries[:, lanes] = normed(raw[0, :, lanes])
        fresh_keys = normed(raw[1, :, lanes])
        for slot in range(slots):
            keys[slot, 0:slot_len, lanes] = fresh_keys[slot * slot_len : (slot + 1) * slot_len]
    fresh_values = jnp.dot(xm[...], wv[2], preferred_element_type=jnp.float32).astype(jnp.bfloat16)
    for slot in range(slots):
        values[slot, 0:slot_len, :] = fresh_values[slot * slot_len : (slot + 1) * slot_len]
    contract = (((1,), (1,)), ((), ()))
    for slot in range(slots):
        rows = pl.ds(slot * slot_len, slot_len)
        fresh, valid = fresh_and_valid(ends_ref, slot, slot_len)
        for lanes in lanes_of:
            both = lax.dot_general(
                queries[rows, lanes],
                keys[slot, :, lanes],
                contract,
                preferred_element_type=jnp.float32,
            )
            scores = jnp.where(fresh, both[:, :slot_len], both[:, slot_len:])
            weights = jnp.where(valid, jnp.exp(scores * (1.0 / math.sqrt(HD))), 0.0)
            weights = weights * (1.0 / jnp.sum(weights, axis=-1, keepdims=True))
            both = jnp.concatenate(
                [
                    jnp.where(fresh, weights, 0.0).astype(jnp.bfloat16),
                    jnp.where(fresh, 0.0, weights).astype(jnp.bfloat16),
                ],
                axis=1,
            )
            mixed = jnp.dot(both, values[slot, :, lanes], preferred_element_type=jnp.float32)
            att[rows, lanes] = mixed.astype(jnp.bfloat16)
    for copy in copies[3]:
        copy.wait()
    out_copies = []
    for k, (side, out_ref) in enumerate(((1 - s, pass_ref), (s, keep_ref))):
        blocks = []
        for slot in range(slots):
            row = pl.multiple_of(slot * slot_len + side * half, half)
            blocks.append(att[pl.ds(row, half), :])
        lhs = jnp.concatenate(blocks, axis=0)
        for place in range(n_w):
            row = lax.rem(c * (n_w // cols) + place, n_w)
            part = jnp.dot(lhs, ov[row], preferred_element_type=jnp.float32).astype(jnp.bfloat16)
            for slot in range(slots):
                out[k, slot, :, place * nr : (place + 1) * nr] = part[
                    slot * half : (slot + 1) * half
                ]
        out_copies.append(pltpu.make_async_copy(out.at[k], out_ref, out_sem.at[k]))
        out_copies[-1].start()
    for copy in out_copies:
        copy.wait()


def mod_kernel(slots, feats_ref, weight_ref, out_ref):
    for k in range(3):
        part = jnp.dot(feats_ref[...], weight_ref[k], preferred_element_type=jnp.float32)
        for slot in range(slots):
            out_ref[slot, k : k + 1, :] = part[slot : slot + 1, :]


GATES = {
    "K0.4": ("Q0.4",),
    "K0.6": ("Q0.6",),
    "V0.4": ("K0.4",),
    "V0.6": ("K0.6",),
    "O0.4": ("V0.4",),
    "O0.6": ("V0.6",),
    "Q1.4": ("O0.4",),
    "Q1.6": ("O0.6",),
    "K1.4": ("Q1.4",),
    "K1.6": ("Q1.6",),
    "V1.4": ("K1.4",),
    "V1.6": ("K1.6",),
    "O1.4": ("V1.4",),
    "O1.6": ("V1.6",),
    "O0.2": ("Q0.2",),
    "Q1.2": ("S0.2",),
    "K1.2": ("K0.2",),
    "V1.2": ("V0.2",),
    "O1.2": ("O0.2", "O0.5",),
    "S1.2": ("Q1.2",),
    "K0.1": ("Q0.1",),
    "K0.3": ("Q0.3",),
    "Q0.5": ("K0.1",),
    "Q0.7": ("K0.3",),
    "V0.1": ("Q0.5", "O0.2",),
    "V0.3": ("Q0.7",),
    "K0.5": ("V0.1",),
    "K0.7": ("V0.3",),
    "O0.1": ("K0.5",),
    "O0.3": ("K0.7",),
    "V0.5": ("O0.1",),
    "V0.7": ("O0.3",),
    "Q1.1": ("V0.5",),
    "Q1.3": ("V0.7",),
    "O0.5": ("Q1.1",),
    "O0.7": ("Q1.3",),
    "K1.1": ("O0.5",),
    "K1.3": ("O0.7",),
    "Q1.5": ("K1.1",),
    "Q1.7": ("K1.3",),
    "V1.1": ("Q1.5",),
    "V1.3": ("Q1.7",),
    "K1.5": ("V1.1",),
    "K1.7": ("V1.3",),
    "O1.1": ("K1.5",),
    "O1.3": ("K1.7",),
    "V1.5": ("O1.1",),
    "V1.7": ("O1.3",),
    "O1.5": ("V1.5",),
    "O1.7": ("V1.7",),
    "n": ("aQ", "O0.2",),
    "m": ("Q0.6", "aV",),
    "p0": ("Q1.4", "Q1.6",),
    "r0.0.1": ("K1.4",),
    "O1.0": ("V1.3",),
    "x.0.0c": ("aV",),
    "V0.2": ("Q0.6",),
    "v0": ("aQ",),
    "l1": ("O1.6",),
}
TREE = ("x", "r0", "g", )


def shards(
    hidden_in, patch_ends, timestep, mod_weight, qkv_weight, out_weight, stale_keys, stale_values
):
    s, i, c = (lax.axis_index(axis) for axis in AXES)
    sections, rows, cols = (lax.axis_size(axis) for axis in AXES)
    _, slot_len, wc = hidden_in.shape
    feat = mod_weight.shape[-1]
    kr, nr = qkv_weight.shape[1], out_weight.shape[2]
    half = slot_len // 2
    slots = 2 if (wc // HD) % (2 * sections) == 0 else 1
    bw = wc // (sections * slots)
    pair_bit = 2 if slots == 2 else 0
    group_bits = [1 << b for b in reversed(range(rows.bit_length() - 1)) if 1 << b != pair_bit]
    first_bit, last_bits = group_bits[0], group_bits[1:]
    offsets = [0, pair_bit] if slots == 2 else [0]
    places = [(di, dc) for di in offsets for dc in range(cols)]
    mine_at = (i // 2) % 2 if slots == 2 else 0
    gates = GATES if rows == 8 and slots == 2 else {}
    made, steps = {}, {}

    def get(name):
        if name not in made:
            made[name] = None
            made[name] = steps[name]()
        return made[name]

    def gated(array, name):
        waits = [get(other) for other in gates.get(name, ())]
        return after(array, *waits) if waits else array

    def send(name, array, di=0, dc=0):
        def where(si, ii, ci):
            return si, ii ^ di, (ci + dc) % cols

        return send_to(gated(array, name), where)

    def swap(name, array):
        return send_to(gated(array, name), lambda si, ii, ci: (1 - si, ii, ci))

    def step(name):
        def note(make):
            steps[name] = make
            return make

        return note

    wide = slots * bw
    qkv = qkv_weight[0].transpose(1, 0, 2)
    stale = (stale_keys[0, 0], stale_values[0, 0])

    def columns(array, start, width):
        return lax.dynamic_slice_in_dim(array, start, width, array.ndim - 1)

    def cut(kind, start, width):
        if kind == "O":
            return lax.dynamic_slice_in_dim(out_weight[0], start, width, 0)
        if kind == "S":
            return jnp.concatenate([columns(one, start, width) for one in stale])
        return columns(qkv["QKV".index(kind)], start, width)

    def block_of(kind, layer, slot):
        at = (mine_at if slot == 0 else 1 - mine_at) * bw
        got = get("a" + kind)
        other = lax.dynamic_slice_in_dim(got, at, bw, 0) if kind == "O" else columns(got, at, bw)
        block = jnp.where(s == layer, cut(kind, s * wide + at, bw), other)
        return block.reshape(2, slot_len, bw) if kind == "S" else block

    for kind in "QKVOS":
        step("a" + kind)(
            lambda kind=kind: swap("a" + kind, cut(kind, (1 - s) * wide, wide))
        )

    def move(kind, layer, d):
        name = f"{kind}{layer}.{d}"
        for bit in reversed(last_bits):
            if d & bit:
                return send(name, get(f"{kind}{layer}.{d ^ bit}"), bit)
        block = block_of(kind, layer, 1 if d & pair_bit else 0)
        return send(name, block, d) if d else gated(block, name)

    for layer in range(2):
        for kind in "QKVO":
            for d in range(rows):
                step(f"{kind}{layer}.{d}")(functools.partial(move, kind, layer, d))
        for d in offsets:
            step(f"S{layer}.{d}")(functools.partial(move, "S", layer, d))

    def of_rows(kind, layer):
        return [get(f"{kind}{layer}.{d}") for d in range(rows)]

    def stale_of(layer):
        return [get(f"S{layer}.{d}") for d in offsets]

    @step("n")
    def _():
        numbers = jnp.concatenate([patch_ends[0], timestep])
        return jnp.stack([numbers] + [send("n", numbers, di) for di in offsets[1:]])

    @step("m")
    def _():
        feats = jnp.pad(embed_time(get("n")[:, NP]), ((0, 8 - slots), (0, 0)))
        own = pl.pallas_call(
            functools.partial(mod_kernel, slots),
            out_shape=jax.ShapeDtypeStruct((slots, 3, feat), jnp.float32),
            in_specs=[vmem_spec(), vmem_spec()],
            out_specs=vmem_spec(),
            compiler_params=pltpu.CompilerParams(vmem_limit_bytes=VMEM_LIMIT),
            name="modulation",
        )(gated(feats, "m"), mod_weight[0].transpose(1, 0, 2))
        other = swap("mc", own)
        return [jnp.where(s == layer, own, other) for layer in range(2)]

    x_half = lax.dynamic_slice_in_dim(hidden_in[0], s * half, half, 0)
    step("x.0.0")(lambda: gated(x_half, "x.0.0"))
    step("g.0.0")(lambda: finish(0, x_half))
    for kind in "xg":
        for di, dc in places:
            name = f"{kind}.{di}.{dc}"

            def bring(kind=kind, name=name, di=di, dc=dc):
                if dc and kind in TREE:
                    return send(name, get(f"{kind}.{di}.0"), 0, dc)
                return send(name, get(f"{kind}.0.0"), di, dc)

            if (di, dc) != (0, 0):
                step(name)(bring)
            step(name + "c")(lambda name=name: swap(name + "c", get(name)))
    x_rest = lax.dynamic_slice_in_dim(hidden_in[0], (1 - s) * half, half, 0)
    step("x.0.0c")(lambda: x_rest)

    def x_pieces(kind):
        return [get(f"{kind}.{di}.{dc}" + end) for di, dc in places for end in ("", "c")]

    def heads_of(layer):
        pieces = x_pieces("xg"[layer])
        plan = (slots, slot_len, cols, len(pieces), rows, kr, nr, bw, wc)
        shape = jax.ShapeDtypeStruct((slots, half, feat), jnp.bfloat16)
        every = slots * slot_len
        return pl.pallas_call(
            functools.partial(layer_kernel, plan),
            out_shape=(shape, shape),
            in_specs=[pl.BlockSpec(memory_space=pltpu.SMEM), vmem_spec()]
            + [any_spec()] * (len(pieces) + 4 * rows + slots),
            out_specs=(any_spec(), any_spec()),
            scratch_shapes=[
                pltpu.VMEM((cols, every, wc), jnp.bfloat16),
                pltpu.VMEM((2, every, 128), jnp.float32),
                pltpu.VMEM((slots, 1, feat), jnp.float32),
                pltpu.VMEM((every, feat), jnp.bfloat16),
                pltpu.VMEM((3, feat, bw), jnp.bfloat16),
                pltpu.VMEM((rows, bw, nr), jnp.bfloat16),
                pltpu.VMEM((2, every, bw), jnp.float32),
                pltpu.VMEM((every, bw), jnp.bfloat16),
                pltpu.VMEM((slots, 2 * slot_len, bw), jnp.bfloat16),
                pltpu.VMEM((slots, 2 * slot_len, bw), jnp.bfloat16),
                pltpu.VMEM((every, bw), jnp.bfloat16),
                pltpu.VMEM((2, slots, half, feat), jnp.bfloat16),
                pltpu.SemaphoreType.DMA((len(pieces),)),
                pltpu.SemaphoreType.DMA((4 * rows,)),
                pltpu.SemaphoreType.DMA((2 * slots,)),
                pltpu.SemaphoreType.DMA((2,)),
            ],
            compiler_params=pltpu.CompilerParams(vmem_limit_bytes=VMEM_LIMIT),
            name="layer",
        )(
            gated(get("n")[:, :NP], f"v{layer}"),
            get("m")[layer],
            *pieces,
            *[one for kind in "QKVO" for one in of_rows(kind, layer)],
            *stale_of(layer),
        )

    def parts(layer):
        keep, other = get(f"v{layer}")[0], get(f"p{layer}")

        def part(array, di, dc):
            return array[offsets.index(di), :, dc * wc : (dc + 1) * wc].astype(jnp.float32)

        return {place: part(keep, *place) + part(other, *place) for place in places}

    def summed(layer, di):
        part = get(f"t{layer}")[di, 0]
        for dc in range(1, cols):
            part = part + get(f"r{layer}.{di}.{dc}").astype(jnp.float32)
        return part

    def give(layer, di, dc):
        name = f"r{layer}.{di}.{dc}"
        if f"r{layer}" not in TREE:
            return send(name, get(f"t{layer}")[di, dc].astype(jnp.bfloat16), di, dc)
        if dc:
            return send(name, get(f"t{layer}")[di, dc].astype(jnp.bfloat16), 0, dc)
        return send(name, get(f"u{layer}.{di}").astype(jnp.bfloat16), di, 0)

    for layer in range(2):
        step(f"v{layer}")(functools.partial(heads_of, layer))
        step(f"p{layer}")(lambda layer=layer: swap(f"p{layer}", get(f"v{layer}")[1]))
        step(f"t{layer}")(functools.partial(parts, layer))
        for di, dc in places:
            if (di, dc) != (0, 0):
                step(f"r{layer}.{di}.{dc}")(functools.partial(give, layer, di, dc))
        for di in offsets:
            step(f"u{layer}.{di}")(functools.partial(summed, layer, di))

    def finish(layer, x_own):
        if f"r{layer}" in TREE:
            branch = get(f"u{layer}.0")
            for di in offsets[1:]:
                branch = branch + get(f"r{layer}.{di}.0").astype(jnp.float32)
        else:
            branch = get(f"t{layer}")[0, 0]
            for di, dc in places[1:]:
                branch = branch + get(f"r{layer}.{di}.{dc}").astype(jnp.float32)
        gate_own = columns(get("m")[layer][0, 2], c * wc, wc)
        updated = x_own.astype(jnp.float32) + gate_own[None, :] * branch
        positions = jnp.arange(half)[:, None] + s * half
        return jnp.where(positions < patch_ends[0, NP - 1], updated, 0.0).astype(jnp.bfloat16)

    first = get("g.0.0")
    second = finish(1, first)
    low = jnp.where(s == 0, first, swap("e", second))
    high = jnp.where(s == 0, get("g.0.0c"), second)
    return jnp.concatenate([low, high], axis=0)[None, None]


def solution(mesh):
    return jax.shard_map(
        shards,
        mesh=mesh,
        in_specs=(
            P("row", None, "col"),
            P("row", None),
            P("row"),
            P("section", None, None, None),
            P("section", "row", None, "col"),
            P("section", "col", "row"),
            P("section", "row", None, "col"),
            P("section", "row", None, "col"),
        ),
        out_specs=P("section", "row", None, "col"),
        check_vma=False,
    )
```

```python
import functools
import math

import jax
import jax.numpy as jnp
from jax import lax
from jax.experimental import pallas as pl
from jax.experimental.pallas import tpu as pltpu
from jax.sharding import PartitionSpec as P

HD = 128
FREQ = 256
NP = 4
AXES = ("section", "row", "col")
VMEM_LIMIT = 56 * 1024 * 1024


def send_to(array, where):
    ns, nr, nc = (lax.axis_size(axis) for axis in AXES)
    pairs = []
    for s in range(ns):
        for i in range(nr):
            for c in range(nc):
                ts, ti, tc = where(s, i, c)
                pairs.append(((s * nr + i) * nc + c, (ts * nr + ti) * nc + tc))
    return lax.ppermute(array, AXES, pairs)


def to_core(array):
    return send_to(array, lambda s, i, c: (1 - s, i, c))


def after(array, *others):
    return lax.optimization_barrier((array,) + others)[0]


def pick(array, index):
    return lax.dynamic_index_in_dim(array, index, 0, keepdims=False)


def embed_time(timestep):
    half_width = FREQ // 2
    frequency = jnp.exp(
        jnp.arange(half_width, dtype=jnp.float32) * (-math.log(10000.0) / half_width)
    )
    angles = timestep.astype(jnp.float32)[:, None] * frequency[None, :]
    return jnp.concatenate([jnp.cos(angles), jnp.sin(angles)], axis=1).astype(jnp.bfloat16)


def any_spec():
    return pl.BlockSpec(memory_space=pl.ANY)


def vmem_spec():
    return pl.BlockSpec(memory_space=pltpu.VMEM)


def load_rows(pieces, target, sem, first, rows_each):
    i = lax.axis_index("row")
    copies = []
    for d, piece in enumerate(pieces):
        if rows_each is None:
            place = target.at[i ^ d]
        else:
            place = target.at[pl.ds(pl.multiple_of((i ^ d) * rows_each, 32), rows_each), :]
        copies.append(pltpu.make_async_copy(piece, place, sem.at[first + d]))
        copies[-1].start()
    return copies


def fresh_and_valid(ends_ref, slot, slot_len):
    key_at = lax.broadcasted_iota(jnp.int32, (slot_len, slot_len), 1)
    query_at = lax.broadcasted_iota(jnp.int32, (slot_len, slot_len), 0)
    limit = jnp.full((slot_len, slot_len), ends_ref[slot, NP - 1], jnp.int32)
    for m in range(NP - 2, -1, -1):
        limit = jnp.where(query_at < ends_ref[slot, m], ends_ref[slot, m], limit)
    return key_at < limit, key_at < ends_ref[slot, NP - 1]


def load_x(plan, x_refs, xv, sem):
    slots, slot_len, cols = plan
    s, c = lax.axis_index("section"), lax.axis_index("col")
    half = slot_len // 2
    copies = []
    for slot in range(slots):
        for dc in range(cols):
            for h in range(2):
                place = len(copies)
                col = lax.rem(c + cols - dc, cols)
                row = pl.multiple_of(slot * slot_len + jnp.where(s == h, 0, half), half)
                copies.append(
                    pltpu.make_async_copy(
                        x_refs[place], xv.at[col, pl.ds(row, half), :], sem.at[place]
                    )
                )
                copies[-1].start()
    return copies


def modulate(plan, wc, mod_ref, xv, stats, one_plus, xm):
    slots, slot_len, cols = plan
    feat, tile, lane = cols * wc, 16, 128

    def add_up(step, carry):
        rows = pl.ds(pl.multiple_of(step * tile, tile), tile)
        total = jnp.zeros((tile, lane), jnp.float32)
        squares = jnp.zeros((tile, lane), jnp.float32)
        for col in range(cols):
            for first in range(0, wc, lane):
                part = xv[col, rows, first : first + lane].astype(jnp.float32)
                total += part
                squares += part * part
        stats[0, rows, :] = total
        stats[1, rows, :] = squares
        return carry

    steps = slots * slot_len // tile
    lax.fori_loop(0, steps, add_up, 0, unroll=4)
    mean = jnp.sum(stats[0], axis=-1, keepdims=True) / feat
    var = jnp.sum(stats[1], axis=-1, keepdims=True) / feat - mean * mean
    shape = (slots * slot_len, lane)
    stats[0] = jnp.broadcast_to(mean, shape)
    stats[1] = jnp.broadcast_to(lax.rsqrt(var + 1e-06), shape)
    for slot in range(slots):

        def write(step, carry, slot=slot):
            rows = pl.ds(pl.multiple_of(slot * slot_len + step * tile, tile), tile)
            mean, inverse = stats[0, rows, :], stats[1, rows, :]
            for col in range(cols):
                for first in range(0, wc, lane):
                    span = slice(col * wc + first, col * wc + first + lane)
                    part = xv[col, rows, first : first + lane].astype(jnp.float32)
                    part = (part - mean) * inverse * one_plus[slot, :, span]
                    xm[rows, span] = (part + mod_ref[slot, 0:1, span]).astype(jnp.bfloat16)
            return carry

        lax.fori_loop(0, slot_len // tile, write, 0, unroll=2)


def layer_kernel(plan, ends_ref, mod_ref, *refs):
    slots, slot_len, cols, n_x, n_w, kr, nr, bw, wc = plan
    x_refs, refs = refs[:n_x], refs[n_x:]
    w_refs, refs = [refs[t * n_w : (t + 1) * n_w] for t in range(4)], refs[4 * n_w :]
    kv_refs, refs = refs[:slots], refs[slots:]
    keep_ref, pass_ref, xv, stats, one_plus, xm, wv, ov, raw, queries, keys, values, att, out = refs[:14]
    x_sem, w_sem, kv_sem, out_sem = refs[14:]
    s, c = lax.axis_index("section"), lax.axis_index("col")
    half, lanes_of = slot_len // 2, [slice(h * HD, (h + 1) * HD) for h in range(bw // HD)]
    one_plus[...] = 1.0 + mod_ref[:, 1:2, :]
    for copy in load_x((slots, slot_len, cols), x_refs, xv, x_sem):
        copy.wait()
    copies = [load_rows(w_refs[t], wv.at[t], w_sem, t * n_w, kr) for t in range(2)]
    modulate((slots, slot_len, cols), wc, mod_ref, xv, stats, one_plus, xm)
    for copy in copies[0] + copies[1]:
        copy.wait()
    copies.append(load_rows(w_refs[2], wv.at[2], w_sem, 2 * n_w, kr))
    kv_copies = []
    for slot in range(slots):
        for t, target in enumerate((keys, values)):
            place = target.at[slot, pl.ds(slot_len, slot_len), :]
            kv_copies.append(
                pltpu.make_async_copy(kv_refs[slot].at[t], place, kv_sem.at[2 * slot + t])
            )
            kv_copies[-1].start()
    copies.append(load_rows(w_refs[3], ov, w_sem, 3 * n_w, None))
    for t in range(2):
        raw[t] = jnp.dot(xm[...], wv[t], preferred_element_type=jnp.float32)
    for copy in kv_copies + copies[2]:
        copy.wait()

    def normed(block):
        mean = jnp.mean(block * block, axis=-1, keepdims=True)
        return (block * lax.rsqrt(mean + 1e-06)).astype(jnp.bfloat16)

    for lanes in lanes_of:
        queries[:, lanes] = normed(raw[0, :, lanes])
        fresh_keys = normed(raw[1, :, lanes])
        for slot in range(slots):
            keys[slot, 0:slot_len, lanes] = fresh_keys[slot * slot_len : (slot + 1) * slot_len]
    fresh_values = jnp.dot(xm[...], wv[2], preferred_element_type=jnp.float32).astype(jnp.bfloat16)
    for slot in range(slots):
        values[slot, 0:slot_len, :] = fresh_values[slot * slot_len : (slot + 1) * slot_len]
    contract = (((1,), (1,)), ((), ()))
    for slot in range(slots):
        rows = pl.ds(slot * slot_len, slot_len)
        fresh, valid = fresh_and_valid(ends_ref, slot, slot_len)
        for lanes in lanes_of:
            both = lax.dot_general(
                queries[rows, lanes],
                keys[slot, :, lanes],
                contract,
                preferred_element_type=jnp.float32,
            )
            scores = jnp.where(fresh, both[:, :slot_len], both[:, slot_len:])
            weights = jnp.where(valid, jnp.exp(scores * (1.0 / math.sqrt(HD))), 0.0)
            weights = weights * (1.0 / jnp.sum(weights, axis=-1, keepdims=True))
            both = jnp.concatenate(
                [
                    jnp.where(fresh, weights, 0.0).astype(jnp.bfloat16),
                    jnp.where(fresh, 0.0, weights).astype(jnp.bfloat16),
                ],
                axis=1,
            )
            mixed = jnp.dot(both, values[slot, :, lanes], preferred_element_type=jnp.float32)
            att[rows, lanes] = mixed.astype(jnp.bfloat16)
    for copy in copies[3]:
        copy.wait()
    out_copies = []
    for k, (side, out_ref) in enumerate(((1 - s, pass_ref), (s, keep_ref))):
        blocks = []
        for slot in range(slots):
            row = pl.multiple_of(slot * slot_len + side * half, half)
            blocks.append(att[pl.ds(row, half), :])
        lhs = jnp.concatenate(blocks, axis=0)
        for place in range(n_w):
            row = lax.rem(c * (n_w // cols) + place, n_w)
            part = jnp.dot(lhs, ov[row], preferred_element_type=jnp.float32).astype(jnp.bfloat16)
            for slot in range(slots):
                out[k, slot, :, place * nr : (place + 1) * nr] = part[
                    slot * half : (slot + 1) * half
                ]
        out_copies.append(pltpu.make_async_copy(out.at[k], out_ref, out_sem.at[k]))
        out_copies[-1].start()
    for copy in out_copies:
        copy.wait()


def mod_kernel(slots, feats_ref, weight_ref, out_ref):
    for k in range(3):
        part = jnp.dot(feats_ref[...], weight_ref[k], preferred_element_type=jnp.float32)
        for slot in range(slots):
            out_ref[slot, k : k + 1, :] = part[slot : slot + 1, :]


GATES = {
    "K0.4": ("Q0.4",),
    "K0.6": ("Q0.6",),
    "V0.4": ("K0.4",),
    "V0.6": ("K0.6",),
    "O0.4": ("V0.4",),
    "O0.6": ("V0.6",),
    "Q1.4": ("O0.4",),
    "Q1.6": ("O0.6",),
    "K1.4": ("Q1.4",),
    "K1.6": ("Q1.6",),
    "V1.4": ("K1.4",),
    "V1.6": ("K1.6",),
    "O1.4": ("V1.4",),
    "O1.6": ("V1.6",),
    "O0.2": ("Q0.2",),
    "Q1.2": ("S0.2",),
    "K1.2": ("K0.2",),
    "V1.2": ("V0.2",),
    "O1.2": ("O0.2", "O0.5",),
    "S1.2": ("Q1.2",),
    "K0.1": ("Q0.1",),
    "K0.3": ("Q0.3",),
    "Q0.5": ("K0.1",),
    "Q0.7": ("K0.3",),
    "V0.1": ("Q0.5", "O0.2",),
    "V0.3": ("Q0.7",),
    "K0.5": ("V0.1",),
    "K0.7": ("V0.3",),
    "O0.1": ("K0.5",),
    "O0.3": ("K0.7",),
    "V0.5": ("O0.1",),
    "V0.7": ("O0.3",),
    "Q1.1": ("V0.5",),
    "Q1.3": ("V0.7",),
    "O0.5": ("Q1.1",),
    "O0.7": ("Q1.3",),
    "K1.1": ("O0.5",),
    "K1.3": ("O0.7", "Q0.1",),
    "Q1.5": ("K1.1",),
    "Q1.7": ("K1.3",),
    "V1.1": ("Q1.5", "V1.4",),
    "V1.3": ("Q1.7",),
    "K1.5": ("V1.1",),
    "K1.7": ("V1.3",),
    "O1.1": ("K1.5",),
    "O1.3": ("K1.7",),
    "V1.5": ("O1.1",),
    "V1.7": ("O1.3",),
    "O1.5": ("V1.5",),
    "O1.7": ("V1.7",),
    "n": ("aQ", "O0.2",),
    "m": ("Q0.6", "aV",),
    "p0": ("Q1.4", "Q1.6",),
    "r0.0.1": ("K1.4",),
    "O1.0": ("V1.3",),
    "x.0.0c": ("aV",),
    "V0.2": ("Q0.6",),
    "v0": ("aQ",),
    "l1": ("O1.6",),
    "x.0.1": ("Q1.1",),
}
TREE = ("x", "r0", "g", )


def shards(
    hidden_in, patch_ends, timestep, mod_weight, qkv_weight, out_weight, stale_keys, stale_values
):
    s, i, c = (lax.axis_index(axis) for axis in AXES)
    sections, rows, cols = (lax.axis_size(axis) for axis in AXES)
    _, slot_len, wc = hidden_in.shape
    feat = mod_weight.shape[-1]
    kr, nr = qkv_weight.shape[1], out_weight.shape[2]
    half = slot_len // 2
    slots = 2 if (wc // HD) % (2 * sections) == 0 else 1
    bw = wc // (sections * slots)
    pair_bit = 2 if slots == 2 else 0
    group_bits = [1 << b for b in reversed(range(rows.bit_length() - 1)) if 1 << b != pair_bit]
    first_bit, last_bits = group_bits[0], group_bits[1:]
    offsets = [0, pair_bit] if slots == 2 else [0]
    places = [(di, dc) for di in offsets for dc in range(cols)]
    mine_at = (i // 2) % 2 if slots == 2 else 0
    gates = GATES if rows == 8 and slots == 2 else {}
    made, steps = {}, {}

    def get(name):
        if name not in made:
            made[name] = None
            made[name] = steps[name]()
        return made[name]

    def gated(array, name):
        waits = [get(other) for other in gates.get(name, ())]
        return after(array, *waits) if waits else array

    def send(name, array, di=0, dc=0):
        def where(si, ii, ci):
            return si, ii ^ di, (ci + dc) % cols

        return send_to(gated(array, name), where)

    def swap(name, array):
        return send_to(gated(array, name), lambda si, ii, ci: (1 - si, ii, ci))

    def step(name):
        def note(make):
            steps[name] = make
            return make

        return note

    wide = slots * bw
    qkv = qkv_weight[0].transpose(1, 0, 2)
    stale = (stale_keys[0, 0], stale_values[0, 0])

    def columns(array, start, width):
        return lax.dynamic_slice_in_dim(array, start, width, array.ndim - 1)

    def cut(kind, start, width):
        if kind == "O":
            return lax.dynamic_slice_in_dim(out_weight[0], start, width, 0)
        if kind == "S":
            return jnp.concatenate([columns(one, start, width) for one in stale])
        return columns(qkv["QKV".index(kind)], start, width)

    def block_of(kind, layer, slot):
        at = (mine_at if slot == 0 else 1 - mine_at) * bw
        got = get("a" + kind)
        other = lax.dynamic_slice_in_dim(got, at, bw, 0) if kind == "O" else columns(got, at, bw)
        block = jnp.where(s == layer, cut(kind, s * wide + at, bw), other)
        return block.reshape(2, slot_len, bw) if kind == "S" else block

    for kind in "QKVOS":
        step("a" + kind)(
            lambda kind=kind: swap("a" + kind, cut(kind, (1 - s) * wide, wide))
        )

    def move(kind, layer, d):
        name = f"{kind}{layer}.{d}"
        for bit in reversed(last_bits):
            if d & bit:
                return send(name, get(f"{kind}{layer}.{d ^ bit}"), bit)
        block = block_of(kind, layer, 1 if d & pair_bit else 0)
        return send(name, block, d) if d else gated(block, name)

    for layer in range(2):
        for kind in "QKVO":
            for d in range(rows):
                step(f"{kind}{layer}.{d}")(functools.partial(move, kind, layer, d))
        for d in offsets:
            step(f"S{layer}.{d}")(functools.partial(move, "S", layer, d))

    def of_rows(kind, layer):
        return [get(f"{kind}{layer}.{d}") for d in range(rows)]

    def stale_of(layer):
        return [get(f"S{layer}.{d}") for d in offsets]

    @step("n")
    def _():
        numbers = jnp.concatenate([patch_ends[0], timestep])
        return jnp.stack([numbers] + [send("n", numbers, di) for di in offsets[1:]])

    @step("m")
    def _():
        feats = jnp.pad(embed_time(get("n")[:, NP]), ((0, 8 - slots), (0, 0)))
        own = pl.pallas_call(
            functools.partial(mod_kernel, slots),
            out_shape=jax.ShapeDtypeStruct((slots, 3, feat), jnp.float32),
            in_specs=[vmem_spec(), vmem_spec()],
            out_specs=vmem_spec(),
            compiler_params=pltpu.CompilerParams(vmem_limit_bytes=VMEM_LIMIT),
            name="modulation",
        )(gated(feats, "m"), mod_weight[0].transpose(1, 0, 2))
        other = swap("mc", own)
        return [jnp.where(s == layer, own, other) for layer in range(2)]

    x_half = lax.dynamic_slice_in_dim(hidden_in[0], s * half, half, 0)
    step("x.0.0")(lambda: gated(x_half, "x.0.0"))
    step("g.0.0")(lambda: finish(0, x_half))
    for kind in "xg":
        for di, dc in places:
            name = f"{kind}.{di}.{dc}"

            def bring(kind=kind, name=name, di=di, dc=dc):
                if dc and kind in TREE:
                    return send(name, get(f"{kind}.{di}.0"), 0, dc)
                return send(name, get(f"{kind}.0.0"), di, dc)

            if (di, dc) != (0, 0):
                step(name)(bring)
            step(name + "c")(lambda name=name: swap(name + "c", get(name)))
    x_rest = lax.dynamic_slice_in_dim(hidden_in[0], (1 - s) * half, half, 0)
    step("x.0.0c")(lambda: x_rest)

    def x_pieces(kind):
        return [get(f"{kind}.{di}.{dc}" + end) for di, dc in places for end in ("", "c")]

    def heads_of(layer):
        pieces = x_pieces("xg"[layer])
        plan = (slots, slot_len, cols, len(pieces), rows, kr, nr, bw, wc)
        shape = jax.ShapeDtypeStruct((slots, half, feat), jnp.bfloat16)
        every = slots * slot_len
        return pl.pallas_call(
            functools.partial(layer_kernel, plan),
            out_shape=(shape, shape),
            in_specs=[pl.BlockSpec(memory_space=pltpu.SMEM), vmem_spec()]
            + [any_spec()] * (len(pieces) + 4 * rows + slots),
            out_specs=(any_spec(), any_spec()),
            scratch_shapes=[
                pltpu.VMEM((cols, every, wc), jnp.bfloat16),
                pltpu.VMEM((2, every, 128), jnp.float32),
                pltpu.VMEM((slots, 1, feat), jnp.float32),
                pltpu.VMEM((every, feat), jnp.bfloat16),
                pltpu.VMEM((3, feat, bw), jnp.bfloat16),
                pltpu.VMEM((rows, bw, nr), jnp.bfloat16),
                pltpu.VMEM((2, every, bw), jnp.float32),
                pltpu.VMEM((every, bw), jnp.bfloat16),
                pltpu.VMEM((slots, 2 * slot_len, bw), jnp.bfloat16),
                pltpu.VMEM((slots, 2 * slot_len, bw), jnp.bfloat16),
                pltpu.VMEM((every, bw), jnp.bfloat16),
                pltpu.VMEM((2, slots, half, feat), jnp.bfloat16),
                pltpu.SemaphoreType.DMA((len(pieces),)),
                pltpu.SemaphoreType.DMA((4 * rows,)),
                pltpu.SemaphoreType.DMA((2 * slots,)),
                pltpu.SemaphoreType.DMA((2,)),
            ],
            compiler_params=pltpu.CompilerParams(vmem_limit_bytes=VMEM_LIMIT),
            name="layer",
        )(
            gated(get("n")[:, :NP], f"v{layer}"),
            get("m")[layer],
            *pieces,
            *[one for kind in "QKVO" for one in of_rows(kind, layer)],
            *stale_of(layer),
        )

    def parts(layer):
        keep, other = get(f"v{layer}")[0], get(f"p{layer}")

        def part(array, di, dc):
            return array[offsets.index(di), :, dc * wc : (dc + 1) * wc].astype(jnp.float32)

        return {place: part(keep, *place) + part(other, *place) for place in places}

    def summed(layer, di):
        part = get(f"t{layer}")[di, 0]
        for dc in range(1, cols):
            part = part + get(f"r{layer}.{di}.{dc}").astype(jnp.float32)
        return part

    def give(layer, di, dc):
        name = f"r{layer}.{di}.{dc}"
        if f"r{layer}" not in TREE:
            return send(name, get(f"t{layer}")[di, dc].astype(jnp.bfloat16), di, dc)
        if dc:
            return send(name, get(f"t{layer}")[di, dc].astype(jnp.bfloat16), 0, dc)
        return send(name, get(f"u{layer}.{di}").astype(jnp.bfloat16), di, 0)

    for layer in range(2):
        step(f"v{layer}")(functools.partial(heads_of, layer))
        step(f"p{layer}")(lambda layer=layer: swap(f"p{layer}", get(f"v{layer}")[1]))
        step(f"t{layer}")(functools.partial(parts, layer))
        for di, dc in places:
            if (di, dc) != (0, 0):
                step(f"r{layer}.{di}.{dc}")(functools.partial(give, layer, di, dc))
        for di in offsets:
            step(f"u{layer}.{di}")(functools.partial(summed, layer, di))

    def finish(layer, x_own):
        if f"r{layer}" in TREE:
            branch = get(f"u{layer}.0")
            for di in offsets[1:]:
                branch = branch + get(f"r{layer}.{di}.0").astype(jnp.float32)
        else:
            branch = get(f"t{layer}")[0, 0]
            for di, dc in places[1:]:
                branch = branch + get(f"r{layer}.{di}.{dc}").astype(jnp.float32)
        gate_own = columns(get("m")[layer][0, 2], c * wc, wc)
        updated = x_own.astype(jnp.float32) + gate_own[None, :] * branch
        positions = jnp.arange(half)[:, None] + s * half
        return jnp.where(positions < patch_ends[0, NP - 1], updated, 0.0).astype(jnp.bfloat16)

    first = get("g.0.0")
    second = finish(1, first)
    low = jnp.where(s == 0, first, swap("e", second))
    high = jnp.where(s == 0, get("g.0.0c"), second)
    return jnp.concatenate([low, high], axis=0)[None, None]


def solution(mesh):
    return jax.shard_map(
        shards,
        mesh=mesh,
        in_specs=(
            P("row", None, "col"),
            P("row", None),
            P("row"),
            P("section", None, None, None),
            P("section", "row", None, "col"),
            P("section", "col", "row"),
            P("section", "row", None, "col"),
            P("section", "row", None, "col"),
        ),
        out_specs=P("section", "row", None, "col"),
        check_vma=False,
    )
```

```python
import functools
import math

import jax
import jax.numpy as jnp
from jax import lax
from jax.experimental import pallas as pl
from jax.experimental.pallas import tpu as pltpu
from jax.sharding import PartitionSpec as P

HD = 128
FREQ = 256
NP = 4
AXES = ("section", "row", "col")
VMEM_LIMIT = 56 * 1024 * 1024


def send_to(array, where):
    ns, nr, nc = (lax.axis_size(axis) for axis in AXES)
    pairs = []
    for s in range(ns):
        for i in range(nr):
            for c in range(nc):
                ts, ti, tc = where(s, i, c)
                pairs.append(((s * nr + i) * nc + c, (ts * nr + ti) * nc + tc))
    return lax.ppermute(array, AXES, pairs)


def to_core(array):
    return send_to(array, lambda s, i, c: (1 - s, i, c))


def after(array, *others):
    return lax.optimization_barrier((array,) + others)[0]


def pick(array, index):
    return lax.dynamic_index_in_dim(array, index, 0, keepdims=False)


def embed_time(timestep):
    half_width = FREQ // 2
    frequency = jnp.exp(
        jnp.arange(half_width, dtype=jnp.float32) * (-math.log(10000.0) / half_width)
    )
    angles = timestep.astype(jnp.float32)[:, None] * frequency[None, :]
    return jnp.concatenate([jnp.cos(angles), jnp.sin(angles)], axis=1).astype(jnp.bfloat16)


def any_spec():
    return pl.BlockSpec(memory_space=pl.ANY)


def vmem_spec():
    return pl.BlockSpec(memory_space=pltpu.VMEM)


def load_rows(pieces, target, sem, first, rows_each):
    i = lax.axis_index("row")
    copies = []
    for d, piece in enumerate(pieces):
        if rows_each is None:
            place = target.at[i ^ d]
        else:
            place = target.at[pl.ds(pl.multiple_of((i ^ d) * rows_each, 32), rows_each), :]
        copies.append(pltpu.make_async_copy(piece, place, sem.at[first + d]))
        copies[-1].start()
    return copies


def fresh_and_valid(ends_ref, slot, slot_len):
    key_at = lax.broadcasted_iota(jnp.int32, (slot_len, slot_len), 1)
    query_at = lax.broadcasted_iota(jnp.int32, (slot_len, slot_len), 0)
    limit = jnp.full((slot_len, slot_len), ends_ref[slot, NP - 1], jnp.int32)
    for m in range(NP - 2, -1, -1):
        limit = jnp.where(query_at < ends_ref[slot, m], ends_ref[slot, m], limit)
    return key_at < limit, key_at < ends_ref[slot, NP - 1]


def load_x(plan, x_refs, xv, sem):
    slots, slot_len, cols = plan
    s, c = lax.axis_index("section"), lax.axis_index("col")
    half = slot_len // 2
    copies = []
    for slot in range(slots):
        for dc in range(cols):
            for h in range(2):
                place = len(copies)
                col = lax.rem(c + cols - dc, cols)
                row = pl.multiple_of(slot * slot_len + jnp.where(s == h, 0, half), half)
                copies.append(
                    pltpu.make_async_copy(
                        x_refs[place], xv.at[col, pl.ds(row, half), :], sem.at[place]
                    )
                )
                copies[-1].start()
    return copies


def modulate(plan, wc, mod_ref, xv, stats, one_plus, xm):
    slots, slot_len, cols = plan
    feat, tile, lane = cols * wc, 16, 128

    def add_up(step, carry):
        rows = pl.ds(pl.multiple_of(step * tile, tile), tile)
        total = jnp.zeros((tile, lane), jnp.float32)
        squares = jnp.zeros((tile, lane), jnp.float32)
        for col in range(cols):
            for first in range(0, wc, lane):
                part = xv[col, rows, first : first + lane].astype(jnp.float32)
                total += part
                squares += part * part
        stats[0, rows, :] = total
        stats[1, rows, :] = squares
        return carry

    steps = slots * slot_len // tile
    lax.fori_loop(0, steps, add_up, 0, unroll=4)
    mean = jnp.sum(stats[0], axis=-1, keepdims=True) / feat
    var = jnp.sum(stats[1], axis=-1, keepdims=True) / feat - mean * mean
    shape = (slots * slot_len, lane)
    stats[0] = jnp.broadcast_to(mean, shape)
    stats[1] = jnp.broadcast_to(lax.rsqrt(var + 1e-06), shape)
    for slot in range(slots):

        def write(step, carry, slot=slot):
            rows = pl.ds(pl.multiple_of(slot * slot_len + step * tile, tile), tile)
            mean, inverse = stats[0, rows, :], stats[1, rows, :]
            for col in range(cols):
                for first in range(0, wc, lane):
                    span = slice(col * wc + first, col * wc + first + lane)
                    part = xv[col, rows, first : first + lane].astype(jnp.float32)
                    part = (part - mean) * inverse * one_plus[slot, :, span]
                    xm[rows, span] = (part + mod_ref[slot, 0:1, span]).astype(jnp.bfloat16)
            return carry

        lax.fori_loop(0, slot_len // tile, write, 0, unroll=2)


def layer_kernel(plan, ends_ref, mod_ref, *refs):
    slots, slot_len, cols, n_x, n_w, kr, bw, wc = plan
    x_refs, refs = refs[:n_x], refs[n_x:]
    w_refs, refs = [refs[t * n_w : (t + 1) * n_w] for t in range(3)], refs[3 * n_w :]
    kv_refs, refs = refs[:slots], refs[slots:]
    att, xv, stats, one_plus, xm, wv, raw, queries, keys, values, x_sem, w_sem, kv_sem = refs
    lanes_of = [slice(h * HD, (h + 1) * HD) for h in range(bw // HD)]
    one_plus[...] = 1.0 + mod_ref[:, 1:2, :]
    for copy in load_x((slots, slot_len, cols), x_refs, xv, x_sem):
        copy.wait()
    copies = [load_rows(w_refs[t], wv.at[t], w_sem, t * n_w, kr) for t in range(2)]
    modulate((slots, slot_len, cols), wc, mod_ref, xv, stats, one_plus, xm)
    for copy in copies[0] + copies[1]:
        copy.wait()
    copies.append(load_rows(w_refs[2], wv.at[2], w_sem, 2 * n_w, kr))
    kv_copies = []
    for slot in range(slots):
        for t, target in enumerate((keys, values)):
            place = target.at[slot, pl.ds(slot_len, slot_len), :]
            kv_copies.append(
                pltpu.make_async_copy(kv_refs[slot].at[t], place, kv_sem.at[2 * slot + t])
            )
            kv_copies[-1].start()
    for t in range(2):
        raw[t] = jnp.dot(xm[...], wv[t], preferred_element_type=jnp.float32)
    for copy in kv_copies + copies[2]:
        copy.wait()

    def normed(block):
        mean = jnp.mean(block * block, axis=-1, keepdims=True)
        return (block * lax.rsqrt(mean + 1e-06)).astype(jnp.bfloat16)

    for lanes in lanes_of:
        queries[:, lanes] = normed(raw[0, :, lanes])
        fresh_keys = normed(raw[1, :, lanes])
        for slot in range(slots):
            keys[slot, 0:slot_len, lanes] = fresh_keys[slot * slot_len : (slot + 1) * slot_len]
    fresh_values = jnp.dot(xm[...], wv[2], preferred_element_type=jnp.float32).astype(jnp.bfloat16)
    for slot in range(slots):
        values[slot, 0:slot_len, :] = fresh_values[slot * slot_len : (slot + 1) * slot_len]
    contract = (((1,), (1,)), ((), ()))
    for slot in range(slots):
        rows = pl.ds(slot * slot_len, slot_len)
        fresh, valid = fresh_and_valid(ends_ref, slot, slot_len)
        for lanes in lanes_of:
            both = lax.dot_general(
                queries[rows, lanes],
                keys[slot, :, lanes],
                contract,
                preferred_element_type=jnp.float32,
            )
            scores = jnp.where(fresh, both[:, :slot_len], both[:, slot_len:])
            weights = jnp.where(valid, jnp.exp(scores * (1.0 / math.sqrt(HD))), 0.0)
            weights = weights * (1.0 / jnp.sum(weights, axis=-1, keepdims=True))
            both = jnp.concatenate(
                [
                    jnp.where(fresh, weights, 0.0).astype(jnp.bfloat16),
                    jnp.where(fresh, 0.0, weights).astype(jnp.bfloat16),
                ],
                axis=1,
            )
            mixed = jnp.dot(both, values[slot, :, lanes], preferred_element_type=jnp.float32)
            att[rows, lanes] = mixed.astype(jnp.bfloat16)


def project_kernel(plan, att_ref, *refs):
    slots, slot_len, cols, n_w, nr = plan
    o_refs, refs = refs[:n_w], refs[n_w:]
    keep_ref, pass_ref, att, ov, out, o_sem, out_sem = refs
    s, c = lax.axis_index("section"), lax.axis_index("col")
    half = slot_len // 2
    first = pltpu.make_async_copy(att_ref, att, o_sem.at[n_w])
    first.start()
    for copy in load_rows(o_refs, ov, o_sem, 0, None) + [first]:
        copy.wait()
    out_copies = []
    for k, (side, out_ref) in enumerate(((1 - s, pass_ref), (s, keep_ref))):
        blocks = []
        for slot in range(slots):
            row = pl.multiple_of(slot * slot_len + side * half, half)
            blocks.append(att[pl.ds(row, half), :])
        lhs = jnp.concatenate(blocks, axis=0)
        for place in range(n_w):
            row = lax.rem(c * (n_w // cols) + place, n_w)
            part = jnp.dot(lhs, ov[row], preferred_element_type=jnp.float32).astype(jnp.bfloat16)
            for slot in range(slots):
                out[k, slot, :, place * nr : (place + 1) * nr] = part[
                    slot * half : (slot + 1) * half
                ]
        out_copies.append(pltpu.make_async_copy(out.at[k], out_ref, out_sem.at[k]))
        out_copies[-1].start()
    for copy in out_copies:
        copy.wait()


def mod_kernel(slots, feats_ref, weight_ref, out_ref):
    for k in range(3):
        part = jnp.dot(feats_ref[...], weight_ref[k], preferred_element_type=jnp.float32)
        for slot in range(slots):
            out_ref[slot, k : k + 1, :] = part[slot : slot + 1, :]


GATES = {
    "K0.4": ("Q0.4",),
    "K0.6": ("Q0.6", "K0.1",),
    "V0.4": ("K0.4",),
    "V0.6": ("K0.6",),
    "O0.4": ("V0.4",),
    "O0.6": ("V0.6",),
    "Q1.4": ("O0.4",),
    "Q1.6": ("O0.6",),
    "K1.4": ("Q1.4",),
    "K1.6": ("Q1.6",),
    "V1.4": ("K1.4", "K1.1",),
    "V1.6": ("K1.6",),
    "O1.4": ("V1.4",),
    "O1.6": ("V1.6",),
    "O0.2": ("Q0.2",),
    "Q1.2": ("S0.2",),
    "K1.2": ("K0.2",),
    "V1.2": ("V0.2",),
    "O1.2": ("O0.2", "aK",),
    "S1.2": ("Q1.2",),
    "K0.1": ("Q0.1",),
    "K0.3": ("Q0.3",),
    "Q0.5": ("K0.1",),
    "Q0.7": ("K0.3",),
    "V0.1": ("Q0.5", "O0.2",),
    "V0.3": ("Q0.7",),
    "K0.5": ("V0.1",),
    "K0.7": ("V0.3",),
    "O0.1": ("K0.5",),
    "O0.3": ("K0.7",),
    "V0.5": ("O0.1",),
    "V0.7": ("O0.3",),
    "Q1.1": ("V0.5",),
    "Q1.3": ("V0.7",),
    "O0.5": ("Q1.1",),
    "O0.7": ("Q1.3",),
    "K1.1": ("O0.5",),
    "K1.3": ("O0.7", "Q0.1",),
    "Q1.5": ("K1.1",),
    "Q1.7": ("K1.3",),
    "V1.1": ("Q1.5", "V1.4",),
    "V1.3": ("Q1.7",),
    "K1.5": ("V1.1",),
    "K1.7": ("V1.3",),
    "O1.1": ("K1.5",),
    "O1.3": ("K1.7",),
    "V1.5": ("O1.1",),
    "V1.7": ("O1.3",),
    "O1.5": ("V1.5",),
    "O1.7": ("V1.7",),
    "n": ("aQ", "O0.2",),
    "m": ("Q0.6", "aV",),
    "p0": ("Q1.4", "Q1.6",),
    "r0.0.1": ("K1.4",),
    "O1.0": ("V1.3",),
    "x.0.0c": ("aV",),
    "V0.2": ("Q0.6",),
    "v0": ("aQ",),
    "l1": ("O1.6",),
}
TREE = ("x", "r0", "g", )


def shards(
    hidden_in, patch_ends, timestep, mod_weight, qkv_weight, out_weight, stale_keys, stale_values
):
    s, i, c = (lax.axis_index(axis) for axis in AXES)
    sections, rows, cols = (lax.axis_size(axis) for axis in AXES)
    _, slot_len, wc = hidden_in.shape
    feat = mod_weight.shape[-1]
    kr, nr = qkv_weight.shape[1], out_weight.shape[2]
    half = slot_len // 2
    slots = 2 if (wc // HD) % (2 * sections) == 0 else 1
    bw = wc // (sections * slots)
    pair_bit = 2 if slots == 2 else 0
    group_bits = [1 << b for b in reversed(range(rows.bit_length() - 1)) if 1 << b != pair_bit]
    first_bit, last_bits = group_bits[0], group_bits[1:]
    offsets = [0, pair_bit] if slots == 2 else [0]
    places = [(di, dc) for di in offsets for dc in range(cols)]
    mine_at = (i // 2) % 2 if slots == 2 else 0
    gates = GATES if rows == 8 and slots == 2 else {}
    made, steps = {}, {}

    def get(name):
        if name not in made:
            made[name] = None
            made[name] = steps[name]()
        return made[name]

    def gated(array, name):
        waits = [get(other) for other in gates.get(name, ())]
        return after(array, *waits) if waits else array

    def send(name, array, di=0, dc=0):
        def where(si, ii, ci):
            return si, ii ^ di, (ci + dc) % cols

        return send_to(gated(array, name), where)

    def swap(name, array):
        return send_to(gated(array, name), lambda si, ii, ci: (1 - si, ii, ci))

    def step(name):
        def note(make):
            steps[name] = make
            return make

        return note

    wide = slots * bw
    qkv = qkv_weight[0].transpose(1, 0, 2)
    stale = (stale_keys[0, 0], stale_values[0, 0])

    def columns(array, start, width):
        return lax.dynamic_slice_in_dim(array, start, width, array.ndim - 1)

    def cut(kind, start, width):
        if kind == "O":
            return lax.dynamic_slice_in_dim(out_weight[0], start, width, 0)
        if kind == "S":
            return jnp.concatenate([columns(one, start, width) for one in stale])
        return columns(qkv["QKV".index(kind)], start, width)

    def block_of(kind, layer, slot):
        at = (mine_at if slot == 0 else 1 - mine_at) * bw
        got = get("a" + kind)
        other = lax.dynamic_slice_in_dim(got, at, bw, 0) if kind == "O" else columns(got, at, bw)
        block = jnp.where(s == layer, cut(kind, s * wide + at, bw), other)
        return block.reshape(2, slot_len, bw) if kind == "S" else block

    for kind in "QKVOS":
        step("a" + kind)(
            lambda kind=kind: swap("a" + kind, cut(kind, (1 - s) * wide, wide))
        )

    def move(kind, layer, d):
        name = f"{kind}{layer}.{d}"
        for bit in reversed(last_bits):
            if d & bit:
                return send(name, get(f"{kind}{layer}.{d ^ bit}"), bit)
        block = block_of(kind, layer, 1 if d & pair_bit else 0)
        return send(name, block, d) if d else gated(block, name)

    for layer in range(2):
        for kind in "QKVO":
            for d in range(rows):
                step(f"{kind}{layer}.{d}")(functools.partial(move, kind, layer, d))
        for d in offsets:
            step(f"S{layer}.{d}")(functools.partial(move, "S", layer, d))

    def of_rows(kind, layer):
        return [get(f"{kind}{layer}.{d}") for d in range(rows)]

    def stale_of(layer):
        return [get(f"S{layer}.{d}") for d in offsets]

    @step("n")
    def _():
        numbers = jnp.concatenate([patch_ends[0], timestep])
        return jnp.stack([numbers] + [send("n", numbers, di) for di in offsets[1:]])

    @step("m")
    def _():
        feats = jnp.pad(embed_time(get("n")[:, NP]), ((0, 8 - slots), (0, 0)))
        own = pl.pallas_call(
            functools.partial(mod_kernel, slots),
            out_shape=jax.ShapeDtypeStruct((slots, 3, feat), jnp.float32),
            in_specs=[vmem_spec(), vmem_spec()],
            out_specs=vmem_spec(),
            compiler_params=pltpu.CompilerParams(vmem_limit_bytes=VMEM_LIMIT),
            name="modulation",
        )(gated(feats, "m"), mod_weight[0].transpose(1, 0, 2))
        other = swap("mc", own)
        return [jnp.where(s == layer, own, other) for layer in range(2)]

    x_half = lax.dynamic_slice_in_dim(hidden_in[0], s * half, half, 0)
    step("x.0.0")(lambda: gated(x_half, "x.0.0"))
    step("g.0.0")(lambda: finish(0, x_half))
    for kind in "xg":
        for di, dc in places:
            name = f"{kind}.{di}.{dc}"

            def bring(kind=kind, name=name, di=di, dc=dc):
                if dc and kind in TREE:
                    return send(name, get(f"{kind}.{di}.0"), 0, dc)
                return send(name, get(f"{kind}.0.0"), di, dc)

            if (di, dc) != (0, 0):
                step(name)(bring)
            step(name + "c")(lambda name=name: swap(name + "c", get(name)))
    x_rest = lax.dynamic_slice_in_dim(hidden_in[0], (1 - s) * half, half, 0)
    step("x.0.0c")(lambda: x_rest)

    def x_pieces(kind):
        return [get(f"{kind}.{di}.{dc}" + end) for di, dc in places for end in ("", "c")]

    every = slots * slot_len

    def heads_of(layer):
        pieces = x_pieces("xg"[layer])
        plan = (slots, slot_len, cols, len(pieces), rows, kr, bw, wc)
        return pl.pallas_call(
            functools.partial(layer_kernel, plan),
            out_shape=jax.ShapeDtypeStruct((every, bw), jnp.bfloat16),
            in_specs=[pl.BlockSpec(memory_space=pltpu.SMEM), vmem_spec()]
            + [any_spec()] * (len(pieces) + 3 * rows + slots),
            out_specs=vmem_spec(),
            scratch_shapes=[
                pltpu.VMEM((cols, every, wc), jnp.bfloat16),
                pltpu.VMEM((2, every, 128), jnp.float32),
                pltpu.VMEM((slots, 1, feat), jnp.float32),
                pltpu.VMEM((every, feat), jnp.bfloat16),
                pltpu.VMEM((3, feat, bw), jnp.bfloat16),
                pltpu.VMEM((2, every, bw), jnp.float32),
                pltpu.VMEM((every, bw), jnp.bfloat16),
                pltpu.VMEM((slots, 2 * slot_len, bw), jnp.bfloat16),
                pltpu.VMEM((slots, 2 * slot_len, bw), jnp.bfloat16),
                pltpu.SemaphoreType.DMA((len(pieces),)),
                pltpu.SemaphoreType.DMA((3 * rows,)),
                pltpu.SemaphoreType.DMA((2 * slots,)),
            ],
            compiler_params=pltpu.CompilerParams(vmem_limit_bytes=VMEM_LIMIT),
            name="layer",
        )(
            gated(get("n")[:, :NP], f"k{layer}"),
            get("m")[layer],
            *pieces,
            *[one for kind in "QKV" for one in of_rows(kind, layer)],
            *stale_of(layer),
        )

    def project(layer):
        shape = jax.ShapeDtypeStruct((slots, half, feat), jnp.bfloat16)
        return pl.pallas_call(
            functools.partial(project_kernel, (slots, slot_len, cols, rows, nr)),
            out_shape=(shape, shape),
            in_specs=[any_spec()] * (1 + rows),
            out_specs=(any_spec(), any_spec()),
            scratch_shapes=[
                pltpu.VMEM((every, bw), jnp.bfloat16),
                pltpu.VMEM((rows, bw, nr), jnp.bfloat16),
                pltpu.VMEM((2, slots, half, feat), jnp.bfloat16),
                pltpu.SemaphoreType.DMA((rows + 1,)),
                pltpu.SemaphoreType.DMA((2,)),
            ],
            compiler_params=pltpu.CompilerParams(vmem_limit_bytes=VMEM_LIMIT),
            name="project",
        )(gated(get(f"k{layer}"), f"v{layer}"), *of_rows("O", layer))

    def parts(layer):
        keep, other = get(f"v{layer}")[0], get(f"p{layer}")

        def part(array, di, dc):
            return array[offsets.index(di), :, dc * wc : (dc + 1) * wc].astype(jnp.float32)

        return {place: part(keep, *place) + part(other, *place) for place in places}

    def summed(layer, di):
        part = get(f"t{layer}")[di, 0]
        for dc in range(1, cols):
            part = part + get(f"r{layer}.{di}.{dc}").astype(jnp.float32)
        return part

    def give(layer, di, dc):
        name = f"r{layer}.{di}.{dc}"
        if f"r{layer}" not in TREE:
            return send(name, get(f"t{layer}")[di, dc].astype(jnp.bfloat16), di, dc)
        if dc:
            return send(name, get(f"t{layer}")[di, dc].astype(jnp.bfloat16), 0, dc)
        return send(name, get(f"u{layer}.{di}").astype(jnp.bfloat16), di, 0)

    for layer in range(2):
        step(f"k{layer}")(functools.partial(heads_of, layer))
        step(f"v{layer}")(functools.partial(project, layer))
        step(f"p{layer}")(lambda layer=layer: swap(f"p{layer}", get(f"v{layer}")[1]))
        step(f"t{layer}")(functools.partial(parts, layer))
        for di, dc in places:
            if (di, dc) != (0, 0):
                step(f"r{layer}.{di}.{dc}")(functools.partial(give, layer, di, dc))
        for di in offsets:
            step(f"u{layer}.{di}")(functools.partial(summed, layer, di))

    def finish(layer, x_own):
        if f"r{layer}" in TREE:
            branch = get(f"u{layer}.0")
            for di in offsets[1:]:
                branch = branch + get(f"r{layer}.{di}.0").astype(jnp.float32)
        else:
            branch = get(f"t{layer}")[0, 0]
            for di, dc in places[1:]:
                branch = branch + get(f"r{layer}.{di}.{dc}").astype(jnp.float32)
        gate_own = columns(get("m")[layer][0, 2], c * wc, wc)
        updated = x_own.astype(jnp.float32) + gate_own[None, :] * branch
        positions = jnp.arange(half)[:, None] + s * half
        return jnp.where(positions < patch_ends[0, NP - 1], updated, 0.0).astype(jnp.bfloat16)

    first = get("g.0.0")
    second = finish(1, first)
    low = jnp.where(s == 0, first, swap("e", second))
    high = jnp.where(s == 0, get("g.0.0c"), second)
    return jnp.concatenate([low, high], axis=0)[None, None]


def solution(mesh):
    return jax.shard_map(
        shards,
        mesh=mesh,
        in_specs=(
            P("row", None, "col"),
            P("row", None),
            P("row"),
            P("section", None, None, None),
            P("section", "row", None, "col"),
            P("section", "col", "row"),
            P("section", "row", None, "col"),
            P("section", "row", None, "col"),
        ),
        out_specs=P("section", "row", None, "col"),
        check_vma=False,
    )
```

```python
import functools
import math

import jax
import jax.numpy as jnp
from jax import lax
from jax.experimental import pallas as pl
from jax.experimental.pallas import tpu as pltpu
from jax.sharding import PartitionSpec as P

HD = 128
FREQ = 256
NP = 4
AXES = ("section", "row", "col")
VMEM_LIMIT = 56 * 1024 * 1024


def send_to(array, where):
    ns, nr, nc = (lax.axis_size(axis) for axis in AXES)
    pairs = []
    for s in range(ns):
        for i in range(nr):
            for c in range(nc):
                ts, ti, tc = where(s, i, c)
                pairs.append(((s * nr + i) * nc + c, (ts * nr + ti) * nc + tc))
    return lax.ppermute(array, AXES, pairs)


def to_core(array):
    return send_to(array, lambda s, i, c: (1 - s, i, c))


def after(array, *others):
    return lax.optimization_barrier((array,) + others)[0]


def pick(array, index):
    return lax.dynamic_index_in_dim(array, index, 0, keepdims=False)


def embed_time(timestep):
    half_width = FREQ // 2
    frequency = jnp.exp(
        jnp.arange(half_width, dtype=jnp.float32) * (-math.log(10000.0) / half_width)
    )
    angles = timestep.astype(jnp.float32)[:, None] * frequency[None, :]
    return jnp.concatenate([jnp.cos(angles), jnp.sin(angles)], axis=1).astype(jnp.bfloat16)


def any_spec():
    return pl.BlockSpec(memory_space=pl.ANY)


def vmem_spec():
    return pl.BlockSpec(memory_space=pltpu.VMEM)


def load_rows(pieces, target, sem, first, rows_each):
    i = lax.axis_index("row")
    copies = []
    for d, piece in enumerate(pieces):
        if rows_each is None:
            place = target.at[i ^ d]
        else:
            place = target.at[pl.ds(pl.multiple_of((i ^ d) * rows_each, 32), rows_each), :]
        copies.append(pltpu.make_async_copy(piece, place, sem.at[first + d]))
        copies[-1].start()
    return copies


def fresh_and_valid(ends_ref, slot, slot_len):
    key_at = lax.broadcasted_iota(jnp.int32, (slot_len, slot_len), 1)
    query_at = lax.broadcasted_iota(jnp.int32, (slot_len, slot_len), 0)
    limit = jnp.full((slot_len, slot_len), ends_ref[slot, NP - 1], jnp.int32)
    for m in range(NP - 2, -1, -1):
        limit = jnp.where(query_at < ends_ref[slot, m], ends_ref[slot, m], limit)
    return key_at < limit, key_at < ends_ref[slot, NP - 1]


def load_x(plan, x_refs, xv, sem):
    slots, slot_len, cols = plan
    s, c = lax.axis_index("section"), lax.axis_index("col")
    half = slot_len // 2
    copies = []
    for slot in range(slots):
        for dc in range(cols):
            for h in range(2):
                place = len(copies)
                col = lax.rem(c + cols - dc, cols)
                row = pl.multiple_of(slot * slot_len + jnp.where(s == h, 0, half), half)
                copies.append(
                    pltpu.make_async_copy(
                        x_refs[place], xv.at[col, pl.ds(row, half), :], sem.at[place]
                    )
                )
                copies[-1].start()
    return copies


def modulate(plan, wc, mod_ref, xv, stats, one_plus, xm):
    slots, slot_len, cols = plan
    feat, tile, lane = cols * wc, 16, 128

    def add_up(step, carry):
        rows = pl.ds(pl.multiple_of(step * tile, tile), tile)
        total = jnp.zeros((tile, lane), jnp.float32)
        squares = jnp.zeros((tile, lane), jnp.float32)
        for col in range(cols):
            for first in range(0, wc, lane):
                part = xv[col, rows, first : first + lane].astype(jnp.float32)
                total += part
                squares += part * part
        stats[0, rows, :] = total
        stats[1, rows, :] = squares
        return carry

    steps = slots * slot_len // tile
    lax.fori_loop(0, steps, add_up, 0, unroll=4)
    mean = jnp.sum(stats[0], axis=-1, keepdims=True) / feat
    var = jnp.sum(stats[1], axis=-1, keepdims=True) / feat - mean * mean
    shape = (slots * slot_len, lane)
    stats[0] = jnp.broadcast_to(mean, shape)
    stats[1] = jnp.broadcast_to(lax.rsqrt(var + 1e-06), shape)
    for slot in range(slots):

        def write(step, carry, slot=slot):
            rows = pl.ds(pl.multiple_of(slot * slot_len + step * tile, tile), tile)
            mean, inverse = stats[0, rows, :], stats[1, rows, :]
            for col in range(cols):
                for first in range(0, wc, lane):
                    span = slice(col * wc + first, col * wc + first + lane)
                    part = xv[col, rows, first : first + lane].astype(jnp.float32)
                    part = (part - mean) * inverse * one_plus[slot, :, span]
                    xm[rows, span] = (part + mod_ref[slot, 0:1, span]).astype(jnp.bfloat16)
            return carry

        lax.fori_loop(0, slot_len // tile, write, 0, unroll=2)


def layer_kernel(plan, ends_ref, mod_ref, *refs):
    slots, slot_len, cols, n_x, n_w, kr, bw, wc = plan
    x_refs, refs = refs[:n_x], refs[n_x:]
    w_refs, refs = [refs[t * n_w : (t + 1) * n_w] for t in range(3)], refs[3 * n_w :]
    kv_refs, refs = refs[:slots], refs[slots:]
    att, xv, stats, one_plus, xm, wv, raw, queries, keys, values, x_sem, w_sem, kv_sem = refs
    lanes_of = [slice(h * HD, (h + 1) * HD) for h in range(bw // HD)]
    one_plus[...] = 1.0 + mod_ref[:, 1:2, :]
    for copy in load_x((slots, slot_len, cols), x_refs, xv, x_sem):
        copy.wait()
    copies = [load_rows(w_refs[t], wv.at[t], w_sem, t * n_w, kr) for t in range(2)]
    modulate((slots, slot_len, cols), wc, mod_ref, xv, stats, one_plus, xm)
    for copy in copies[0]:
        copy.wait()
    raw[0] = jnp.dot(xm[...], wv[0], preferred_element_type=jnp.float32)
    for copy in copies[1]:
        copy.wait()
    copies.append(load_rows(w_refs[2], wv.at[2], w_sem, 2 * n_w, kr))
    kv_copies = []
    for slot in range(slots):
        for t, target in enumerate((keys, values)):
            place = target.at[slot, pl.ds(slot_len, slot_len), :]
            kv_copies.append(
                pltpu.make_async_copy(kv_refs[slot].at[t], place, kv_sem.at[2 * slot + t])
            )
            kv_copies[-1].start()
    raw[1] = jnp.dot(xm[...], wv[1], preferred_element_type=jnp.float32)
    for copy in kv_copies + copies[2]:
        copy.wait()

    def normed(block):
        mean = jnp.mean(block * block, axis=-1, keepdims=True)
        return (block * lax.rsqrt(mean + 1e-06)).astype(jnp.bfloat16)

    for lanes in lanes_of:
        queries[:, lanes] = normed(raw[0, :, lanes])
        fresh_keys = normed(raw[1, :, lanes])
        for slot in range(slots):
            keys[slot, 0:slot_len, lanes] = fresh_keys[slot * slot_len : (slot + 1) * slot_len]
    fresh_values = jnp.dot(xm[...], wv[2], preferred_element_type=jnp.float32).astype(jnp.bfloat16)
    for slot in range(slots):
        values[slot, 0:slot_len, :] = fresh_values[slot * slot_len : (slot + 1) * slot_len]
    contract = (((1,), (1,)), ((), ()))
    for slot in range(slots):
        rows = pl.ds(slot * slot_len, slot_len)
        fresh, valid = fresh_and_valid(ends_ref, slot, slot_len)
        for lanes in lanes_of:
            both = lax.dot_general(
                queries[rows, lanes],
                keys[slot, :, lanes],
                contract,
                preferred_element_type=jnp.float32,
            )
            scores = jnp.where(fresh, both[:, :slot_len], both[:, slot_len:])
            weights = jnp.where(valid, jnp.exp(scores * (1.0 / math.sqrt(HD))), 0.0)
            weights = weights * (1.0 / jnp.sum(weights, axis=-1, keepdims=True))
            both = jnp.concatenate(
                [
                    jnp.where(fresh, weights, 0.0).astype(jnp.bfloat16),
                    jnp.where(fresh, 0.0, weights).astype(jnp.bfloat16),
                ],
                axis=1,
            )
            mixed = jnp.dot(both, values[slot, :, lanes], preferred_element_type=jnp.float32)
            att[rows, lanes] = mixed.astype(jnp.bfloat16)


def project_kernel(plan, att_ref, *refs):
    slots, slot_len, cols, n_w, nr = plan
    o_refs, refs = refs[:n_w], refs[n_w:]
    keep_ref, pass_ref, att, ov, out, o_sem, out_sem = refs
    s, c = lax.axis_index("section"), lax.axis_index("col")
    half = slot_len // 2
    first = pltpu.make_async_copy(att_ref, att, o_sem.at[n_w])
    first.start()
    for copy in load_rows(o_refs, ov, o_sem, 0, None) + [first]:
        copy.wait()
    out_copies = []
    for k, (side, out_ref) in enumerate(((1 - s, pass_ref), (s, keep_ref))):
        blocks = []
        for slot in range(slots):
            row = pl.multiple_of(slot * slot_len + side * half, half)
            blocks.append(att[pl.ds(row, half), :])
        lhs = jnp.concatenate(blocks, axis=0)
        for place in range(n_w):
            row = lax.rem(c * (n_w // cols) + place, n_w)
            part = jnp.dot(lhs, ov[row], preferred_element_type=jnp.float32).astype(jnp.bfloat16)
            for slot in range(slots):
                out[k, slot, :, place * nr : (place + 1) * nr] = part[
                    slot * half : (slot + 1) * half
                ]
        out_copies.append(pltpu.make_async_copy(out.at[k], out_ref, out_sem.at[k]))
        out_copies[-1].start()
    for copy in out_copies:
        copy.wait()


def mod_kernel(slots, feats_ref, weight_ref, out_ref):
    for k in range(3):
        part = jnp.dot(feats_ref[...], weight_ref[k], preferred_element_type=jnp.float32)
        for slot in range(slots):
            out_ref[slot, k : k + 1, :] = part[slot : slot + 1, :]


GATES = {
    "K0.4": ("Q0.4",),
    "K0.6": ("Q0.6", "K0.1",),
    "V0.4": ("K0.4",),
    "V0.6": ("K0.6",),
    "O0.4": ("V0.4",),
    "O0.6": ("V0.6",),
    "Q1.4": ("O0.4",),
    "Q1.6": ("O0.6",),
    "K1.4": ("Q1.4",),
    "K1.6": ("Q1.6",),
    "V1.4": ("K1.4", "K1.1",),
    "V1.6": ("K1.6",),
    "O1.4": ("V1.4",),
    "O1.6": ("V1.6",),
    "O0.2": ("Q0.2",),
    "Q1.2": ("S0.2",),
    "K1.2": ("K0.2",),
    "V1.2": ("V0.2",),
    "O1.2": ("O0.2", "aK",),
    "S1.2": ("Q1.2",),
    "K0.1": ("Q0.1",),
    "K0.3": ("Q0.3",),
    "Q0.5": ("K0.1",),
    "Q0.7": ("K0.3",),
    "V0.1": ("Q0.5", "O0.2",),
    "V0.3": ("Q0.7",),
    "K0.5": ("V0.1",),
    "K0.7": ("V0.3",),
    "O0.1": ("K0.5",),
    "O0.3": ("K0.7",),
    "V0.5": ("O0.1",),
    "V0.7": ("O0.3",),
    "Q1.1": ("V0.5",),
    "Q1.3": ("V0.7",),
    "O0.5": ("Q1.1",),
    "O0.7": ("Q1.3",),
    "K1.1": ("O0.5",),
    "K1.3": ("O0.7", "Q0.1",),
    "Q1.5": ("K1.1",),
    "Q1.7": ("K1.3",),
    "V1.1": ("Q1.5", "V1.4",),
    "V1.3": ("Q1.7",),
    "K1.5": ("V1.1",),
    "K1.7": ("V1.3",),
    "O1.1": ("K1.5",),
    "O1.3": ("K1.7",),
    "V1.5": ("O1.1",),
    "V1.7": ("O1.3",),
    "O1.5": ("V1.5",),
    "O1.7": ("V1.7",),
    "n": ("aQ", "O0.2",),
    "m": ("Q0.6", "aV",),
    "p0": ("Q1.4", "Q1.6",),
    "r0.0.1": ("K1.4",),
    "O1.0": ("V1.3",),
    "x.0.0c": ("aV",),
    "V0.2": ("Q0.6",),
    "v0": ("aQ",),
    "l1": ("O1.6",),
}
TREE = ("x", "r0", "g", )


def shards(
    hidden_in, patch_ends, timestep, mod_weight, qkv_weight, out_weight, stale_keys, stale_values
):
    s, i, c = (lax.axis_index(axis) for axis in AXES)
    sections, rows, cols = (lax.axis_size(axis) for axis in AXES)
    _, slot_len, wc = hidden_in.shape
    feat = mod_weight.shape[-1]
    kr, nr = qkv_weight.shape[1], out_weight.shape[2]
    half = slot_len // 2
    slots = 2 if (wc // HD) % (2 * sections) == 0 else 1
    bw = wc // (sections * slots)
    pair_bit = 2 if slots == 2 else 0
    group_bits = [1 << b for b in reversed(range(rows.bit_length() - 1)) if 1 << b != pair_bit]
    first_bit, last_bits = group_bits[0], group_bits[1:]
    offsets = [0, pair_bit] if slots == 2 else [0]
    places = [(di, dc) for di in offsets for dc in range(cols)]
    mine_at = (i // 2) % 2 if slots == 2 else 0
    gates = GATES if rows == 8 and slots == 2 else {}
    made, steps = {}, {}

    def get(name):
        if name not in made:
            made[name] = None
            made[name] = steps[name]()
        return made[name]

    def gated(array, name):
        waits = [get(other) for other in gates.get(name, ())]
        return after(array, *waits) if waits else array

    def send(name, array, di=0, dc=0):
        def where(si, ii, ci):
            return si, ii ^ di, (ci + dc) % cols

        return send_to(gated(array, name), where)

    def swap(name, array):
        return send_to(gated(array, name), lambda si, ii, ci: (1 - si, ii, ci))

    def step(name):
        def note(make):
            steps[name] = make
            return make

        return note

    wide = slots * bw
    qkv = qkv_weight[0].transpose(1, 0, 2)
    stale = (stale_keys[0, 0], stale_values[0, 0])

    def columns(array, start, width):
        return lax.dynamic_slice_in_dim(array, start, width, array.ndim - 1)

    def cut(kind, start, width):
        if kind == "O":
            return lax.dynamic_slice_in_dim(out_weight[0], start, width, 0)
        if kind == "S":
            return jnp.concatenate([columns(one, start, width) for one in stale])
        return columns(qkv["QKV".index(kind)], start, width)

    def block_of(kind, layer, slot):
        at = (mine_at if slot == 0 else 1 - mine_at) * bw
        got = get("a" + kind)
        other = lax.dynamic_slice_in_dim(got, at, bw, 0) if kind == "O" else columns(got, at, bw)
        block = jnp.where(s == layer, cut(kind, s * wide + at, bw), other)
        return block.reshape(2, slot_len, bw) if kind == "S" else block

    for kind in "QKVOS":
        step("a" + kind)(
            lambda kind=kind: swap("a" + kind, cut(kind, (1 - s) * wide, wide))
        )

    def move(kind, layer, d):
        name = f"{kind}{layer}.{d}"
        for bit in reversed(last_bits):
            if d & bit:
                return send(name, get(f"{kind}{layer}.{d ^ bit}"), bit)
        block = block_of(kind, layer, 1 if d & pair_bit else 0)
        return send(name, block, d) if d else gated(block, name)

    for layer in range(2):
        for kind in "QKVO":
            for d in range(rows):
                step(f"{kind}{layer}.{d}")(functools.partial(move, kind, layer, d))
        for d in offsets:
            step(f"S{layer}.{d}")(functools.partial(move, "S", layer, d))

    def of_rows(kind, layer):
        return [get(f"{kind}{layer}.{d}") for d in range(rows)]

    def stale_of(layer):
        return [get(f"S{layer}.{d}") for d in offsets]

    @step("n")
    def _():
        numbers = jnp.concatenate([patch_ends[0], timestep])
        return jnp.stack([numbers] + [send("n", numbers, di) for di in offsets[1:]])

    @step("m")
    def _():
        feats = jnp.pad(embed_time(get("n")[:, NP]), ((0, 8 - slots), (0, 0)))
        own = pl.pallas_call(
            functools.partial(mod_kernel, slots),
            out_shape=jax.ShapeDtypeStruct((slots, 3, feat), jnp.float32),
            in_specs=[vmem_spec(), vmem_spec()],
            out_specs=vmem_spec(),
            compiler_params=pltpu.CompilerParams(vmem_limit_bytes=VMEM_LIMIT),
            name="modulation",
        )(gated(feats, "m"), mod_weight[0].transpose(1, 0, 2))
        other = swap("mc", own)
        return [jnp.where(s == layer, own, other) for layer in range(2)]

    x_half = lax.dynamic_slice_in_dim(hidden_in[0], s * half, half, 0)
    step("x.0.0")(lambda: gated(x_half, "x.0.0"))
    step("g.0.0")(lambda: finish(0, x_half))
    for kind in "xg":
        for di, dc in places:
            name = f"{kind}.{di}.{dc}"

            def bring(kind=kind, name=name, di=di, dc=dc):
                if dc and kind in TREE:
                    return send(name, get(f"{kind}.{di}.0"), 0, dc)
                return send(name, get(f"{kind}.0.0"), di, dc)

            if (di, dc) != (0, 0):
                step(name)(bring)
            step(name + "c")(lambda name=name: swap(name + "c", get(name)))
    x_rest = lax.dynamic_slice_in_dim(hidden_in[0], (1 - s) * half, half, 0)
    step("x.0.0c")(lambda: x_rest)

    def x_pieces(kind):
        return [get(f"{kind}.{di}.{dc}" + end) for di, dc in places for end in ("", "c")]

    every = slots * slot_len

    def heads_of(layer):
        pieces = x_pieces("xg"[layer])
        plan = (slots, slot_len, cols, len(pieces), rows, kr, bw, wc)
        return pl.pallas_call(
            functools.partial(layer_kernel, plan),
            out_shape=jax.ShapeDtypeStruct((every, bw), jnp.bfloat16),
            in_specs=[pl.BlockSpec(memory_space=pltpu.SMEM), vmem_spec()]
            + [any_spec()] * (len(pieces) + 3 * rows + slots),
            out_specs=vmem_spec(),
            scratch_shapes=[
                pltpu.VMEM((cols, every, wc), jnp.bfloat16),
                pltpu.VMEM((2, every, 128), jnp.float32),
                pltpu.VMEM((slots, 1, feat), jnp.float32),
                pltpu.VMEM((every, feat), jnp.bfloat16),
                pltpu.VMEM((3, feat, bw), jnp.bfloat16),
                pltpu.VMEM((2, every, bw), jnp.float32),
                pltpu.VMEM((every, bw), jnp.bfloat16),
                pltpu.VMEM((slots, 2 * slot_len, bw), jnp.bfloat16),
                pltpu.VMEM((slots, 2 * slot_len, bw), jnp.bfloat16),
                pltpu.SemaphoreType.DMA((len(pieces),)),
                pltpu.SemaphoreType.DMA((3 * rows,)),
                pltpu.SemaphoreType.DMA((2 * slots,)),
            ],
            compiler_params=pltpu.CompilerParams(vmem_limit_bytes=VMEM_LIMIT),
            name="layer",
        )(
            gated(get("n")[:, :NP], f"k{layer}"),
            get("m")[layer],
            *pieces,
            *[one for kind in "QKV" for one in of_rows(kind, layer)],
            *stale_of(layer),
        )

    def project(layer):
        shape = jax.ShapeDtypeStruct((slots, half, feat), jnp.bfloat16)
        return pl.pallas_call(
            functools.partial(project_kernel, (slots, slot_len, cols, rows, nr)),
            out_shape=(shape, shape),
            in_specs=[any_spec()] * (1 + rows),
            out_specs=(any_spec(), any_spec()),
            scratch_shapes=[
                pltpu.VMEM((every, bw), jnp.bfloat16),
                pltpu.VMEM((rows, bw, nr), jnp.bfloat16),
                pltpu.VMEM((2, slots, half, feat), jnp.bfloat16),
                pltpu.SemaphoreType.DMA((rows + 1,)),
                pltpu.SemaphoreType.DMA((2,)),
            ],
            compiler_params=pltpu.CompilerParams(vmem_limit_bytes=VMEM_LIMIT),
            name="project",
        )(gated(get(f"k{layer}"), f"v{layer}"), *of_rows("O", layer))

    def parts(layer):
        keep, other = get(f"v{layer}")[0], get(f"p{layer}")

        def part(array, di, dc):
            return array[offsets.index(di), :, dc * wc : (dc + 1) * wc].astype(jnp.float32)

        return {place: part(keep, *place) + part(other, *place) for place in places}

    def summed(layer, di):
        part = get(f"t{layer}")[di, 0]
        for dc in range(1, cols):
            part = part + get(f"r{layer}.{di}.{dc}").astype(jnp.float32)
        return part

    def give(layer, di, dc):
        name = f"r{layer}.{di}.{dc}"
        if f"r{layer}" not in TREE:
            return send(name, get(f"t{layer}")[di, dc].astype(jnp.bfloat16), di, dc)
        if dc:
            return send(name, get(f"t{layer}")[di, dc].astype(jnp.bfloat16), 0, dc)
        return send(name, get(f"u{layer}.{di}").astype(jnp.bfloat16), di, 0)

    for layer in range(2):
        step(f"k{layer}")(functools.partial(heads_of, layer))
        step(f"v{layer}")(functools.partial(project, layer))
        step(f"p{layer}")(lambda layer=layer: swap(f"p{layer}", get(f"v{layer}")[1]))
        step(f"t{layer}")(functools.partial(parts, layer))
        for di, dc in places:
            if (di, dc) != (0, 0):
                step(f"r{layer}.{di}.{dc}")(functools.partial(give, layer, di, dc))
        for di in offsets:
            step(f"u{layer}.{di}")(functools.partial(summed, layer, di))

    def finish(layer, x_own):
        if f"r{layer}" in TREE:
            branch = get(f"u{layer}.0")
            for di in offsets[1:]:
                branch = branch + get(f"r{layer}.{di}.0").astype(jnp.float32)
        else:
            branch = get(f"t{layer}")[0, 0]
            for di, dc in places[1:]:
                branch = branch + get(f"r{layer}.{di}.{dc}").astype(jnp.float32)
        gate_own = columns(get("m")[layer][0, 2], c * wc, wc)
        updated = x_own.astype(jnp.float32) + gate_own[None, :] * branch
        positions = jnp.arange(half)[:, None] + s * half
        return jnp.where(positions < patch_ends[0, NP - 1], updated, 0.0).astype(jnp.bfloat16)

    first = get("g.0.0")
    second = finish(1, first)
    low = jnp.where(s == 0, first, swap("e", second))
    high = jnp.where(s == 0, get("g.0.0c"), second)
    return jnp.concatenate([low, high], axis=0)[None, None]


def solution(mesh):
    return jax.shard_map(
        shards,
        mesh=mesh,
        in_specs=(
            P("row", None, "col"),
            P("row", None),
            P("row"),
            P("section", None, None, None),
            P("section", "row", None, "col"),
            P("section", "col", "row"),
            P("section", "row", None, "col"),
            P("section", "row", None, "col"),
        ),
        out_specs=P("section", "row", None, "col"),
        check_vma=False,
    )
```
